32 devices in a mesh: seq: 16 (over z, x, core), tp: 2 (over y).
Axes of the slice: x: 2, y: 2, z: 4, core: 2. Of those that a mesh axis runs over, the one named last changes fastest.
Arguments:
- frames: bfloat16 [2, 4, 1024, 1024], P(None, 'tp', 'seq'), may hold values from -6 to 6
- time_embed: float32 [2, 4, 1024], replicated, may hold values from -6 to 6
- lengths: int32 [2, 4], replicated, may hold values from 1 to 1024, 2560 in all within a row
- w_query: bfloat16 [1024, 1024], P('seq', 'tp'), may hold values from -0.1875 to 0.1875
- w_key: bfloat16 [1024, 1024], P('seq', 'tp'), may hold values from -0.1875 to 0.1875
- w_value: bfloat16 [1024, 1024], P('seq', 'tp'), may hold values from -0.1875 to 0.1875
- w_out: bfloat16 [1024, 1024], P('tp', 'seq'), may hold values from -0.75 to 0.75
- w_up: bfloat16 [1024, 2048], P('seq', 'tp'), may hold values from -0.1875 to 0.1875
- w_down: bfloat16 [2048, 1024], P('tp', 'seq'), may hold values from -0.125 to 0.125
- w_mod: bfloat16 [1024, 6144], P('seq', 'tp'), may hold values from -0.1875 to 0.1875
- out_grad: bfloat16 [2, 4, 1024, 1024], P(None, 'tp', 'seq'), may hold values from -6 to 6
Outputs:
- layer_out: bfloat16 [2, 4, 1024, 1024], P(None, 'tp', 'seq')
- grad_input: bfloat16 [2, 4, 1024, 1024], P(None, 'tp', 'seq')
- grad_query: float32 [1024, 1024], P('seq', 'tp')
- grad_key: float32 [1024, 1024], P('seq', 'tp')
- grad_value: float32 [1024, 1024], P('seq', 'tp')
- grad_out: float32 [1024, 1024], P('tp', 'seq')
- grad_up: float32 [1024, 2048], P('seq', 'tp')
- grad_down: float32 [2048, 1024], P('tp', 'seq')
- grad_mod: float32 [1024, 6144], P('seq', 'tp')
The draws below stay inside these ranges and needn't reach their ends.
Inputs may be any that keep to these rules, and one draw needn't show every extreme that they name: In every micro-batch the 4 lengths add up to 2560, and one item has exactly 1024 live frames.
All inputs are finite; a program needn't handle non-finite values.
Results may differ from the reference program's by a relative error of at most 0.024.
Values may be sent and summed in bfloat16 or wider, within the bound.
A program may use at most 384 MiB of HBM per device.

```python
import math
import jax
import jax.numpy as jnp
import numpy as np
from jax import lax

D = 1024
HEADS = 16
FF = 2048
HEAD_DIM = 64
MB = 2
BATCH = 4
LEN = 1024


def levels(own_key, shape, cuts, least, high):
    level = 1.0
    for dim, parts in cuts:
        draws = jax.random.uniform(jax.random.fold_in(jax.random.fold_in(own_key, 6), dim), (parts,), jnp.float32, least / len(cuts), high / len(cuts))
        level = level * jnp.repeat(jnp.exp(draws), shape[dim] // parts).reshape((-1,) + (1,) * (len(shape) - 1 - dim))
    return level


def profile(amount, total, reach, lean):
    portions = [(1 << 20) // math.isqrt(rank ** lean) + 1 for rank in range(2, amount + 1)]
    rest, given = total - reach - (amount - 1), [1] * (amount - 1)
    while rest > 0:
        candidates = [i for i in range(amount - 1) if given[i] < reach]
        whole, budget = sum([portions[i] for i in candidates]), rest
        for i in candidates:
            more = min(reach - given[i], max(1, budget * portions[i] // whole), rest)
            given[i] = given[i] + more
            rest = rest - more
    return np.array([reach] + given)


def uneven(rng, amount, total, limit, skew):
    if amount == 2:
        one = jax.random.randint(rng, (), max(1, total - limit), min(limit, total - 1) + 1)
        return jnp.stack([one, total - one])
    sizes = jnp.asarray(profile(amount, total, limit, skew), jnp.int32)
    couples = (amount - 1) // 2
    giver, taker = sizes[1:1 + 2 * couples:2], sizes[2:2 + 2 * couples:2]
    room = jnp.minimum(giver - 1, limit - taker)
    passed = jax.random.randint(jax.random.fold_in(rng, 1), (couples,), 0, 1 << 20) % (room + 1)
    sizes = sizes.at[1:1 + 2 * couples:2].set(giver - passed).at[2:2 + 2 * couples:2].set(taker + passed)
    return sizes[jax.random.permutation(jax.random.fold_in(rng, 2), amount)]


def noise(key, shape, width, limit, cuts=(), kind=jnp.bfloat16):
    entries = width * jax.random.normal(key, shape, jnp.float32)
    if cuts:
        entries = entries * levels(key, shape, cuts, -0.22, 0.18)
    return jnp.clip(entries, -limit, limit).astype(kind)


def setup_inputs(seed: int = 0) -> dict:
    key_of = jax.random.split(jax.random.key(seed), 12)
    frames = noise(key_of[0], (MB, BATCH, LEN, D), 1.0, 6.0, ((1, 2), (2, 16)))
    time_embed = noise(key_of[1], (MB, BATCH, D), 1.0, 6.0, (), jnp.float32)
    lengths = jax.vmap(lambda own: uneven(own, BATCH, BATCH * LEN * 5 // 8, LEN, 1))(jax.random.split(key_of[2], MB)).reshape((MB, BATCH)).astype(jnp.int32)
    w_query = noise(key_of[3], (D, D), D ** -0.5, 0.1875, ((0, 16), (1, 2)))
    w_key = noise(key_of[4], (D, D), D ** -0.5, 0.1875, ((0, 16), (1, 2)))
    w_value = noise(key_of[5], (D, D), D ** -0.5, 0.1875, ((0, 16), (1, 2)))
    w_out = noise(key_of[6], (D, D), (D // 16) ** -0.5, 0.75, ((0, 2), (1, 16)))
    w_up = noise(key_of[7], (D, FF), D ** -0.5, 0.1875, ((0, 16), (1, 2)))
    w_down = noise(key_of[8], (FF, D), FF ** -0.5, 0.125, ((0, 2), (1, 16)))
    w_mod = noise(key_of[9], (D, 6 * D), D ** -0.5, 0.1875, ((0, 16), (1, 2)))
    out_grad = noise(key_of[10], (MB, BATCH, LEN, D), 1.0, 6.0, ((1, 2), (2, 16)))
    return {"frames": frames, "time_embed": time_embed, "lengths": lengths, "w_query": w_query, "w_key": w_key, "w_value": w_value, "w_out": w_out, "w_up": w_up, "w_down": w_down, "w_mod": w_mod, "out_grad": out_grad}


EPSILON = 1e-06
HIGHEST = lax.Precision.HIGHEST

@jax.custom_vjp
def low(v):
    return lax.optimization_barrier(v.astype(jnp.bfloat16)).astype(jnp.float32)

@jax.custom_vjp
def low_back(v):
    return v

def low_keep(v):
    return (low(v), None)

def low_pass(kept, grad):
    return (grad,)

def back_keep(v):
    return (v, None)

def back_low(kept, grad):
    return (low(grad),)
low.defvjp(low_keep, low_pass)
low_back.defvjp(back_keep, back_low)

def layer_norm(values):
    center = values - lax.optimization_barrier(jnp.mean(values, axis=-1, keepdims=True))
    return center * lax.rsqrt(lax.optimization_barrier(jnp.mean(center * center, axis=-1, keepdims=True)) + EPSILON)

def rotary_tables(first_row, row_count, column_count, head_size):
    position = (first_row + jnp.arange(row_count)).astype(jnp.float32)
    column = (jnp.arange(column_count) % head_size // 2).astype(jnp.float32)
    inverse = jnp.exp(column * (-2.0 * math.log(10000.0) / head_size))
    angles = position[:, None] * inverse[None, :]
    return (jnp.cos(angles), jnp.sin(angles))

def turn_half(values):
    paired = values.reshape(values.shape[:-1] + (values.shape[-1] // 2, 2))
    return jnp.stack((-paired[..., 1], paired[..., 0]), axis=-1).reshape(values.shape)

def rotate(values, cosine, sine_table):
    return values * cosine + turn_half(values) * sine_table

def to_heads(matrix):
    return matrix.reshape(LEN, HEADS, HEAD_DIM).transpose(1, 0, 2)

def item_forward(frame_rows, time_row, length, query_w, key_w, value_w, out_w, up_w, down_w, mod_w):
    silu_time = low(jax.nn.silu(time_row))
    modulation = low(jnp.dot(silu_time, mod_w, precision=HIGHEST))
    shift_attn = modulation[0:D]
    scale_attn = modulation[D:2 * D]
    gate_attn = modulation[2 * D:3 * D]
    shift_ff = modulation[3 * D:4 * D]
    scale_ff = modulation[4 * D:5 * D]
    gate_ff = modulation[5 * D:6 * D]
    position = jnp.arange(LEN)
    key_live = position < length
    frame_mask = key_live.astype(jnp.float32)
    cosine, sine_table = rotary_tables(0, LEN, D, HEAD_DIM)
    normed_a = low(layer_norm(frame_rows))
    modulated_a = low(normed_a * (1.0 + scale_attn) + shift_attn)
    query_lin = low_back(jnp.dot(modulated_a, query_w, precision=HIGHEST))
    key_lin = low_back(jnp.dot(modulated_a, key_w, precision=HIGHEST))
    value_rows = low(low_back(jnp.dot(modulated_a, value_w, precision=HIGHEST)))
    queries = low(rotate(query_lin, cosine, sine_table))
    key_rows = low(rotate(key_lin, cosine, sine_table))

    def one_head(pieces):
        head_query, head_key, head_value = pieces
        scores = low_back(jnp.dot(head_query, head_key.T, precision=HIGHEST) * HEAD_DIM ** (-0.5))
        scores = jnp.where(key_live[None, :], scores, -1e+30)
        chances = jax.nn.softmax(scores, axis=-1)
        return jnp.dot(low(chances), head_value, precision=HIGHEST)
    attended = lax.map(jax.checkpoint(one_head), (to_heads(queries), to_heads(key_rows), to_heads(value_rows)))
    attended = low(low_back(attended.transpose(1, 0, 2).reshape(LEN, D)))
    branch_a = low_back(jnp.dot(attended, out_w, precision=HIGHEST))
    middle = frame_rows + gate_attn * frame_mask[:, None] * branch_a
    normed_f = low(layer_norm(middle))
    modulated_f = low(normed_f * (1.0 + scale_ff) + shift_ff)
    upper = low_back(jnp.dot(modulated_f, up_w, precision=HIGHEST))
    active = low(jax.nn.gelu(upper, approximate=True))
    branch_f = low_back(jnp.dot(active, down_w, precision=HIGHEST))
    return middle + gate_ff * branch_f

def reference(frames, time_embed, lengths, w_query, w_key, w_value, w_out, w_up, w_down, w_mod, out_grad):
    weights = tuple((matrix.astype(jnp.float32) for matrix in (w_query, w_key, w_value, w_out, w_up, w_down, w_mod)))
    item_frames = frames.reshape(MB * BATCH, LEN, D)
    item_times = time_embed.reshape(MB * BATCH, D)
    item_lengths = lengths.reshape(MB * BATCH)
    item_grads = out_grad.reshape(MB * BATCH, LEN, D)

    def visit(totals, pieces):
        frame_rows, time_row, length, cotangent = pieces

        def forward(rows, *matrices):
            return item_forward(rows, time_row, length, *matrices)
        result, pullback = jax.vjp(forward, frame_rows.astype(jnp.float32), *weights)
        gradients = pullback(cotangent.astype(jnp.float32))
        totals = tuple((total + extra for total, extra in zip(totals, gradients[1:])))
        return (totals, (result.astype(jnp.bfloat16), gradients[0].astype(jnp.bfloat16)))
    zeros = tuple((jnp.zeros(matrix.shape, jnp.float32) for matrix in weights))
    totals, (results, input_grads) = lax.scan(visit, zeros, (item_frames, item_times, item_lengths, item_grads))
    return (results.reshape(frames.shape), input_grads.reshape(frames.shape), totals[0], totals[1], totals[2], totals[3], totals[4], totals[5], totals[6])
```

```python
from functools import partial
import math

import jax
import jax.numpy as jnp
from jax import lax
from jax.experimental import pallas as pl
from jax.experimental.pallas import tpu as pltpu
from jax.sharding import PartitionSpec as P

D = 1024
HEAD_DIM = 64
EPSILON = 1e-06
NEGATIVE = -1e30
BF = jnp.bfloat16
F32 = jnp.float32
HIGHEST = lax.Precision.HIGHEST
MESH = pl.DeviceIdType.MESH
ANY = pl.BlockSpec(memory_space=pl.ANY)
VMEM = pl.BlockSpec(memory_space=pltpu.VMEM)
LIMIT = 60 * 1024 * 1024


def nn(a, b):
    return lax.dot_general(a, b, (((1,), (0,)), ((), ())), preferred_element_type=F32)


def nt(a, b):
    return lax.dot_general(a, b, (((1,), (1,)), ((), ())), preferred_element_type=F32)


class Place:
    def __init__(self, S, T, I):
        self.S, self.T, self.I = S, T, I
        self.Z, self.R = S // 4, S // I
        self.Q = self.R // 2
        self.s, self.t = lax.axis_index("seq"), lax.axis_index("tp")
        self.z = lax.div(self.s, 4)
        self.x = lax.rem(lax.div(self.s, 2), 2)
        self.c = lax.rem(self.s, 2)
        self.i = lax.div(self.s, self.R)
        self.r = lax.rem(self.s, self.R)
        self.q = lax.div(self.r, 2)

    def at(self, z=None, x=None, c=None, t=None):
        z = self.z if z is None else z
        x = self.x if x is None else x
        c = self.c if c is None else c
        t = self.t if t is None else t
        return ((z * 2 + x) * 2 + c, t)

    def tp(self, k):
        return (self.s, lax.rem(self.t + k, self.T))

    def zs(self, k):
        return lax.rem(self.z + k, self.Z)

    def group(self, k, c=None):
        c = self.c if c is None else c
        return (self.i * self.R + lax.rem(self.q + k, self.Q) * 2 + c, self.t)


class Wires:
    def __init__(self, send, recv, local):
        self.send, self.recv, self.local = send, recv, local
        self.remote_count = self.local_count = 0
        self.sent = []

    def push(self, src, dst, device):
        n = self.remote_count
        self.remote_count += 1
        copy = pltpu.make_async_remote_copy(
            src_ref=src,
            dst_ref=dst,
            send_sem=self.send.at[n],
            recv_sem=self.recv.at[n],
            device_id=device,
            device_id_type=MESH,
        )
        copy.start()
        self.sent.append(copy)
        return copy

    def move(self, src, dst):
        n = self.local_count
        self.local_count += 1
        copy = pltpu.make_async_copy(src, dst, self.local.at[n])
        copy.start()
        return copy

    def close(self):
        for copy in self.sent:
            copy.wait_send()


def landed(copies):
    for copy in copies:
        copy.wait_recv()


def greet_all(place):
    total = place.S * place.T
    me = place.s * place.T + place.t
    barrier = pltpu.get_barrier_semaphore()

    def body(d, carry):
        other = lax.rem(me + d, total)
        pl.semaphore_signal(
            barrier,
            inc=1,
            device_id=(lax.div(other, place.T), lax.rem(other, place.T)),
            device_id_type=MESH,
        )
        return carry

    lax.fori_loop(1, total, body, 0)
    pl.semaphore_wait(barrier, total - 1)


def greet_group(place):
    barrier = pltpu.get_barrier_semaphore()
    pl.semaphore_signal(barrier, inc=1, device_id=place.group(0, 1 - place.c), device_id_type=MESH)
    for k in range(1, place.Q):
        pl.semaphore_signal(barrier, inc=1, device_id=place.group(k), device_id_type=MESH)
    pl.semaphore_wait(barrier, place.Q)


def scatter_rows(place, send, recv, copy_of):
    total = place.S * place.T
    me = place.s * place.T + place.t

    def copy(d):
        other = lax.rem(me + d, total)
        s, t = lax.div(other, place.T), lax.rem(other, place.T)
        src, dst = copy_of(s, t)
        return pltpu.make_async_remote_copy(
            src_ref=src,
            dst_ref=dst,
            send_sem=send.at[d],
            recv_sem=recv.at[d],
            device_id=(s, t),
            device_id_type=MESH,
        )

    def start(d, carry):
        copy(d).start()
        return carry

    def wait(d, carry):
        copy(d).wait()
        return carry

    lax.fori_loop(1, total, start, 0)
    return lambda: lax.fori_loop(1, total, wait, 0)


class Gather:
    def __init__(self, place, wires, src, dst):
        self.p, self.w, self.src, self.dst = place, wires, src, dst
        half = src.shape[0] // 2
        self.upper, self.lower = pl.ds(0, half), pl.ds(half, half)

    def phase0(self):
        p, w, dst = self.p, self.w, self.dst
        own = dst.at[0, p.z, p.x, p.c]
        self.own = w.move(self.src, own)
        self.along = [w.push(self.src, own, p.at(z=p.zs(k))) for k in range(1, p.Z)]

    def phase1(self):
        p, w, dst = self.p, self.w, self.dst
        self.own.wait()
        landed(self.along)
        line = dst.at[0, :, p.x, p.c]
        self.sides = [
            w.push(
                dst.at[0, :, p.x, p.c, self.upper],
                dst.at[0, :, p.x, p.c, self.upper],
                p.at(x=1 - p.x),
            )
        ]
        for k in range(1, p.T):
            self.sides.append(
                w.push(
                    dst.at[0, :, p.x, p.c, self.lower],
                    dst.at[p.T - k, :, p.x, p.c, self.lower],
                    p.tp(k),
                )
            )
        self.cores = [w.push(line, line, p.at(c=1 - p.c))]

    def phase2(self):
        p, w, dst = self.p, self.w, self.dst
        landed(self.sides)
        self.last = []
        for k in range(1, p.T):
            self.last.append(
                w.push(
                    dst.at[0, :, :, p.c, self.upper],
                    dst.at[p.T - k, :, :, p.c, self.upper],
                    p.tp(k),
                )
            )
        part = dst.at[:, :, p.x, p.c, self.lower]
        self.last.append(w.push(part, part, p.at(x=1 - p.x)))
        part = dst.at[0, :, 1 - p.x, p.c, self.upper]
        self.cores.append(w.push(part, part, p.at(c=1 - p.c)))
        part = dst.at[pl.ds(1, p.T - 1), :, p.x, p.c, self.lower]
        self.cores.append(w.push(part, part, p.at(c=1 - p.c)))

    def phase3(self):
        p, w, dst = self.p, self.w, self.dst
        landed(self.last)
        part = dst.at[pl.ds(1, p.T - 1), :, :, p.c, self.upper]
        self.cores.append(w.push(part, part, p.at(c=1 - p.c)))
        part = dst.at[:, :, 1 - p.x, p.c, self.lower]
        self.cores.append(w.push(part, part, p.at(c=1 - p.c)))

    def phase4(self):
        landed(self.cores)


class Reduce:
    def __init__(self, place, wires, src, out, own, core, y_up, x_low, x_up, y_low, z_in):
        self.p, self.w, self.src, self.out = place, wires, src, out
        self.own, self.core, self.y_up, self.x_low = own, core, y_up, x_low
        self.x_up, self.y_low, self.z_in = x_up, y_low, z_in
        half = own.shape[3] // 2
        self.half = half
        self.upper, self.lower = pl.ds(0, half), pl.ds(half, half)

    @staticmethod
    def scratch(T, Z, rs, C):
        half = rs // 2
        return [
            pltpu.VMEM((T, Z, 2, rs, C), BF),
            pltpu.VMEM((T, Z, 2, rs, C), BF),
            pltpu.VMEM((T - 1, Z, 2, half, C), BF),
            pltpu.VMEM((T, Z, half, C), BF),
            pltpu.VMEM((Z, half, C), BF),
            pltpu.VMEM((T - 1, Z, half, C), BF),
            pltpu.VMEM((Z - 1, rs, C), BF),
        ]

    def phase0(self):
        p, w, src = self.p, self.w, self.src
        self.mine = w.move(src.at[:, :, :, p.c], self.own)
        self.pair = [w.push(src.at[:, :, :, 1 - p.c], self.core, p.at(c=1 - p.c))]

    def phase1(self):
        p, w, own = self.p, self.w, self.own
        self.mine.wait()
        landed(self.pair)

        def add(n, carry):
            k, z = lax.div(n, p.Z), lax.rem(n, p.Z)
            for x in range(2):
                own[k, z, x] = own[k, z, x] + self.core[k, z, x]
            return carry

        lax.fori_loop(0, p.T * p.Z, add, 0)
        self.sides = [
            w.push(own.at[k, :, :, self.upper], self.y_up.at[k - 1], p.tp(k))
            for k in range(1, p.T)
        ]
        self.sides.append(w.push(own.at[:, :, 1 - p.x, self.lower], self.x_low, p.at(x=1 - p.x)))

    def phase2(self):
        p, w, own = self.p, self.w, self.own
        landed(self.sides)

        def add(z, carry):
            for x in range(2):
                total = own[0, z, x, self.upper].astype(F32)
                for k in range(1, p.T):
                    total = total + self.y_up[k - 1, z, x].astype(F32)
                own[0, z, x, self.upper] = total.astype(BF)
            for k in range(p.T):
                own[k, z, p.x, self.lower] = own[k, z, p.x, self.lower] + self.x_low[k, z]
            return carry

        lax.fori_loop(0, p.Z, add, 0)
        self.last = [w.push(own.at[0, :, 1 - p.x, self.upper], self.x_up, p.at(x=1 - p.x))]
        for k in range(1, p.T):
            self.last.append(
                w.push(own.at[k, :, p.x, self.lower], self.y_low.at[k - 1], p.tp(k))
            )

    def phase3(self):
        p, w, own = self.p, self.w, self.own
        landed(self.last)

        def add(z, carry):
            own[0, z, p.x, self.upper] = own[0, z, p.x, self.upper] + self.x_up[z]
            total = own[0, z, p.x, self.lower].astype(F32)
            for k in range(1, p.T):
                total = total + self.y_low[k - 1, z].astype(F32)
            own[0, z, p.x, self.lower] = total.astype(BF)
            return carry

        lax.fori_loop(0, p.Z, add, 0)
        self.along = [
            w.push(own.at[0, p.zs(k), p.x], self.z_in.at[k - 1], p.at(z=p.zs(k)))
            for k in range(1, p.Z)
        ]

    def phase4(self):
        p = self.p
        landed(self.along)
        total = self.own[0, p.z, p.x].astype(F32)
        for k in range(1, p.Z):
            total = total + self.z_in[k - 1].astype(F32)
        self.out[...] = total


def swap_items(place, wires, src, dst):
    p = place
    own = wires.move(src.at[p.i], dst.at[p.i])
    copies = []
    for k in range(1, p.I):
        other = lax.rem(p.i + k, p.I)
        copies.append(wires.push(src.at[other], dst.at[p.i], (other * p.R + p.r, p.t)))
    return own, copies


def first_kernel(
    S, T, I, frames, cotangent, parts, w_a, w_f,
    frames_out, cotangent_out, parts_out, all_a, all_f,
    send, recv, local, row_send, row_recv,
):
    p = Place(S, T, I)
    wires = Wires(send, recv, local)
    greet_all(p)
    frames_own, frames_in = swap_items(p, wires, frames, frames_out)
    rows_done = scatter_rows(
        p, row_send, row_recv,
        lambda s, t: (parts.at[t, lax.div(s, p.R)], parts_out.at[p.t, p.s]),
    )
    parts_own = wires.move(parts.at[p.t, p.i], parts_out.at[p.t, p.s])
    a, f = Gather(p, wires, w_a, all_a), Gather(p, wires, w_f, all_f)
    a.phase0()
    cotangent_own, cotangent_in = swap_items(p, wires, cotangent, cotangent_out)
    f.phase0()
    a.phase1()
    f.phase1()
    a.phase2()
    f.phase2()
    a.phase3()
    f.phase3()
    a.phase4()
    f.phase4()
    for own in (frames_own, parts_own, cotangent_own):
        own.wait()
    landed(frames_in)
    landed(cotangent_in)
    rows_done()
    wires.close()


def first_call(S, T, I, frames, cotangent, parts, w_a, w_f):
    rs = w_a.shape[0]
    Z = S // 4
    remote = 2 * (I - 1) + 2 * (Z - 1 + 2 * T + 5)
    out_shape = (
        jax.ShapeDtypeStruct(frames.shape, BF),
        jax.ShapeDtypeStruct(cotangent.shape, BF),
        jax.ShapeDtypeStruct((T, S) + parts.shape[2:], F32),
        jax.ShapeDtypeStruct((T, Z, 2, 2, rs, w_a.shape[1]), BF),
        jax.ShapeDtypeStruct((T, Z, 2, 2, rs, w_f.shape[1]), BF),
    )
    return pl.pallas_call(
        partial(first_kernel, S, T, I),
        out_shape=out_shape,
        in_specs=[ANY] * 5,
        out_specs=(ANY,) * 5,
        scratch_shapes=[
            pltpu.SemaphoreType.DMA((remote,)),
            pltpu.SemaphoreType.DMA((remote,)),
            pltpu.SemaphoreType.DMA((8,)),
            pltpu.SemaphoreType.DMA((S * T,)),
            pltpu.SemaphoreType.DMA((S * T,)),
        ],
        compiler_params=pltpu.CompilerParams(
            collective_id=0, has_side_effects=True, vmem_limit_bytes=LIMIT
        ),
        name="spread_inputs",
    )(frames, cotangent, parts, w_a, w_f)


def share_kernel(S, T, I, own, out, send, recv, local):
    p = Place(S, T, I)
    wires = Wires(send, recv, local)
    greet_group(p)
    across = [wires.push(own, out.at[p.Q - k, 0], p.group(k)) for k in range(1, p.Q)]
    sibling = p.group(0, 1 - p.c)
    cores = [wires.push(own, out.at[0, 1], sibling)]
    mine = wires.move(own, out.at[0, 0])
    for k in range(1, p.Q):
        across[k - 1].wait_recv()
        cores.append(wires.push(out.at[p.Q - k, 0], out.at[p.Q - k, 1], sibling))
    landed(cores)
    mine.wait()
    wires.close()


def share_call(S, T, I, own):
    Q = S // I // 2
    count = 2 * Q
    return pl.pallas_call(
        partial(share_kernel, S, T, I),
        out_shape=jax.ShapeDtypeStruct((Q, 2) + own.shape, BF),
        in_specs=[ANY],
        out_specs=ANY,
        scratch_shapes=[
            pltpu.SemaphoreType.DMA((count,)),
            pltpu.SemaphoreType.DMA((count,)),
            pltpu.SemaphoreType.DMA((1,)),
        ],
        compiler_params=pltpu.CompilerParams(
            collective_id=1, has_side_effects=True, vmem_limit_bytes=LIMIT
        ),
        name="share_rows",
    )(own)


def unshare_kernel(S, T, I, parts, out, near, far, pair, send, recv, local):
    p = Place(S, T, I)
    wires = Wires(send, recv, local)
    greet_group(p)
    core = wires.push(parts.at[:, 1], near, p.group(0, 1 - p.c))
    core.wait_recv()
    across = []
    for k in range(1, p.Q):
        pair[k - 1] = parts[k, 0] + near[k]
        across.append(wires.push(pair.at[k - 1], far.at[k - 1], p.group(k)))
    total = parts[0, 0].astype(F32) + near[0].astype(F32)
    for k in range(1, p.Q):
        across[k - 1].wait_recv()
        total = total + far[k - 1].astype(F32)
    out[...] = total
    wires.close()


def unshare_call(S, T, I, parts):
    Q = S // I // 2
    block = parts.shape[2:]
    return pl.pallas_call(
        partial(unshare_kernel, S, T, I),
        out_shape=jax.ShapeDtypeStruct(block, F32),
        in_specs=[VMEM],
        out_specs=VMEM,
        scratch_shapes=[
            pltpu.VMEM((Q,) + block, BF),
            pltpu.VMEM((Q - 1,) + block, BF),
            pltpu.VMEM((Q - 1,) + block, BF),
            pltpu.SemaphoreType.DMA((Q,)),
            pltpu.SemaphoreType.DMA((Q,)),
            pltpu.SemaphoreType.DMA((1,)),
        ],
        compiler_params=pltpu.CompilerParams(
            collective_id=2, has_side_effects=True, vmem_limit_bytes=LIMIT
        ),
        name="sum_rows",
    )(parts)


def last_kernel(S, T, I, *refs):
    (layer, grads, rows, grad_a, grad_f,
     layer_out, grads_out, rows_out, sum_a, sum_f) = refs[:10]
    scratch_a, scratch_f = refs[10:17], refs[17:24]
    send, recv, local, row_send, row_recv = refs[24:]
    p = Place(S, T, I)
    wires = Wires(send, recv, local)
    greet_all(p)
    f = Reduce(p, wires, grad_f, sum_f, *scratch_f)
    a = Reduce(p, wires, grad_a, sum_a, *scratch_a)
    f.phase0()
    a.phase0()
    grads_own, grads_in = swap_items(p, wires, grads, grads_out)
    layer_own, layer_in = swap_items(p, wires, layer, layer_out)
    rows_done = scatter_rows(
        p, row_send, row_recv, lambda s, t: (rows.at[t], rows_out.at[p.t, p.s])
    )
    rows_own = wires.move(rows.at[p.t], rows_out.at[p.t, p.s])
    f.phase1()
    a.phase1()
    f.phase2()
    a.phase2()
    f.phase3()
    a.phase3()
    f.phase4()
    a.phase4()
    for own in (grads_own, layer_own, rows_own):
        own.wait()
    landed(grads_in)
    landed(layer_in)
    rows_done()
    wires.close()


def last_call(S, T, I, layer, grads, rows, grad_a, grad_f):
    Z, rs = S // 4, grad_a.shape[4]
    ca, cf = grad_a.shape[5], grad_f.shape[5]
    remote = 2 * (I - 1) + 2 * (Z + 2 * T + 2)
    return pl.pallas_call(
        partial(last_kernel, S, T, I),
        out_shape=(
            jax.ShapeDtypeStruct(layer.shape, BF),
            jax.ShapeDtypeStruct(grads.shape, BF),
            jax.ShapeDtypeStruct((T, S) + rows.shape[1:], F32),
            jax.ShapeDtypeStruct((rs, ca), F32),
            jax.ShapeDtypeStruct((rs, cf), F32),
        ),
        in_specs=[ANY] * 5,
        out_specs=(ANY, ANY, ANY, VMEM, VMEM),
        scratch_shapes=Reduce.scratch(T, Z, rs, ca)
        + Reduce.scratch(T, Z, rs, cf)
        + [
            pltpu.SemaphoreType.DMA((remote,)),
            pltpu.SemaphoreType.DMA((remote,)),
            pltpu.SemaphoreType.DMA((8,)),
            pltpu.SemaphoreType.DMA((S * T,)),
            pltpu.SemaphoreType.DMA((S * T,)),
        ],
        compiler_params=pltpu.CompilerParams(
            collective_id=3, has_side_effects=True, vmem_limit_bytes=LIMIT
        ),
        name="collect_outputs",
    )(layer, grads, rows, grad_a, grad_f)


def swap_pairs(v):
    lane = lax.broadcasted_iota(jnp.int32, v.shape, 1)
    return jnp.where(lax.rem(lane, 2) == 0, pltpu.roll(v, 127, 1), pltpu.roll(v, 1, 1))


def head_split(v):
    lane = lax.broadcasted_iota(jnp.int32, v.shape, 1)
    zero = jnp.zeros_like(v)
    return jnp.where(lane < HEAD_DIM, v, zero), jnp.where(lane < HEAD_DIM, zero, v)


def first_lane(rows):
    lane = lax.broadcasted_iota(jnp.int32, (rows, 128), 1)
    return jnp.where(lane == 0, 1.0, 0.0).astype(BF)


def attend_kernel(
    rows, cb, xm_ref, w_ref, cos_ref, sin_ref, mask_ref,
    q_ref, k_ref, v_ref, att_ref, lse_ref, branch_ref,
):
    step = pl.program_id(0)
    q_lin = nn(xm_ref[0:rows, :], w_ref[0, :, 0:cb])
    k_lin = nn(xm_ref[...], w_ref[0, :, cb : 2 * cb])
    v_ref[...] = nn(xm_ref[...], w_ref[0, :, 2 * cb : 3 * cb]).astype(BF)
    ones = first_lane(rows)
    factor = HEAD_DIM**-0.5
    for p in range(cb // 128):
        lanes = slice(p * 128, p * 128 + 128)
        q2, k2 = q_lin[:, lanes], k_lin[:, lanes]
        q2 = (q2 * cos_ref[0:rows, :] + swap_pairs(q2) * sin_ref[0:rows, :]).astype(BF)
        q2 = q2 * jnp.asarray(factor, BF)
        k2 = (k2 * cos_ref[...] + swap_pairs(k2) * sin_ref[...]).astype(BF)
        q_ref[:, lanes] = q2
        k_ref[:, lanes] = k2
        k_long = jnp.concatenate([k2, mask_ref[...]], axis=1)
        v_turned = v_ref[:, lanes].T
        outs = []
        for h, q1 in enumerate(head_split(q2)):
            scores = nt(k_long, jnp.concatenate([q1, ones], axis=1))
            highest = jnp.max(scores, axis=0, keepdims=True)
            unnormed = jnp.exp(scores - highest)
            total = jnp.sum(unnormed, axis=0, keepdims=True)
            probs = (unnormed * (1.0 / total)).astype(BF)
            lse_ref[0, pl.ds(2 * p + h, 1), :] = highest + jnp.log(total)
            outs.append(nn(v_turned[h * HEAD_DIM : (h + 1) * HEAD_DIM], probs))
        att_ref[:, lanes] = jnp.concatenate(outs, axis=0).T.astype(BF)
    part = nt(att_ref[...], w_ref[0, :, 3 * cb : 4 * cb])

    @pl.when(step == 0)
    def _():
        branch_ref[...] = part

    @pl.when(step > 0)
    def _():
        branch_ref[...] += part


def attend_call(rows, cb, xm, w_all, cosine, sine, mask):
    T, _, wide = w_all.shape
    per_t = wide // (4 * cb)
    L = xm.shape[0]
    steps = T * per_t
    fixed = lambda n: (0, 0)
    column = lambda n: (0, n)
    return pl.pallas_call(
        partial(attend_kernel, rows, cb),
        grid=(steps,),
        out_shape=(
            jax.ShapeDtypeStruct((rows, D), BF),
            jax.ShapeDtypeStruct((L, D), BF),
            jax.ShapeDtypeStruct((L, D), BF),
            jax.ShapeDtypeStruct((rows, D), BF),
            jax.ShapeDtypeStruct((steps, 8, rows), F32),
            jax.ShapeDtypeStruct((rows, D), F32),
        ),
        in_specs=[
            pl.BlockSpec((L, D), fixed),
            pl.BlockSpec((1, D, 4 * cb), lambda n: (n // per_t, 0, n % per_t)),
            pl.BlockSpec((L, 128), fixed),
            pl.BlockSpec((L, 128), fixed),
            pl.BlockSpec((L, 128), fixed),
        ],
        out_specs=(
            pl.BlockSpec((rows, cb), column),
            pl.BlockSpec((L, cb), column),
            pl.BlockSpec((L, cb), column),
            pl.BlockSpec((rows, cb), column),
            pl.BlockSpec((1, 8, rows), lambda n: (n, 0, 0)),
            pl.BlockSpec((rows, D), fixed),
        ),
        compiler_params=pltpu.CompilerParams(vmem_limit_bytes=LIMIT),
        name="attend",
    )(xm, w_all, cosine, sine, mask)


def attend_back_kernel(
    rows, cb, db_ref, xm_ref, w_ref, cos_ref, sin_ref, mask_ref,
    q_ref, k_ref, v_ref, att_ref, lse_ref,
    grad_ref, dx_ref, xm_turned, db_turned, dx_sum,
):
    step = pl.program_id(0)

    @pl.when(step == 0)
    def _():
        xm_turned[...] = xm_ref[...].T
        db_turned[...] = db_ref[...].T
        dx_sum[...] = jnp.zeros_like(dx_sum)

    d_att = nn(db_ref[...], w_ref[0, :, 3 * cb : 4 * cb]).astype(BF)
    grad_ref[0, :, 3 * cb : 4 * cb] = nn(db_turned[...], att_ref[...]).astype(BF)
    ones = first_lane(rows)
    factor = HEAD_DIM**-0.5
    dqs, dks, dvs = [], [], []
    for p in range(cb // 128):
        lanes = slice(p * 128, p * 128 + 128)
        q2, k2, v2 = q_ref[:, lanes], k_ref[:, lanes], v_ref[:, lanes]
        k_long = jnp.concatenate([k2, mask_ref[...]], axis=1)
        k_turned = k2.T
        dq_parts, ds_all, p_all = [], [], []
        q_heads, d_heads = head_split(q2), head_split(d_att[:, lanes])
        for h in range(2):
            scores = nt(k_long, jnp.concatenate([q_heads[h], ones], axis=1))
            probs = jnp.exp(scores - lse_ref[0, pl.ds(2 * p + h, 1), :])
            d_probs = nt(v2, d_heads[h])
            row_dot = jnp.sum(probs * d_probs, axis=0, keepdims=True)
            d_scores = (probs * (d_probs - row_dot)).astype(BF)
            dq_parts.append(nn(k_turned[h * HEAD_DIM : (h + 1) * HEAD_DIM], d_scores))
            ds_all.append(d_scores)
            p_all.append(probs.astype(BF))
        dk2 = nn(jnp.concatenate(ds_all, axis=1), jnp.concatenate(q_heads, axis=0))
        dv2 = nn(jnp.concatenate(p_all, axis=1), jnp.concatenate(d_heads, axis=0))
        dq2 = jnp.concatenate(dq_parts, axis=0).T * factor
        dqs.append(
            (dq2 * cos_ref[0:rows, :] - swap_pairs(dq2) * sin_ref[0:rows, :]).astype(BF)
        )
        dks.append((dk2 * cos_ref[...] - swap_pairs(dk2) * sin_ref[...]).astype(BF))
        dvs.append(dv2.astype(BF))
    dq, dk, dv = (jnp.concatenate(v, axis=1) for v in (dqs, dks, dvs))
    grad_ref[0, :, 0:cb] = nn(xm_turned[:, 0:rows], dq).astype(BF)
    grad_ref[0, :, cb : 2 * cb] = nn(xm_turned[...], dk).astype(BF)
    grad_ref[0, :, 2 * cb : 3 * cb] = nn(xm_turned[...], dv).astype(BF)
    dx_sum[...] += nt(
        jnp.concatenate([dk, dv], axis=1), w_ref[0, :, cb : 3 * cb]
    )
    dx_sum[0:rows, :] += nt(dq, w_ref[0, :, 0:cb])

    @pl.when(step == pl.num_programs(0) - 1)
    def _():
        dx_ref[...] = dx_sum[...].astype(BF)


def attend_back_call(rows, cb, d_branch, xm, w_all, cosine, sine, mask, q, k, v, att, lse):
    T, _, wide = w_all.shape
    per_t = wide // (4 * cb)
    L = xm.shape[0]
    steps = T * per_t
    fixed = lambda n: (0, 0)
    column = lambda n: (0, n)
    weight = pl.BlockSpec((1, D, 4 * cb), lambda n: (n // per_t, 0, n % per_t))
    return pl.pallas_call(
        partial(attend_back_kernel, rows, cb),
        grid=(steps,),
        out_shape=(
            jax.ShapeDtypeStruct(w_all.shape, BF),
            jax.ShapeDtypeStruct((L, D), BF),
        ),
        in_specs=[
            pl.BlockSpec((rows, D), fixed),
            pl.BlockSpec((L, D), fixed),
            weight,
            pl.BlockSpec((L, 128), fixed),
            pl.BlockSpec((L, 128), fixed),
            pl.BlockSpec((L, 128), fixed),
            pl.BlockSpec((rows, cb), column),
            pl.BlockSpec((L, cb), column),
            pl.BlockSpec((L, cb), column),
            pl.BlockSpec((rows, cb), column),
            pl.BlockSpec((1, 8, rows), lambda n: (n, 0, 0)),
        ],
        out_specs=(weight, pl.BlockSpec((L, D), fixed)),
        scratch_shapes=[
            pltpu.VMEM((D, L), BF),
            pltpu.VMEM((D, rows), BF),
            pltpu.VMEM((L, D), F32),
        ],
        compiler_params=pltpu.CompilerParams(vmem_limit_bytes=LIMIT),
        name="attend_back",
    )(d_branch, xm, w_all, cosine, sine, mask, q, k, v, att, lse)


def layer_stats(values):
    center = values - jnp.mean(values, axis=-1, keepdims=True)
    inverse = lax.rsqrt(jnp.mean(center * center, axis=-1, keepdims=True) + EPSILON)
    return center * inverse, inverse


def layer_back(normed, inverse, incoming):
    return inverse * (
        incoming
        - jnp.mean(incoming, axis=-1, keepdims=True)
        - normed * jnp.mean(incoming * normed, axis=-1, keepdims=True)
    )


def feed_kernel(
    hb, frames_ref, cot_ref, branch_ref, live_ref, mod_ref, w_ref,
    layer_ref, grad_ref, dmid_ref, dbranch_ref, dmod_ref,
    mf_ref, mf_turned, db_ref, db_turned, mid_ref, normed_ref, out_sum, dmf_sum,
):
    step = pl.program_id(0)
    gate_attn, shift_ff = mod_ref[2:3, :], mod_ref[3:4, :]
    scale_ff, gate_ff = mod_ref[4:5, :], mod_ref[5:6, :]

    @pl.when(step == 0)
    def _():
        middle = frames_ref[...].astype(F32) + gate_attn * live_ref[...] * branch_ref[...]
        mid_ref[...] = middle
        normed, _ = layer_stats(middle)
        low = normed.astype(BF)
        normed_ref[...] = low
        modulated = (low.astype(F32) * (1.0 + scale_ff) + shift_ff).astype(BF)
        mf_ref[...] = modulated
        mf_turned[...] = modulated.T
        d_branch = (cot_ref[...].astype(F32) * gate_ff).astype(BF)
        db_ref[...] = d_branch
        db_turned[...] = d_branch.T
        out_sum[...] = jnp.zeros_like(out_sum)
        dmf_sum[...] = jnp.zeros_like(dmf_sum)

    w_up, w_down = w_ref[0, :, 0:hb], w_ref[0, :, hb : 2 * hb]
    upper = nn(mf_ref[...], w_up)
    square = upper * upper
    slope = 0.7978845608
    tanh = jnp.tanh(slope * (upper + 0.044715 * upper * square))
    half = 0.5 * (1.0 + tanh)
    active = (upper * half).astype(BF)
    bend = half + 0.5 * upper * (1.0 - tanh * tanh) * (slope * (1.0 + 3 * 0.044715 * square))
    out_sum[...] += nt(active, w_down)
    d_upper = (nn(db_ref[...], w_down) * bend).astype(BF)
    dmf_sum[...] += nt(d_upper, w_up)
    grad_ref[0, :, 0:hb] = nn(mf_turned[...], d_upper).astype(BF)
    grad_ref[0, :, hb : 2 * hb] = nn(db_turned[...], active).astype(BF)

    @pl.when(step == pl.num_programs(0) - 1)
    def _():
        middle, branch_f = mid_ref[...], out_sum[...]
        layer_ref[...] = (middle + gate_ff * branch_f).astype(BF)
        cot = cot_ref[...].astype(F32)
        normed, inverse = layer_stats(middle)
        dmf = dmf_sum[...]
        d_mid = cot + layer_back(normed, inverse, dmf * (1.0 + scale_ff))
        dmid_ref[...] = d_mid
        live = d_mid * live_ref[...]
        dbranch_ref[...] = (live * gate_attn).astype(BF)
        dmod_ref[...] = jnp.zeros_like(dmod_ref)
        dmod_ref[0:1, :] = jnp.sum(live * branch_ref[...], axis=0, keepdims=True)
        dmod_ref[1:2, :] = jnp.sum(dmf, axis=0, keepdims=True)
        dmod_ref[2:3, :] = jnp.sum(dmf * normed_ref[...].astype(F32), axis=0, keepdims=True)
        dmod_ref[3:4, :] = jnp.sum(cot * branch_f, axis=0, keepdims=True)


def feed_call(hb, frames, cotangent, branch, live, mod, w_all):
    T, _, wide = w_all.shape
    per_t = wide // (2 * hb)
    rows = frames.shape[0]
    fixed = lambda n: (0, 0)
    weight = pl.BlockSpec((1, D, 2 * hb), lambda n: (n // per_t, 0, n % per_t))
    row_block = pl.BlockSpec((rows, D), fixed)
    return pl.pallas_call(
        partial(feed_kernel, hb),
        grid=(T * per_t,),
        out_shape=(
            jax.ShapeDtypeStruct((rows, D), BF),
            jax.ShapeDtypeStruct(w_all.shape, BF),
            jax.ShapeDtypeStruct((rows, D), F32),
            jax.ShapeDtypeStruct((rows, D), BF),
            jax.ShapeDtypeStruct((8, D), F32),
        ),
        in_specs=[
            row_block, row_block, row_block,
            pl.BlockSpec((rows, 1), fixed), pl.BlockSpec((6, D), fixed), weight,
        ],
        out_specs=(row_block, weight, row_block, row_block, pl.BlockSpec((8, D), fixed)),
        scratch_shapes=[
            pltpu.VMEM((rows, D), BF),
            pltpu.VMEM((D, rows), BF),
            pltpu.VMEM((rows, D), BF),
            pltpu.VMEM((D, rows), BF),
            pltpu.VMEM((rows, D), F32),
            pltpu.VMEM((rows, D), BF),
            pltpu.VMEM((rows, D), F32),
            pltpu.VMEM((rows, D), F32),
        ],
        compiler_params=pltpu.CompilerParams(vmem_limit_bytes=LIMIT),
        name="feed_forward",
    )(frames, cotangent, branch, live, mod, w_all)


def pack(blocks, width):
    rows = blocks[0].shape[0]
    cut = [b.reshape(rows, -1, 1, width) for b in blocks]
    return jnp.concatenate(cut, axis=2).reshape(rows, -1)


def unpack(packed, count, width):
    cut = packed.reshape(packed.shape[0], -1, count, width)
    return [cut[:, :, n].reshape(packed.shape[0], -1) for n in range(count)]


def per_device(
    S, T, frames, time_embed, lengths, w_query, w_key, w_value, w_out, w_up, w_down, w_mod, out_grad
):
    micro, rows_own, fl, _ = frames.shape
    batch = lengths.shape[1]
    I = micro * rows_own
    R = S // I
    Q = R // 2
    rs = w_query.shape[0]
    rows = I * fl
    L = R * rows
    cb = min(256, w_query.shape[1])
    hb = min(512, w_up.shape[1])
    s, t = lax.axis_index("seq"), lax.axis_index("tp")
    item = s // R
    place_r = s % R

    w_a = pack([w_query, w_key, w_value, w_out.T], cb)
    w_f = pack([w_up, w_down.T], hb)
    silu = jax.nn.silu(time_embed).astype(BF).reshape(micro * batch, D)
    silu_own = lax.dynamic_slice_in_dim(silu, s * rs, rs, 1)
    cols = w_mod.shape[1]
    parts = jnp.dot(silu_own, w_mod, preferred_element_type=F32)
    parts = parts.reshape(micro, T, rows_own, cols // 128, 128)
    parts = parts.transpose(1, 0, 2, 3, 4).reshape(T, I, cols // 128, 128)
    frames_in, cot_in, parts_in, all_a, all_f = first_call(
        S, T, I, frames.reshape(I, fl, D), out_grad.reshape(I, fl, D), parts, w_a, w_f
    )
    mod = jnp.sum(parts_in, axis=1).astype(BF).astype(F32).reshape(6, D)
    all_a = all_a.reshape(T, D, w_a.shape[1])
    all_f = all_f.reshape(T, D, w_f.shape[1])
    frame_rows = frames_in.reshape(rows, D)
    cot_rows = cot_in.reshape(rows, D)

    g = jnp.arange(R)
    r_of = (place_r // 2 + g // 2) % Q * 2 + (place_r % 2 + g % 2) % 2
    pos = fl * (jnp.arange(I)[None, :] * R + r_of[:, None])
    pos = (pos[:, :, None] + jnp.arange(fl)).reshape(L)
    length = lengths[item // rows_own, t * rows_own + item % rows_own]
    alive = pos < length
    live = alive[:rows].astype(F32)[:, None]
    lane = jnp.arange(128)
    mask = jnp.where((lane[None, :] == 0) & ~alive[:, None], NEGATIVE, 0.0).astype(BF)
    column = (lane % HEAD_DIM // 2).astype(F32)
    inverse = jnp.exp(column * (-2.0 * math.log(10000.0) / HEAD_DIM))
    angles = pos.astype(F32)[:, None] * inverse[None, :]
    cosine = jnp.cos(angles)
    sine = jnp.sin(angles) * jnp.where(lane % 2 == 0, -1.0, 1.0)

    normed_a, inverse_a = layer_stats(frame_rows.astype(F32))
    normed_low = normed_a.astype(BF).astype(F32)
    xm_own = (normed_low * (1.0 + mod[1:2]) + mod[0:1]).astype(BF)
    xm = share_call(S, T, I, xm_own).reshape(L, D)
    q, k, v, att, lse, branch = attend_call(rows, cb, xm, all_a, cosine, sine, mask)
    layer, grad_f, d_mid, d_branch, d_rows = feed_call(
        hb, frame_rows, cot_rows, branch, live, mod, all_f
    )
    grad_a, dx = attend_back_call(
        rows, cb, d_branch, xm, all_a, cosine, sine, mask, q, k, v, att, lse
    )
    d_mod_a = unshare_call(S, T, I, dx.reshape(Q, 2, rows, D))
    grad_in = d_mid + layer_back(normed_a, inverse_a, d_mod_a * (1.0 + mod[1:2]))
    d_modulation = jnp.concatenate(
        [
            jnp.sum(d_mod_a, axis=0, keepdims=True),
            jnp.sum(d_mod_a * normed_low, axis=0, keepdims=True),
            d_rows[0:4],
        ],
        axis=0,
    ).reshape(T, cols // 128, 128)
    shape6 = (T, S // 4, 2, 2, rs)
    layer_out, grad_input, mod_in, sum_a, sum_f = last_call(
        S, T, I, layer.reshape(I, fl, D), grad_in.astype(BF).reshape(I, fl, D), d_modulation,
        grad_a.reshape(shape6 + (w_a.shape[1],)), grad_f.reshape(shape6 + (w_f.shape[1],)),
    )
    mod_items = jnp.sum(mod_in.reshape(T, I, R, cols), axis=2).reshape(T * I, cols)
    silu_items = silu.reshape(micro, T, rows_own, D).transpose(1, 0, 2, 3).reshape(T * I, D)
    silu_items = lax.dynamic_slice_in_dim(silu_items, s * rs, rs, 1).astype(F32)
    grad_mod = jnp.dot(silu_items.T, mod_items, precision=HIGHEST)
    g_query, g_key, g_value, g_out = unpack(sum_a, 4, cb)
    g_up, g_down = unpack(sum_f, 2, hb)
    return (
        layer_out.reshape(frames.shape),
        grad_input.reshape(frames.shape),
        g_query,
        g_key,
        g_value,
        g_out.T,
        g_up,
        g_down.T,
        grad_mod,
    )


def solution(mesh):
    S, T = mesh.shape["seq"], mesh.shape["tp"]
    rows = P(None, "tp", "seq", None)
    return jax.shard_map(
        partial(per_device, S, T),
        mesh=mesh,
        in_specs=(
            rows,
            P(),
            P(),
            P("seq", "tp"),
            P("seq", "tp"),
            P("seq", "tp"),
            P("tp", "seq"),
            P("seq", "tp"),
            P("tp", "seq"),
            P("seq", "tp"),
            rows,
        ),
        out_specs=(
            rows,
            rows,
            P("seq", "tp"),
            P("seq", "tp"),
            P("seq", "tp"),
            P("tp", "seq"),
            P("seq", "tp"),
            P("tp", "seq"),
            P("seq", "tp"),
        ),
        check_vma=False,
    )
```

```python
from functools import partial
import math

import jax
import jax.numpy as jnp
from jax import lax
from jax.experimental import pallas as pl
from jax.experimental.pallas import tpu as pltpu
from jax.sharding import PartitionSpec as P

D = 1024
HEAD_DIM = 64
EPSILON = 1e-06
NEGATIVE = -1e30
BF = jnp.bfloat16
F32 = jnp.float32
HIGHEST = lax.Precision.HIGHEST
MESH = pl.DeviceIdType.MESH
ANY = pl.BlockSpec(memory_space=pl.ANY)
VMEM = pl.BlockSpec(memory_space=pltpu.VMEM)
LIMIT = 60 * 1024 * 1024


def nn(a, b):
    return lax.dot_general(a, b, (((1,), (0,)), ((), ())), preferred_element_type=F32)


def nt(a, b):
    return lax.dot_general(a, b, (((1,), (1,)), ((), ())), preferred_element_type=F32)


class Place:
    def __init__(self, S, T, I):
        self.S, self.T, self.I = S, T, I
        self.Z, self.R = S // 4, S // I
        self.Q = self.R // 2
        self.s, self.t = lax.axis_index("seq"), lax.axis_index("tp")
        self.z = lax.div(self.s, 4)
        self.x = lax.rem(lax.div(self.s, 2), 2)
        self.c = lax.rem(self.s, 2)
        self.i = lax.div(self.s, self.R)
        self.r = lax.rem(self.s, self.R)
        self.q = lax.div(self.r, 2)

    def at(self, z=None, x=None, c=None, t=None):
        z = self.z if z is None else z
        x = self.x if x is None else x
        c = self.c if c is None else c
        t = self.t if t is None else t
        return ((z * 2 + x) * 2 + c, t)

    def tp(self, k):
        return (self.s, lax.rem(self.t + k, self.T))

    def zs(self, k):
        return lax.rem(self.z + k, self.Z)

    def group(self, k, c=None):
        c = self.c if c is None else c
        return (self.i * self.R + lax.rem(self.q + k, self.Q) * 2 + c, self.t)


class Wires:
    def __init__(self, send, recv, local):
        self.send, self.recv, self.local = send, recv, local
        self.remote_count = self.local_count = 0
        self.sent = []

    def push(self, src, dst, device):
        n = self.remote_count
        self.remote_count += 1
        copy = pltpu.make_async_remote_copy(
            src_ref=src,
            dst_ref=dst,
            send_sem=self.send.at[n],
            recv_sem=self.recv.at[n],
            device_id=device,
            device_id_type=MESH,
        )
        copy.start()
        self.sent.append(copy)
        return copy

    def move(self, src, dst):
        n = self.local_count
        self.local_count += 1
        copy = pltpu.make_async_copy(src, dst, self.local.at[n])
        copy.start()
        return copy

    def close(self):
        for copy in self.sent:
            copy.wait_send()


def landed(copies):
    for copy in copies:
        copy.wait_recv()


def greet_all(place):
    total = place.S * place.T
    me = place.s * place.T + place.t
    barrier = pltpu.get_barrier_semaphore()

    def body(d, carry):
        other = lax.rem(me + d, total)
        pl.semaphore_signal(
            barrier,
            inc=1,
            device_id=(lax.div(other, place.T), lax.rem(other, place.T)),
            device_id_type=MESH,
        )
        return carry

    lax.fori_loop(1, total, body, 0)
    pl.semaphore_wait(barrier, total - 1)


def greet_group(place):
    barrier = pltpu.get_barrier_semaphore()
    pl.semaphore_signal(barrier, inc=1, device_id=place.group(0, 1 - place.c), device_id_type=MESH)
    for k in range(1, place.Q):
        pl.semaphore_signal(barrier, inc=1, device_id=place.group(k), device_id_type=MESH)
    pl.semaphore_wait(barrier, place.Q)


def scatter_rows(place, send, recv, copy_of):
    total = place.S * place.T
    me = place.s * place.T + place.t

    def copy(d):
        other = lax.rem(me + d, total)
        s, t = lax.div(other, place.T), lax.rem(other, place.T)
        src, dst = copy_of(s, t)
        return pltpu.make_async_remote_copy(
            src_ref=src,
            dst_ref=dst,
            send_sem=send.at[d],
            recv_sem=recv.at[d],
            device_id=(s, t),
            device_id_type=MESH,
        )

    def start(d, carry):
        copy(d).start()
        return carry

    def wait(d, carry):
        copy(d).wait()
        return carry

    lax.fori_loop(1, total, start, 0)
    return lambda: lax.fori_loop(1, total, wait, 0)


class Gather:
    def __init__(self, place, wires, src, dst):
        self.p, self.w, self.src, self.dst = place, wires, src, dst
        half = src.shape[0] // 2
        self.upper, self.lower = pl.ds(0, half), pl.ds(half, half)

    def phase0(self):
        p, w, dst = self.p, self.w, self.dst
        own = dst.at[0, p.z, p.x, p.c]
        self.own = w.move(self.src, own)
        self.along = [w.push(self.src, own, p.at(z=p.zs(k))) for k in range(1, p.Z)]

    def phase1(self):
        p, w, dst = self.p, self.w, self.dst
        self.own.wait()
        landed(self.along)
        line = dst.at[0, :, p.x, p.c]
        self.sides = [
            w.push(
                dst.at[0, :, p.x, p.c, self.upper],
                dst.at[0, :, p.x, p.c, self.upper],
                p.at(x=1 - p.x),
            )
        ]
        for k in range(1, p.T):
            self.sides.append(
                w.push(
                    dst.at[0, :, p.x, p.c, self.lower],
                    dst.at[p.T - k, :, p.x, p.c, self.lower],
                    p.tp(k),
                )
            )
        self.cores = [w.push(line, line, p.at(c=1 - p.c))]

    def phase2(self):
        p, w, dst = self.p, self.w, self.dst
        landed(self.sides)
        self.last = []
        for k in range(1, p.T):
            self.last.append(
                w.push(
                    dst.at[0, :, :, p.c, self.upper],
                    dst.at[p.T - k, :, :, p.c, self.upper],
                    p.tp(k),
                )
            )
        part = dst.at[:, :, p.x, p.c, self.lower]
        self.last.append(w.push(part, part, p.at(x=1 - p.x)))
        part = dst.at[0, :, 1 - p.x, p.c, self.upper]
        self.cores.append(w.push(part, part, p.at(c=1 - p.c)))
        part = dst.at[pl.ds(1, p.T - 1), :, p.x, p.c, self.lower]
        self.cores.append(w.push(part, part, p.at(c=1 - p.c)))

    def phase3(self):
        p, w, dst = self.p, self.w, self.dst
        landed(self.last)
        part = dst.at[pl.ds(1, p.T - 1), :, :, p.c, self.upper]
        self.cores.append(w.push(part, part, p.at(c=1 - p.c)))
        part = dst.at[:, :, 1 - p.x, p.c, self.lower]
        self.cores.append(w.push(part, part, p.at(c=1 - p.c)))

    def phase4(self):
        landed(self.cores)


class Reduce:
    def __init__(self, place, wires, src, out, own, core, y_up, x_low, x_up, y_low, z_in):
        self.p, self.w, self.src, self.out = place, wires, src, out
        self.own, self.core, self.y_up, self.x_low = own, core, y_up, x_low
        self.x_up, self.y_low, self.z_in = x_up, y_low, z_in
        half = own.shape[3] // 2
        self.half = half
        self.upper, self.lower = pl.ds(0, half), pl.ds(half, half)

    @staticmethod
    def scratch(T, Z, rs, C):
        half = rs // 2
        return [
            pltpu.VMEM((T, Z, 2, rs, C), BF),
            pltpu.VMEM((T, Z, 2, rs, C), BF),
            pltpu.VMEM((T - 1, Z, 2, half, C), BF),
            pltpu.VMEM((T, Z, half, C), BF),
            pltpu.VMEM((Z, half, C), BF),
            pltpu.VMEM((T - 1, Z, half, C), BF),
            pltpu.VMEM((Z - 1, rs, C), BF),
        ]

    def phase0(self):
        p, w, src = self.p, self.w, self.src
        self.mine = w.move(src.at[:, :, :, p.c], self.own)
        self.pair = [w.push(src.at[:, :, :, 1 - p.c], self.core, p.at(c=1 - p.c))]

    def phase1(self):
        p, w, own = self.p, self.w, self.own
        self.mine.wait()
        landed(self.pair)

        def add(n, carry):
            k, z = lax.div(n, p.Z), lax.rem(n, p.Z)
            for x in range(2):
                own[k, z, x] = own[k, z, x] + self.core[k, z, x]
            return carry

        lax.fori_loop(0, p.T * p.Z, add, 0)
        self.sides = [
            w.push(own.at[k, :, :, self.upper], self.y_up.at[k - 1], p.tp(k))
            for k in range(1, p.T)
        ]
        self.sides.append(w.push(own.at[:, :, 1 - p.x, self.lower], self.x_low, p.at(x=1 - p.x)))

    def phase2(self):
        p, w, own = self.p, self.w, self.own
        landed(self.sides)

        def add(z, carry):
            for x in range(2):
                total = own[0, z, x, self.upper].astype(F32)
                for k in range(1, p.T):
                    total = total + self.y_up[k - 1, z, x].astype(F32)
                own[0, z, x, self.upper] = total.astype(BF)
            for k in range(p.T):
                own[k, z, p.x, self.lower] = own[k, z, p.x, self.lower] + self.x_low[k, z]
            return carry

        lax.fori_loop(0, p.Z, add, 0)
        self.last = [w.push(own.at[0, :, 1 - p.x, self.upper], self.x_up, p.at(x=1 - p.x))]
        for k in range(1, p.T):
            self.last.append(
                w.push(own.at[k, :, p.x, self.lower], self.y_low.at[k - 1], p.tp(k))
            )

    def phase3(self):
        p, w, own = self.p, self.w, self.own
        landed(self.last)

        def add(z, carry):
            own[0, z, p.x, self.upper] = own[0, z, p.x, self.upper] + self.x_up[z]
            total = own[0, z, p.x, self.lower].astype(F32)
            for k in range(1, p.T):
                total = total + self.y_low[k - 1, z].astype(F32)
            own[0, z, p.x, self.lower] = total.astype(BF)
            return carry

        lax.fori_loop(0, p.Z, add, 0)
        self.along = [
            w.push(own.at[0, p.zs(k), p.x], self.z_in.at[k - 1], p.at(z=p.zs(k)))
            for k in range(1, p.Z)
        ]

    def phase4(self):
        p = self.p
        landed(self.along)
        total = self.own[0, p.z, p.x].astype(F32)
        for k in range(1, p.Z):
            total = total + self.z_in[k - 1].astype(F32)
        self.out[...] = total


def swap_items(place, wires, src, dst):
    p = place
    own = wires.move(src.at[p.i], dst.at[p.i])
    copies = []
    for k in range(1, p.I):
        other = lax.rem(p.i + k, p.I)
        copies.append(wires.push(src.at[other], dst.at[p.i], (other * p.R + p.r, p.t)))
    return own, copies


def unshare_kernel(S, T, I, parts, out, near, far, pair, send, recv, local):
    p = Place(S, T, I)
    wires = Wires(send, recv, local)
    greet_group(p)
    core = wires.push(parts.at[:, 1], near, p.group(0, 1 - p.c))
    core.wait_recv()
    across = []
    for k in range(1, p.Q):
        pair[k - 1] = parts[k, 0] + near[k]
        across.append(wires.push(pair.at[k - 1], far.at[k - 1], p.group(k)))
    total = parts[0, 0].astype(F32) + near[0].astype(F32)
    for k in range(1, p.Q):
        across[k - 1].wait_recv()
        total = total + far[k - 1].astype(F32)
    out[...] = total
    wires.close()


def unshare_call(S, T, I, parts):
    Q = S // I // 2
    block = parts.shape[2:]
    return pl.pallas_call(
        partial(unshare_kernel, S, T, I),
        out_shape=jax.ShapeDtypeStruct(block, F32),
        in_specs=[VMEM],
        out_specs=VMEM,
        scratch_shapes=[
            pltpu.VMEM((Q,) + block, BF),
            pltpu.VMEM((Q - 1,) + block, BF),
            pltpu.VMEM((Q - 1,) + block, BF),
            pltpu.SemaphoreType.DMA((Q,)),
            pltpu.SemaphoreType.DMA((Q,)),
            pltpu.SemaphoreType.DMA((1,)),
        ],
        compiler_params=pltpu.CompilerParams(
            collective_id=2, has_side_effects=True, vmem_limit_bytes=LIMIT
        ),
        name="sum_rows",
    )(parts)


def last_kernel(S, T, I, nq, nh, *refs):
    (layer, grads, rows, grad_a, grad_f,
     layer_out, grads_out, rows_out, sum_a, sum_f) = refs[:10]
    scratch = [refs[10 + 7 * n : 17 + 7 * n] for n in range(nq + nh)]
    send, recv, local, row_send, row_recv = refs[10 + 7 * (nq + nh) :]
    p = Place(S, T, I)
    wires = Wires(send, recv, local)
    greet_all(p)
    chunks = [Reduce(p, wires, grad_f.at[j], sum_f.at[j], *scratch[j]) for j in range(nh)]
    chunks += [Reduce(p, wires, grad_a.at[j], sum_a.at[j], *scratch[nh + j]) for j in range(nq)]
    ticker = Ticker(chunks)
    ticker.until(0)
    grads_own, grads_in = swap_items(p, wires, grads, grads_out)
    rows_done = scatter_rows(
        p, row_send, row_recv, lambda s, t: (rows.at[t], rows_out.at[p.t, p.s])
    )
    rows_own = wires.move(rows.at[p.t], rows_out.at[p.t, p.s])
    ticker.until(1)
    layer_own, layer_in = swap_items(p, wires, layer, layer_out)
    for tick in range(2, len(chunks) + 3):
        ticker.until(tick)
    for chunk in chunks:
        chunk.phase4()
    for own in (grads_own, layer_own, rows_own):
        own.wait()
    landed(grads_in)
    landed(layer_in)
    rows_done()
    wires.close()


def last_call(S, T, I, layer, grads, rows, grad_a, grad_f):
    Z = S // 4
    (nq, rs, ca), (nh, cf) = (grad_a.shape[i] for i in (0, 5, 6)), (grad_f.shape[i] for i in (0, 6))
    remote = 2 * (I - 1) + (nq + nh) * (Z + 2 * T + 2)
    scratch = []
    for n in range(nh):
        scratch += Reduce.scratch(T, Z, rs, cf)
    for n in range(nq):
        scratch += Reduce.scratch(T, Z, rs, ca)
    return pl.pallas_call(
        partial(last_kernel, S, T, I, nq, nh),
        out_shape=(
            jax.ShapeDtypeStruct(layer.shape, BF),
            jax.ShapeDtypeStruct(grads.shape, BF),
            jax.ShapeDtypeStruct((T, S) + rows.shape[1:], F32),
            jax.ShapeDtypeStruct((nq, rs, ca), F32),
            jax.ShapeDtypeStruct((nh, rs, cf), F32),
        ),
        in_specs=[ANY] * 5,
        out_specs=(ANY, ANY, ANY, VMEM, VMEM),
        scratch_shapes=scratch
        + [
            pltpu.SemaphoreType.DMA((remote,)),
            pltpu.SemaphoreType.DMA((remote,)),
            pltpu.SemaphoreType.DMA((3 + nq + nh,)),
            pltpu.SemaphoreType.DMA((S * T,)),
            pltpu.SemaphoreType.DMA((S * T,)),
        ],
        compiler_params=pltpu.CompilerParams(
            collective_id=3, has_side_effects=True, vmem_limit_bytes=LIMIT
        ),
        name="collect_outputs",
    )(layer, grads, rows, grad_a, grad_f)


def swap_pairs(v):
    lane = lax.broadcasted_iota(jnp.int32, v.shape, 1)
    return jnp.where(lax.rem(lane, 2) == 0, pltpu.roll(v, 127, 1), pltpu.roll(v, 1, 1))


def head_split(v):
    lane = lax.broadcasted_iota(jnp.int32, v.shape, 1)
    zero = jnp.zeros_like(v)
    return jnp.where(lane < HEAD_DIM, v, zero), jnp.where(lane < HEAD_DIM, zero, v)


def first_lane(rows):
    lane = lax.broadcasted_iota(jnp.int32, (rows, 128), 1)
    return jnp.where(lane == 0, 1.0, 0.0).astype(BF)


def attend_block(rows, cb, xm, weight, cos_ref, sin_ref, mask_ref, q_ref, k_ref, v_ref, att_ref, lse_ref):
    q_lin = nn(xm[0:rows, :], weight(0))
    k_lin = nn(xm, weight(1))
    v_ref[...] = nn(xm, weight(2)).astype(BF)
    ones = first_lane(rows)
    factor = HEAD_DIM**-0.5
    for p in range(cb // 128):
        lanes = slice(p * 128, p * 128 + 128)
        q2, k2 = q_lin[:, lanes], k_lin[:, lanes]
        q2 = (q2 * cos_ref[0:rows, :] + swap_pairs(q2) * sin_ref[0:rows, :]).astype(BF)
        q2 = q2 * jnp.asarray(factor, BF)
        k2 = (k2 * cos_ref[...] + swap_pairs(k2) * sin_ref[...]).astype(BF)
        q_ref[:, lanes] = q2
        k_ref[:, lanes] = k2
        k_long = jnp.concatenate([k2, mask_ref[...]], axis=1)
        v_turned = v_ref[:, lanes].T
        outs = []
        for h, q1 in enumerate(head_split(q2)):
            scores = nt(k_long, jnp.concatenate([q1, ones], axis=1))
            highest = jnp.max(scores, axis=0, keepdims=True)
            unnormed = jnp.exp(scores - highest)
            total = jnp.sum(unnormed, axis=0, keepdims=True)
            probs = (unnormed * (1.0 / total)).astype(BF)
            lse_ref[pl.ds(2 * p + h, 1), :] = highest + jnp.log(total)
            outs.append(nn(v_turned[h * HEAD_DIM : (h + 1) * HEAD_DIM], probs))
        att_ref[:, lanes] = jnp.concatenate(outs, axis=0).T.astype(BF)
    return nt(att_ref[...], weight(3))


def ticks_of(chunks):
    ticks = []
    for tick in range(len(chunks) + 3):
        ticks.append(
            [
                getattr(chunk, f"phase{tick - m}")
                for m, chunk in enumerate(chunks)
                if 0 <= tick - m < 4
            ]
        )
    return ticks


class Ticker:
    def __init__(self, chunks):
        self.ticks, self.done = ticks_of(chunks), 0

    def until(self, tick):
        while self.done <= min(tick, len(self.ticks) - 1):
            for phase in self.ticks[self.done]:
                phase()
            self.done += 1


def front_kernel(
    S, T, I, cb, hb,
    frames, cotangent, parts, w_a, w_f, cos_ref, sin_ref, mask_ref, live_ref,
    all_a, frames_in, xm_ref, q_ref, k_ref, v_ref, att_ref, lse_ref,
    mod_ref, layer_ref, grad_f, dmid_ref, dbranch_ref, dmod_ref,
    a_ref, f_ref, cot_in, parts_in, branch_ref, mid_ref, normed_ref,
    mf_ref, mf_turned, db_ref, db_turned, out_sum, dmf_sum, stage,
    send, recv, local, row_send, row_recv, out_sem,
):
    p = Place(S, T, I)
    wires = Wires(send, recv, local)
    nq, nh = a_ref.shape[0], f_ref.shape[0]
    fl = frames.shape[1]
    rows, L = I * fl, I * fl * p.R
    greet_all(p)
    chunks_a = [Gather(p, wires, w_a.at[j], a_ref.at[j]) for j in range(nq)]
    chunks_f = [Gather(p, wires, w_f.at[j], f_ref.at[j]) for j in range(nh)]
    chunks = chunks_a + chunks_f
    ticker = Ticker(chunks)
    ticker.until(0)
    frames_own, frames_got = swap_items(p, wires, frames, frames_in)
    rows_done = scatter_rows(
        p, row_send, row_recv,
        lambda s, t: (parts.at[t, lax.div(s, p.R)], parts_in.at[p.t, p.s]),
    )
    parts_own = wires.move(parts.at[p.t, p.i], parts_in.at[p.t, p.s])
    ticker.until(1)

    parts_own.wait()
    rows_done()
    high = parts_in.shape[2]
    mod_ref[...] = jnp.zeros_like(mod_ref)
    for t in range(T):
        total = jnp.sum(parts_in[t], axis=0).astype(BF).astype(F32)
        for n in range(high):
            row, col = divmod((t * high + n) * 128, D)
            mod_ref[row : row + 1, col : col + 128] = total[n : n + 1]
    frames_own.wait()
    landed(frames_got)
    frame_rows = frames_in[...].reshape(rows, D).astype(F32)
    normed, _ = layer_stats(frame_rows)
    low = normed.astype(BF).astype(F32)
    xm_ref[0, 0] = (low * (1.0 + mod_ref[1:2, :]) + mod_ref[0:1, :]).astype(BF)
    sibling = p.group(0, 1 - p.c)
    across = [wires.push(xm_ref.at[0, 0], xm_ref.at[p.Q - k, 0], p.group(k)) for k in range(1, p.Q)]
    cores = [wires.push(xm_ref.at[0, 0], xm_ref.at[0, 1], sibling)]
    ticker.until(2)
    for k in range(1, p.Q):
        across[k - 1].wait_recv()
        cores.append(wires.push(xm_ref.at[p.Q - k, 0], xm_ref.at[p.Q - k, 1], sibling))
    ticker.until(3)
    cot_own, cot_got = swap_items(p, wires, cotangent, cot_in)
    landed(cores)

    xm = xm_ref[...].reshape(L, D)
    copies = []
    for j in range(nq):
        ticker.until(j + 3)
        chunks_a[j].phase4()
        copies.append(wires.move(a_ref.at[j], all_a.at[j]))
        for t in range(T):
            n = j * T + t
            part = attend_block(
                rows, cb, xm,
                lambda b: a_ref[j, t, :, :, :, :, b * cb : (b + 1) * cb].reshape(D, cb),
                cos_ref, sin_ref, mask_ref,
                q_ref.at[n], k_ref.at[n], v_ref.at[n], att_ref.at[n], lse_ref.at[n],
            )
            if n == 0:
                branch_ref[...] = part
            else:
                branch_ref[...] += part
            if t == 0:
                ticker.until(j + 4)

    gate_attn, shift_ff = mod_ref[2:3, :], mod_ref[3:4, :]
    scale_ff, gate_ff = mod_ref[4:5, :], mod_ref[5:6, :]
    middle = (
        frames_in[...].reshape(rows, D).astype(F32)
        + gate_attn * live_ref[...] * branch_ref[...]
    )
    mid_ref[...] = middle
    normed, _ = layer_stats(middle)
    low = normed.astype(BF)
    normed_ref[...] = low
    modulated = (low.astype(F32) * (1.0 + scale_ff) + shift_ff).astype(BF)
    mf_ref[...] = modulated
    mf_turned[...] = modulated.T
    cot_own.wait()
    landed(cot_got)
    d_branch = (cot_in[...].reshape(rows, D).astype(F32) * gate_ff).astype(BF)
    db_ref[...] = d_branch
    db_turned[...] = d_branch.T

    pending = [None, None]
    for j in range(nh):
        ticker.until(nq + j + 3)
        chunks_f[j].phase4()
        for t in range(T):
            n = j * T + t
            w_up = f_ref[j, t, :, :, :, :, 0:hb].reshape(D, hb)
            w_down = f_ref[j, t, :, :, :, :, hb : 2 * hb].reshape(D, hb)
            upper = nn(mf_ref[...], w_up)
            square = upper * upper
            slope = 0.7978845608
            tanh = jnp.tanh(slope * (upper + 0.044715 * upper * square))
            half = 0.5 * (1.0 + tanh)
            active = (upper * half).astype(BF)
            bend = half + 0.5 * upper * (1.0 - tanh * tanh) * (
                slope * (1.0 + 3 * 0.044715 * square)
            )
            d_upper = (nn(db_ref[...], w_down) * bend).astype(BF)
            if n == 0:
                out_sum[...] = nt(active, w_down)
                dmf_sum[...] = nt(d_upper, w_up)
            else:
                out_sum[...] += nt(active, w_down)
                dmf_sum[...] += nt(d_upper, w_up)
            slot = n % 2
            if pending[slot] is not None:
                pending[slot].wait()
            stage[slot, :, 0:hb] = nn(mf_turned[...], d_upper).astype(BF)
            stage[slot, :, hb : 2 * hb] = nn(db_turned[...], active).astype(BF)
            pending[slot] = pltpu.make_async_copy(stage.at[slot], grad_f.at[j, t], out_sem.at[slot])
            pending[slot].start()
            if t == 0:
                ticker.until(nq + j + 4)

    middle, branch_f = mid_ref[...], out_sum[...]
    layer_ref[...] = (middle + gate_ff * branch_f).astype(BF).reshape(layer_ref.shape)
    cot = cot_in[...].reshape(rows, D).astype(F32)
    normed, inverse = layer_stats(middle)
    dmf = dmf_sum[...]
    d_mid = cot + layer_back(normed, inverse, dmf * (1.0 + scale_ff))
    dmid_ref[...] = d_mid
    alive = d_mid * live_ref[...]
    dbranch_ref[...] = (alive * gate_attn).astype(BF)
    dmod_ref[...] = jnp.zeros_like(dmod_ref)
    dmod_ref[2:3, :] = jnp.sum(alive * branch_ref[...], axis=0, keepdims=True)
    dmod_ref[3:4, :] = jnp.sum(dmf, axis=0, keepdims=True)
    dmod_ref[4:5, :] = jnp.sum(dmf * normed_ref[...].astype(F32), axis=0, keepdims=True)
    dmod_ref[5:6, :] = jnp.sum(cot * branch_f, axis=0, keepdims=True)
    for copy in copies + [c for c in pending if c is not None]:
        copy.wait()
    wires.close()


def front_call(S, T, I, cb, hb, frames, cotangent, parts, w_a, w_f, cosine, sine, mask, live):
    nq, rs, wide_a = w_a.shape
    nh, _, wide_f = w_f.shape
    fl = frames.shape[1]
    rows, Z, R = I * fl, S // 4, S // I
    Q, L, steps = R // 2, rows * R, nq * T
    remote = 2 * (I - 1) + (nq + nh) * (Z + 2 * T + 4) + 2 * Q
    shape = jax.ShapeDtypeStruct
    return pl.pallas_call(
        partial(front_kernel, S, T, I, cb, hb),
        out_shape=(
            shape((nq, T, Z, 2, 2, rs, wide_a), BF),
            shape(frames.shape, BF),
            shape((Q, 2, rows, D), BF),
            shape((steps, rows, cb), BF),
            shape((steps, L, cb), BF),
            shape((steps, L, cb), BF),
            shape((steps, rows, cb), BF),
            shape((steps, 8, rows), F32),
            shape((8, D), F32),
            shape(frames.shape, BF),
            shape((nh, T, D, wide_f), BF),
            shape((rows, D), F32),
            shape((rows, D), BF),
            shape((8, D), F32),
        ),
        in_specs=[ANY] * 5 + [VMEM] * 4,
        out_specs=(ANY,) + (VMEM,) * 9 + (ANY,) + (VMEM,) * 3,
        scratch_shapes=[
            pltpu.VMEM((nq, T, Z, 2, 2, rs, wide_a), BF),
            pltpu.VMEM((nh, T, Z, 2, 2, rs, wide_f), BF),
            pltpu.VMEM(frames.shape, BF),
            pltpu.VMEM((T, S) + parts.shape[2:], F32),
            pltpu.VMEM((rows, D), F32),
            pltpu.VMEM((rows, D), F32),
            pltpu.VMEM((rows, D), BF),
            pltpu.VMEM((rows, D), BF),
            pltpu.VMEM((D, rows), BF),
            pltpu.VMEM((rows, D), BF),
            pltpu.VMEM((D, rows), BF),
            pltpu.VMEM((rows, D), F32),
            pltpu.VMEM((rows, D), F32),
            pltpu.VMEM((2, D, wide_f), BF),
            pltpu.SemaphoreType.DMA((remote,)),
            pltpu.SemaphoreType.DMA((remote,)),
            pltpu.SemaphoreType.DMA((3 + 2 * nq + nh,)),
            pltpu.SemaphoreType.DMA((S * T,)),
            pltpu.SemaphoreType.DMA((S * T,)),
            pltpu.SemaphoreType.DMA((2,)),
        ],
        compiler_params=pltpu.CompilerParams(
            collective_id=0, has_side_effects=True, vmem_limit_bytes=LIMIT
        ),
        name="forward",
    )(frames, cotangent, parts, w_a, w_f, cosine, sine, mask, live)


def attend_back_kernel(
    rows, cb, db_ref, xm_ref, w_ref, cos_ref, sin_ref, mask_ref,
    q_ref, k_ref, v_ref, att_ref, lse_ref,
    grad_ref, dx_ref, xm_turned, db_turned, dx_sum,
):
    step = pl.program_id(0)

    @pl.when(step == 0)
    def _():
        xm_turned[...] = xm_ref[...].T
        db_turned[...] = db_ref[...].T
        dx_sum[...] = jnp.zeros_like(dx_sum)

    d_att = nn(db_ref[...], w_ref[0, 0, :, 3 * cb : 4 * cb]).astype(BF)
    grad_ref[0, 0, :, 3 * cb : 4 * cb] = nn(db_turned[...], att_ref[0]).astype(BF)
    ones = first_lane(rows)
    factor = HEAD_DIM**-0.5
    dqs, dks, dvs = [], [], []
    for p in range(cb // 128):
        lanes = slice(p * 128, p * 128 + 128)
        q2, k2, v2 = q_ref[0, :, lanes], k_ref[0, :, lanes], v_ref[0, :, lanes]
        k_long = jnp.concatenate([k2, mask_ref[...]], axis=1)
        k_turned = k2.T
        dq_parts, ds_all, p_all = [], [], []
        q_heads, d_heads = head_split(q2), head_split(d_att[:, lanes])
        for h in range(2):
            scores = nt(k_long, jnp.concatenate([q_heads[h], ones], axis=1))
            probs = jnp.exp(scores - lse_ref[0, pl.ds(2 * p + h, 1), :])
            d_probs = nt(v2, d_heads[h])
            row_dot = jnp.sum(probs * d_probs, axis=0, keepdims=True)
            d_scores = (probs * (d_probs - row_dot)).astype(BF)
            dq_parts.append(nn(k_turned[h * HEAD_DIM : (h + 1) * HEAD_DIM], d_scores))
            ds_all.append(d_scores)
            p_all.append(probs.astype(BF))
        dk2 = nn(jnp.concatenate(ds_all, axis=1), jnp.concatenate(q_heads, axis=0))
        dv2 = nn(jnp.concatenate(p_all, axis=1), jnp.concatenate(d_heads, axis=0))
        dq2 = jnp.concatenate(dq_parts, axis=0).T * factor
        dqs.append(
            (dq2 * cos_ref[0:rows, :] - swap_pairs(dq2) * sin_ref[0:rows, :]).astype(BF)
        )
        dks.append((dk2 * cos_ref[...] - swap_pairs(dk2) * sin_ref[...]).astype(BF))
        dvs.append(dv2.astype(BF))
    dq, dk, dv = (jnp.concatenate(v, axis=1) for v in (dqs, dks, dvs))
    grad_ref[0, 0, :, 0:cb] = nn(xm_turned[:, 0:rows], dq).astype(BF)
    grad_ref[0, 0, :, cb : 2 * cb] = nn(xm_turned[...], dk).astype(BF)
    grad_ref[0, 0, :, 2 * cb : 3 * cb] = nn(xm_turned[...], dv).astype(BF)
    dx_sum[...] += nt(
        jnp.concatenate([dk, dv], axis=1), w_ref[0, 0, :, cb : 3 * cb]
    )
    dx_sum[0:rows, :] += nt(dq, w_ref[0, 0, :, 0:cb])

    @pl.when(step == pl.num_programs(0) - 1)
    def _():
        dx_ref[...] = dx_sum[...].astype(BF)


def attend_back_call(rows, cb, d_branch, xm, w_all, cosine, sine, mask, q, k, v, att, lse):
    nq, T = w_all.shape[:2]
    L = xm.shape[0]
    fixed = lambda n: (0, 0)
    column = lambda n: (n, 0, 0)
    weight = pl.BlockSpec((1, 1, D, 4 * cb), lambda n: (n // T, n % T, 0, 0))
    return pl.pallas_call(
        partial(attend_back_kernel, rows, cb),
        grid=(nq * T,),
        out_shape=(
            jax.ShapeDtypeStruct(w_all.shape, BF),
            jax.ShapeDtypeStruct((L, D), BF),
        ),
        in_specs=[
            pl.BlockSpec((rows, D), fixed),
            pl.BlockSpec((L, D), fixed),
            weight,
            pl.BlockSpec((L, 128), fixed),
            pl.BlockSpec((L, 128), fixed),
            pl.BlockSpec((L, 128), fixed),
            pl.BlockSpec((1, rows, cb), column),
            pl.BlockSpec((1, L, cb), column),
            pl.BlockSpec((1, L, cb), column),
            pl.BlockSpec((1, rows, cb), column),
            pl.BlockSpec((1, 8, rows), column),
        ],
        out_specs=(weight, pl.BlockSpec((L, D), fixed)),
        scratch_shapes=[
            pltpu.VMEM((D, L), BF),
            pltpu.VMEM((D, rows), BF),
            pltpu.VMEM((L, D), F32),
        ],
        compiler_params=pltpu.CompilerParams(vmem_limit_bytes=LIMIT),
        name="attend_back",
    )(d_branch, xm, w_all, cosine, sine, mask, q, k, v, att, lse)


def layer_stats(values):
    center = values - jnp.mean(values, axis=-1, keepdims=True)
    inverse = lax.rsqrt(jnp.mean(center * center, axis=-1, keepdims=True) + EPSILON)
    return center * inverse, inverse


def layer_back(normed, inverse, incoming):
    return inverse * (
        incoming
        - jnp.mean(incoming, axis=-1, keepdims=True)
        - normed * jnp.mean(incoming * normed, axis=-1, keepdims=True)
    )


def pack(blocks, width):
    rows = blocks[0].shape[0]
    cut = [b.reshape(rows, -1, width) for b in blocks]
    return jnp.concatenate(cut, axis=2).transpose(1, 0, 2)


def unpack(packed, count):
    steps, rows, wide = packed.shape
    cut = packed.reshape(steps, rows, count, wide // count)
    return [cut[:, :, n].transpose(1, 0, 2).reshape(rows, -1) for n in range(count)]


def per_device(
    S, T, frames, time_embed, lengths, w_query, w_key, w_value, w_out, w_up, w_down, w_mod, out_grad
):
    micro, rows_own, fl, _ = frames.shape
    batch = lengths.shape[1]
    I = micro * rows_own
    R = S // I
    Q = R // 2
    rs = w_query.shape[0]
    rows = I * fl
    L = R * rows
    cb = min(256, w_query.shape[1])
    hb = min(512, w_up.shape[1])
    s, t = lax.axis_index("seq"), lax.axis_index("tp")
    item = s // R
    place_r = s % R

    w_a = pack([w_query, w_key, w_value, w_out.T], cb)
    w_f = pack([w_up, w_down.T], hb)
    silu = jax.nn.silu(time_embed).astype(BF).reshape(micro * batch, D)
    silu_own = lax.dynamic_slice_in_dim(silu, s * rs, rs, 1)
    cols = w_mod.shape[1]
    parts = jnp.dot(silu_own, w_mod, preferred_element_type=F32)
    parts = parts.reshape(micro, T, rows_own, cols // 128, 128)
    parts = parts.transpose(1, 0, 2, 3, 4).reshape(T, I, cols // 128, 128)
    g = jnp.arange(R)
    r_of = (place_r // 2 + g // 2) % Q * 2 + (place_r % 2 + g % 2) % 2
    pos = fl * (jnp.arange(I)[None, :] * R + r_of[:, None])
    pos = (pos[:, :, None] + jnp.arange(fl)).reshape(L)
    length = lengths[item // rows_own, t * rows_own + item % rows_own]
    alive = pos < length
    live = alive[:rows].astype(F32)[:, None]
    lane = jnp.arange(128)
    mask = jnp.where((lane[None, :] == 0) & ~alive[:, None], NEGATIVE, 0.0).astype(BF)
    column = (lane % HEAD_DIM // 2).astype(F32)
    inverse = jnp.exp(column * (-2.0 * math.log(10000.0) / HEAD_DIM))
    angles = pos.astype(F32)[:, None] * inverse[None, :]
    cosine = jnp.cos(angles)
    sine = jnp.sin(angles) * jnp.where(lane % 2 == 0, -1.0, 1.0)

    (
        all_a, frames_in, xm, q, k, v, att, lse, mod, layer, grad_f, d_mid, d_branch, d_rows
    ) = front_call(
        S, T, I, cb, hb, frames.reshape(I, fl, D), out_grad.reshape(I, fl, D), parts,
        w_a, w_f, cosine, sine, mask, live,
    )
    grad_a, dx = attend_back_call(
        rows, cb, d_branch, xm.reshape(L, D), all_a.reshape(all_a.shape[:2] + (D, 4 * cb)),
        cosine, sine, mask, q, k, v, att, lse,
    )
    d_mod_a = unshare_call(S, T, I, dx.reshape(Q, 2, rows, D))
    normed_a, inverse_a = layer_stats(frames_in.reshape(rows, D).astype(F32))
    normed_low = normed_a.astype(BF).astype(F32)
    grad_in = d_mid + layer_back(normed_a, inverse_a, d_mod_a * (1.0 + mod[1:2]))
    d_modulation = jnp.concatenate(
        [
            jnp.sum(d_mod_a, axis=0, keepdims=True),
            jnp.sum(d_mod_a * normed_low, axis=0, keepdims=True),
            d_rows[2:6],
        ],
        axis=0,
    ).reshape(T, cols // 128, 128)
    shape6 = (T, S // 4, 2, 2, rs)
    layer_out, grad_input, mod_in, sum_a, sum_f = last_call(
        S, T, I, layer, grad_in.astype(BF).reshape(I, fl, D), d_modulation,
        grad_a.reshape(grad_a.shape[:1] + shape6 + (4 * cb,)),
        grad_f.reshape(grad_f.shape[:1] + shape6 + (2 * hb,)),
    )
    mod_items = jnp.sum(mod_in.reshape(T, I, R, cols), axis=2).reshape(T * I, cols)
    silu_items = silu.reshape(micro, T, rows_own, D).transpose(1, 0, 2, 3).reshape(T * I, D)
    silu_items = lax.dynamic_slice_in_dim(silu_items, s * rs, rs, 1).astype(F32)
    grad_mod = jnp.dot(silu_items.T, mod_items, precision=HIGHEST)
    g_query, g_key, g_value, g_out = unpack(sum_a, 4)
    g_up, g_down = unpack(sum_f, 2)
    return (
        layer_out.reshape(frames.shape),
        grad_input.reshape(frames.shape),
        g_query,
        g_key,
        g_value,
        g_out.T,
        g_up,
        g_down.T,
        grad_mod,
    )


def solution(mesh):
    S, T = mesh.shape["seq"], mesh.shape["tp"]
    rows = P(None, "tp", "seq", None)
    return jax.shard_map(
        partial(per_device, S, T),
        mesh=mesh,
        in_specs=(
            rows,
            P(),
            P(),
            P("seq", "tp"),
            P("seq", "tp"),
            P("seq", "tp"),
            P("tp", "seq"),
            P("seq", "tp"),
            P("tp", "seq"),
            P("seq", "tp"),
            rows,
        ),
        out_specs=(
            rows,
            rows,
            P("seq", "tp"),
            P("seq", "tp"),
            P("seq", "tp"),
            P("tp", "seq"),
            P("seq", "tp"),
            P("tp", "seq"),
            P("seq", "tp"),
        ),
        check_vma=False,
    )
```

```python
from functools import partial
import math

import jax
import jax.numpy as jnp
from jax import lax
from jax.experimental import pallas as pl
from jax.experimental.pallas import tpu as pltpu
from jax.sharding import PartitionSpec as P

D = 1024
HEAD_DIM = 64
EPSILON = 1e-06
NEGATIVE = -1e30
BF = jnp.bfloat16
F32 = jnp.float32
HIGHEST = lax.Precision.HIGHEST
MESH = pl.DeviceIdType.MESH
ANY = pl.BlockSpec(memory_space=pl.ANY)
VMEM = pl.BlockSpec(memory_space=pltpu.VMEM)
LIMIT = 62 * 1024 * 1024


def nn(a, b):
    return lax.dot_general(a, b, (((1,), (0,)), ((), ())), preferred_element_type=F32)


def nt(a, b):
    return lax.dot_general(a, b, (((1,), (1,)), ((), ())), preferred_element_type=F32)


class Place:
    def __init__(self, S, T, I):
        self.S, self.T, self.I = S, T, I
        self.Z, self.R = S // 4, S // I
        self.Q = self.R // 2
        self.s, self.t = lax.axis_index("seq"), lax.axis_index("tp")
        self.z = lax.div(self.s, 4)
        self.x = lax.rem(lax.div(self.s, 2), 2)
        self.c = lax.rem(self.s, 2)
        self.i = lax.div(self.s, self.R)
        self.r = lax.rem(self.s, self.R)
        self.q = lax.div(self.r, 2)

    def at(self, z=None, x=None, c=None, t=None):
        z = self.z if z is None else z
        x = self.x if x is None else x
        c = self.c if c is None else c
        t = self.t if t is None else t
        return ((z * 2 + x) * 2 + c, t)

    def tp(self, k):
        return (self.s, lax.rem(self.t + k, self.T))

    def zs(self, k):
        return lax.rem(self.z + k, self.Z)

    def group(self, k, c=None):
        c = self.c if c is None else c
        return (self.i * self.R + lax.rem(self.q + k, self.Q) * 2 + c, self.t)


class Wires:
    def __init__(self, send, recv, local):
        self.send, self.recv, self.local = send, recv, local
        self.remote_count = self.local_count = 0
        self.sent = []

    def push(self, src, dst, device):
        n = self.remote_count
        self.remote_count += 1
        copy = pltpu.make_async_remote_copy(
            src_ref=src,
            dst_ref=dst,
            send_sem=self.send.at[n],
            recv_sem=self.recv.at[n],
            device_id=device,
            device_id_type=MESH,
        )
        copy.start()
        self.sent.append(copy)
        return copy

    def move(self, src, dst):
        n = self.local_count
        self.local_count += 1
        copy = pltpu.make_async_copy(src, dst, self.local.at[n])
        copy.start()
        return copy

    def close(self):
        for copy in self.sent:
            copy.wait_send()


def landed(copies):
    for copy in copies:
        copy.wait_recv()


def greet_all(place):
    total = place.S * place.T
    me = place.s * place.T + place.t
    barrier = pltpu.get_barrier_semaphore()

    def body(d, carry):
        other = lax.rem(me + d, total)
        pl.semaphore_signal(
            barrier,
            inc=1,
            device_id=(lax.div(other, place.T), lax.rem(other, place.T)),
            device_id_type=MESH,
        )
        return carry

    lax.fori_loop(1, total, body, 0)
    pl.semaphore_wait(barrier, total - 1)


def scatter_rows(place, send, recv, copy_of):
    total = place.S * place.T
    me = place.s * place.T + place.t

    def copy(d):
        other = lax.rem(me + d, total)
        s, t = lax.div(other, place.T), lax.rem(other, place.T)
        src, dst = copy_of(s, t)
        return pltpu.make_async_remote_copy(
            src_ref=src,
            dst_ref=dst,
            send_sem=send.at[d],
            recv_sem=recv.at[d],
            device_id=(s, t),
            device_id_type=MESH,
        )

    def start(d, carry):
        copy(d).start()
        return carry

    def wait(d, carry):
        copy(d).wait()
        return carry

    lax.fori_loop(1, total, start, 0)
    return lambda: lax.fori_loop(1, total, wait, 0)


class Gather:
    def __init__(self, place, wires, src, dst):
        self.p, self.w, self.src, self.dst = place, wires, src, dst
        half = src.shape[0] // 2
        self.upper, self.lower = pl.ds(0, half), pl.ds(half, half)

    def phase0(self):
        p, w, dst = self.p, self.w, self.dst
        own = dst.at[0, p.z, p.x, p.c]
        self.own = w.move(self.src, own)
        self.along = [w.push(self.src, own, p.at(z=p.zs(k))) for k in range(1, p.Z)]

    def phase1(self):
        p, w, dst = self.p, self.w, self.dst
        self.own.wait()
        landed(self.along)
        line = dst.at[0, :, p.x, p.c]
        self.sides = [
            w.push(
                dst.at[0, :, p.x, p.c, self.upper],
                dst.at[0, :, p.x, p.c, self.upper],
                p.at(x=1 - p.x),
            )
        ]
        for k in range(1, p.T):
            self.sides.append(
                w.push(
                    dst.at[0, :, p.x, p.c, self.lower],
                    dst.at[p.T - k, :, p.x, p.c, self.lower],
                    p.tp(k),
                )
            )
        self.cores = [w.push(line, line, p.at(c=1 - p.c))]

    def phase2(self):
        p, w, dst = self.p, self.w, self.dst
        landed(self.sides)
        self.last = []
        for k in range(1, p.T):
            self.last.append(
                w.push(
                    dst.at[0, :, :, p.c, self.upper],
                    dst.at[p.T - k, :, :, p.c, self.upper],
                    p.tp(k),
                )
            )
        part = dst.at[:, :, p.x, p.c, self.lower]
        self.last.append(w.push(part, part, p.at(x=1 - p.x)))
        part = dst.at[0, :, 1 - p.x, p.c, self.upper]
        self.cores.append(w.push(part, part, p.at(c=1 - p.c)))
        part = dst.at[pl.ds(1, p.T - 1), :, p.x, p.c, self.lower]
        self.cores.append(w.push(part, part, p.at(c=1 - p.c)))

    def phase3(self):
        p, w, dst = self.p, self.w, self.dst
        landed(self.last)
        part = dst.at[pl.ds(1, p.T - 1), :, :, p.c, self.upper]
        self.cores.append(w.push(part, part, p.at(c=1 - p.c)))
        part = dst.at[:, :, 1 - p.x, p.c, self.lower]
        self.cores.append(w.push(part, part, p.at(c=1 - p.c)))

    def phase4(self):
        landed(self.cores)


class Reduce:
    def __init__(self, place, wires, src, out, own, core_at, landing):
        self.p, self.w, self.src, self.out = place, wires, src, out
        self.own, self.core_at = own, core_at
        self.core, self.y_up, self.x_low, self.x_up, self.y_low, self.z_in = landing
        half = own.shape[4] // 2
        self.upper, self.lower = pl.ds(0, half), pl.ds(half, half)

    @staticmethod
    def landing(T, Z, rs, C):
        half = rs // 2
        return [
            pltpu.VMEM((T, Z, 2, rs, C), BF),
            pltpu.VMEM((T - 1, Z, 2, half, C), BF),
            pltpu.VMEM((T, Z, half, C), BF),
            pltpu.VMEM((Z, half, C), BF),
            pltpu.VMEM((T - 1, Z, half, C), BF),
            pltpu.VMEM((Z - 1, rs, C), BF),
        ]

    def phase0(self):
        p, w, src = self.p, self.w, self.src
        self.mine = None
        if self.own is not src:
            self.mine = w.move(src.at[:, :, :, pl.ds(p.c, 1)], self.own)
        self.pair = [w.push(src.at[:, :, :, 1 - p.c], self.core, p.at(c=1 - p.c))]

    def phase1(self):
        p, w, own, c = self.p, self.w, self.own, self.core_at
        if self.mine is not None:
            self.mine.wait()
        landed(self.pair)

        def add(n, carry):
            k, z = lax.div(n, p.Z), lax.rem(n, p.Z)
            for x in range(2):
                own[k, z, x, c] = own[k, z, x, c] + self.core[k, z, x]
            return carry

        lax.fori_loop(0, p.T * p.Z, add, 0)
        self.sides = [
            w.push(own.at[k, :, :, c, self.upper], self.y_up.at[k - 1], p.tp(k))
            for k in range(1, p.T)
        ]
        self.sides.append(
            w.push(own.at[:, :, 1 - p.x, c, self.lower], self.x_low, p.at(x=1 - p.x))
        )

    def phase2(self):
        p, w, own, c = self.p, self.w, self.own, self.core_at
        landed(self.sides)

        def add(z, carry):
            for x in range(2):
                total = own[0, z, x, c, self.upper].astype(F32)
                for k in range(1, p.T):
                    total = total + self.y_up[k - 1, z, x].astype(F32)
                own[0, z, x, c, self.upper] = total.astype(BF)
            for k in range(p.T):
                own[k, z, p.x, c, self.lower] = own[k, z, p.x, c, self.lower] + self.x_low[k, z]
            return carry

        lax.fori_loop(0, p.Z, add, 0)
        self.last = [w.push(own.at[0, :, 1 - p.x, c, self.upper], self.x_up, p.at(x=1 - p.x))]
        for k in range(1, p.T):
            self.last.append(
                w.push(own.at[k, :, p.x, c, self.lower], self.y_low.at[k - 1], p.tp(k))
            )

    def phase3(self):
        p, w, own, c = self.p, self.w, self.own, self.core_at
        landed(self.last)

        def add(z, carry):
            own[0, z, p.x, c, self.upper] = own[0, z, p.x, c, self.upper] + self.x_up[z]
            total = own[0, z, p.x, c, self.lower].astype(F32)
            for k in range(1, p.T):
                total = total + self.y_low[k - 1, z].astype(F32)
            own[0, z, p.x, c, self.lower] = total.astype(BF)
            return carry

        lax.fori_loop(0, p.Z, add, 0)
        self.along = [
            w.push(own.at[0, p.zs(k), p.x, c], self.z_in.at[k - 1], p.at(z=p.zs(k)))
            for k in range(1, p.Z)
        ]

    def phase4(self):
        p = self.p
        landed(self.along)
        total = self.own[0, p.z, p.x, self.core_at].astype(F32)
        for k in range(1, p.Z):
            total = total + self.z_in[k - 1].astype(F32)
        self.out[...] = total


def swap_items(place, wires, src, dst):
    p = place
    block = src if callable(src) else lambda n: src.at[n]
    own = wires.move(block(p.i), dst.at[p.i])
    copies = []
    for k in range(1, p.I):
        other = lax.rem(p.i + k, p.I)
        copies.append(wires.push(block(other), dst.at[p.i], (other * p.R + p.r, p.t)))
    return own, copies


def swap_pairs(v):
    lane = lax.broadcasted_iota(jnp.int32, v.shape, 1)
    return jnp.where(lax.rem(lane, 2) == 0, pltpu.roll(v, 127, 1), pltpu.roll(v, 1, 1))


def head_split(v):
    lane = lax.broadcasted_iota(jnp.int32, v.shape, 1)
    zero = jnp.zeros_like(v)
    return jnp.where(lane < HEAD_DIM, v, zero), jnp.where(lane < HEAD_DIM, zero, v)


def first_lane(rows):
    lane = lax.broadcasted_iota(jnp.int32, (rows, 128), 1)
    return jnp.where(lane == 0, 1.0, 0.0).astype(BF)


def attend_block(rows, cb, xm, weight, cos_ref, sin_ref, mask_ref, q_ref, k_ref, v_ref, att_ref, lse_ref):
    q_lin = nn(xm[0:rows, :], weight(0))
    k_lin = nn(xm, weight(1))
    v_ref[...] = nn(xm, weight(2)).astype(BF)
    ones = first_lane(rows)
    factor = HEAD_DIM**-0.5
    for p in range(cb // 128):
        lanes = slice(p * 128, p * 128 + 128)
        q2, k2 = q_lin[:, lanes], k_lin[:, lanes]
        q2 = (q2 * cos_ref[0:rows, :] + swap_pairs(q2) * sin_ref[0:rows, :]).astype(BF)
        q2 = q2 * jnp.asarray(factor, BF)
        k2 = (k2 * cos_ref[...] + swap_pairs(k2) * sin_ref[...]).astype(BF)
        q_ref[:, lanes] = q2
        k_ref[:, lanes] = k2
        k_long = jnp.concatenate([k2, mask_ref[...]], axis=1)
        v_turned = v_ref[:, lanes].T
        outs = []
        for h, q1 in enumerate(head_split(q2)):
            scores = nt(k_long, jnp.concatenate([q1, ones], axis=1))
            highest = jnp.max(scores, axis=0, keepdims=True)
            unnormed = jnp.exp(scores - highest)
            total = jnp.sum(unnormed, axis=0, keepdims=True)
            probs = (unnormed * (1.0 / total)).astype(BF)
            lse_ref[pl.ds(2 * p + h, 1), :] = highest + jnp.log(total)
            outs.append(nn(v_turned[h * HEAD_DIM : (h + 1) * HEAD_DIM], probs))
        att_ref[:, lanes] = jnp.concatenate(outs, axis=0).T.astype(BF)
    return nt(att_ref[...], weight(3))


def ticks_of(chunks):
    ticks = []
    for tick in range(len(chunks) + 3):
        ticks.append(
            [
                getattr(chunk, f"phase{tick - m}")
                for m, chunk in enumerate(chunks)
                if 0 <= tick - m < 4
            ]
        )
    return ticks


class Ticker:
    def __init__(self, chunks):
        self.ticks, self.done = ticks_of(chunks), 0

    def until(self, tick):
        while self.done <= min(tick, len(self.ticks) - 1):
            for phase in self.ticks[self.done]:
                phase()
            self.done += 1


def front_kernel(
    S, T, I, cb, hb,
    frames, cotangent, parts, w_a, w_f, cos_ref, sin_ref, mask_ref, live_ref,
    all_a, frames_in, xm_ref, q_ref, k_ref, v_ref, att_ref, lse_ref,
    mod_ref, layer_ref, grad_f, dmid_ref, dbranch_ref, dmod_ref,
    a_ref, f_ref, cot_in, parts_in, branch_ref, mid_ref, normed_ref,
    mf_ref, mf_turned, db_ref, db_turned, out_sum, dmf_sum, stage,
    send, recv, local, row_send, row_recv, out_sem,
):
    p = Place(S, T, I)
    wires = Wires(send, recv, local)
    nq, nh = a_ref.shape[0], f_ref.shape[0]
    fl = frames.shape[1]
    rows, L = I * fl, I * fl * p.R
    greet_all(p)
    chunks_a = [Gather(p, wires, w_a.at[j], a_ref.at[j]) for j in range(nq)]
    chunks_f = [Gather(p, wires, w_f.at[j], f_ref.at[j]) for j in range(nh)]
    chunks = chunks_a + chunks_f
    ticker = Ticker(chunks)
    ticker.until(0)
    frames_own, frames_got = swap_items(p, wires, frames, frames_in)
    rows_done = scatter_rows(
        p, row_send, row_recv,
        lambda s, t: (parts.at[t, lax.div(s, p.R)], parts_in.at[p.t, p.s]),
    )
    parts_own = wires.move(parts.at[p.t, p.i], parts_in.at[p.t, p.s])
    ticker.until(1)

    parts_own.wait()
    rows_done()
    high = parts_in.shape[2]
    mod_ref[...] = jnp.zeros_like(mod_ref)
    for t in range(T):
        total = jnp.sum(parts_in[t], axis=0).astype(BF).astype(F32)
        for n in range(high):
            row, col = divmod((t * high + n) * 128, D)
            mod_ref[row : row + 1, col : col + 128] = total[n : n + 1]
    frames_own.wait()
    landed(frames_got)
    frame_rows = frames_in[...].reshape(rows, D).astype(F32)
    normed, _ = layer_stats(frame_rows)
    low = normed.astype(BF).astype(F32)
    xm_ref[0, 0] = (low * (1.0 + mod_ref[1:2, :]) + mod_ref[0:1, :]).astype(BF)
    sibling = p.group(0, 1 - p.c)
    across = [wires.push(xm_ref.at[0, 0], xm_ref.at[p.Q - k, 0], p.group(k)) for k in range(1, p.Q)]
    cores = [wires.push(xm_ref.at[0, 0], xm_ref.at[0, 1], sibling)]
    ticker.until(2)
    for k in range(1, p.Q):
        across[k - 1].wait_recv()
        cores.append(wires.push(xm_ref.at[p.Q - k, 0], xm_ref.at[p.Q - k, 1], sibling))
    ticker.until(3)
    cot_own, cot_got = swap_items(p, wires, cotangent, cot_in)
    landed(cores)

    xm = xm_ref[...].reshape(L, D)
    copies = []
    for j in range(nq):
        ticker.until(j + 3)
        chunks_a[j].phase4()
        copies.append(wires.move(a_ref.at[j], all_a.at[j]))
        for t in range(T):
            n = j * T + t
            part = attend_block(
                rows, cb, xm,
                lambda b: a_ref[j, t, :, :, :, :, b * cb : (b + 1) * cb].reshape(D, cb),
                cos_ref, sin_ref, mask_ref,
                q_ref.at[n], k_ref.at[n], v_ref.at[n], att_ref.at[n], lse_ref.at[n],
            )
            if n == 0:
                branch_ref[...] = part
            else:
                branch_ref[...] += part
            if t == 0:
                ticker.until(j + 4)

    gate_attn, shift_ff = mod_ref[2:3, :], mod_ref[3:4, :]
    scale_ff, gate_ff = mod_ref[4:5, :], mod_ref[5:6, :]
    middle = (
        frames_in[...].reshape(rows, D).astype(F32)
        + gate_attn * live_ref[...] * branch_ref[...]
    )
    mid_ref[...] = middle
    normed, _ = layer_stats(middle)
    low = normed.astype(BF)
    normed_ref[...] = low
    modulated = (low.astype(F32) * (1.0 + scale_ff) + shift_ff).astype(BF)
    mf_ref[...] = modulated
    mf_turned[...] = modulated.T
    cot_own.wait()
    landed(cot_got)
    d_branch = (cot_in[...].reshape(rows, D).astype(F32) * gate_ff).astype(BF)
    db_ref[...] = d_branch
    db_turned[...] = d_branch.T

    pending = [None, None]
    for j in range(nh):
        ticker.until(nq + j + 3)
        chunks_f[j].phase4()
        for t in range(T):
            n = j * T + t
            w_up = f_ref[j, t, :, :, :, :, 0:hb].reshape(D, hb)
            w_down = f_ref[j, t, :, :, :, :, hb : 2 * hb].reshape(D, hb)
            upper = nn(mf_ref[...], w_up)
            square = upper * upper
            slope = 0.7978845608
            tanh = jnp.tanh(slope * (upper + 0.044715 * upper * square))
            half = 0.5 * (1.0 + tanh)
            active = (upper * half).astype(BF)
            bend = half + 0.5 * upper * (1.0 - tanh * tanh) * (
                slope * (1.0 + 3 * 0.044715 * square)
            )
            d_upper = (nn(db_ref[...], w_down) * bend).astype(BF)
            if n == 0:
                out_sum[...] = nt(active, w_down)
                dmf_sum[...] = nt(d_upper, w_up)
            else:
                out_sum[...] += nt(active, w_down)
                dmf_sum[...] += nt(d_upper, w_up)
            slot = n % 2
            if pending[slot] is not None:
                pending[slot].wait()
            stage[slot, :, 0:hb] = nn(mf_turned[...], d_upper).astype(BF)
            stage[slot, :, hb : 2 * hb] = nn(db_turned[...], active).astype(BF)
            pending[slot] = pltpu.make_async_copy(stage.at[slot], grad_f.at[j, t], out_sem.at[slot])
            pending[slot].start()
            if t == 0:
                ticker.until(nq + j + 4)

    middle, branch_f = mid_ref[...], out_sum[...]
    layer_ref[...] = (middle + gate_ff * branch_f).astype(BF).reshape(layer_ref.shape)
    cot = cot_in[...].reshape(rows, D).astype(F32)
    normed, inverse = layer_stats(middle)
    dmf = dmf_sum[...]
    d_mid = cot + layer_back(normed, inverse, dmf * (1.0 + scale_ff))
    dmid_ref[...] = d_mid
    alive = d_mid * live_ref[...]
    dbranch_ref[...] = (alive * gate_attn).astype(BF)
    dmod_ref[...] = jnp.zeros_like(dmod_ref)
    dmod_ref[2:3, :] = jnp.sum(alive * branch_ref[...], axis=0, keepdims=True)
    dmod_ref[3:4, :] = jnp.sum(dmf, axis=0, keepdims=True)
    dmod_ref[4:5, :] = jnp.sum(dmf * normed_ref[...].astype(F32), axis=0, keepdims=True)
    dmod_ref[5:6, :] = jnp.sum(cot * branch_f, axis=0, keepdims=True)
    for copy in copies + [c for c in pending if c is not None]:
        copy.wait()
    wires.close()


def front_call(S, T, I, cb, hb, frames, cotangent, parts, w_a, w_f, cosine, sine, mask, live):
    nq, rs, wide_a = w_a.shape
    nh, _, wide_f = w_f.shape
    fl = frames.shape[1]
    rows, Z, R = I * fl, S // 4, S // I
    Q, L, steps = R // 2, rows * R, nq * T
    remote = 2 * (I - 1) + (nq + nh) * (Z + 2 * T + 4) + 2 * Q
    shape = jax.ShapeDtypeStruct
    return pl.pallas_call(
        partial(front_kernel, S, T, I, cb, hb),
        out_shape=(
            shape((nq, T, Z, 2, 2, rs, wide_a), BF),
            shape(frames.shape, BF),
            shape((Q, 2, rows, D), BF),
            shape((steps, rows, cb), BF),
            shape((steps, L, cb), BF),
            shape((steps, L, cb), BF),
            shape((steps, rows, cb), BF),
            shape((steps, 8, rows), F32),
            shape((8, D), F32),
            shape(frames.shape, BF),
            shape((nh, T, D, wide_f), BF),
            shape((rows, D), F32),
            shape((rows, D), BF),
            shape((8, D), F32),
        ),
        in_specs=[ANY] * 5 + [VMEM] * 4,
        out_specs=(ANY,) + (VMEM,) * 9 + (ANY,) + (VMEM,) * 3,
        scratch_shapes=[
            pltpu.VMEM((nq, T, Z, 2, 2, rs, wide_a), BF),
            pltpu.VMEM((nh, T, Z, 2, 2, rs, wide_f), BF),
            pltpu.VMEM(frames.shape, BF),
            pltpu.VMEM((T, S) + parts.shape[2:], F32),
            pltpu.VMEM((rows, D), F32),
            pltpu.VMEM((rows, D), F32),
            pltpu.VMEM((rows, D), BF),
            pltpu.VMEM((rows, D), BF),
            pltpu.VMEM((D, rows), BF),
            pltpu.VMEM((rows, D), BF),
            pltpu.VMEM((D, rows), BF),
            pltpu.VMEM((rows, D), F32),
            pltpu.VMEM((rows, D), F32),
            pltpu.VMEM((2, D, wide_f), BF),
            pltpu.SemaphoreType.DMA((remote,)),
            pltpu.SemaphoreType.DMA((remote,)),
            pltpu.SemaphoreType.DMA((3 + 2 * nq + nh,)),
            pltpu.SemaphoreType.DMA((S * T,)),
            pltpu.SemaphoreType.DMA((S * T,)),
            pltpu.SemaphoreType.DMA((2,)),
        ],
        compiler_params=pltpu.CompilerParams(
            collective_id=0, has_side_effects=True, vmem_limit_bytes=LIMIT
        ),
        name="forward",
    )(frames, cotangent, parts, w_a, w_f, cosine, sine, mask, live)


def attend_back_block(
    rows, cb, weight, wide, db_ref, xm_turned, db_turned, cos_ref, sin_ref, mask_ref,
    q_ref, k_ref, v_ref, att_ref, lse_ref, store,
):
    d_att = nn(db_ref[...], weight(3)).astype(BF)
    store(3, nn(db_turned[...], att_ref[...]))
    ones = first_lane(rows)
    factor = HEAD_DIM**-0.5
    dqs, dks, dvs = [], [], []
    for p in range(cb // 128):
        lanes = slice(p * 128, p * 128 + 128)
        q2, k2, v2 = q_ref[:, lanes], k_ref[:, lanes], v_ref[:, lanes]
        k_long = jnp.concatenate([k2, mask_ref[...]], axis=1)
        k_turned = k2.T
        dq_parts, ds_all, p_all = [], [], []
        q_heads, d_heads = head_split(q2), head_split(d_att[:, lanes])
        for h in range(2):
            scores = nt(k_long, jnp.concatenate([q_heads[h], ones], axis=1))
            probs = jnp.exp(scores - lse_ref[pl.ds(2 * p + h, 1), :])
            d_probs = nt(v2, d_heads[h])
            row_dot = jnp.sum(probs * d_probs, axis=0, keepdims=True)
            d_scores = (probs * (d_probs - row_dot)).astype(BF)
            dq_parts.append(nn(k_turned[h * HEAD_DIM : (h + 1) * HEAD_DIM], d_scores))
            ds_all.append(d_scores)
            p_all.append(probs.astype(BF))
        dk2 = nn(jnp.concatenate(ds_all, axis=1), jnp.concatenate(q_heads, axis=0))
        dv2 = nn(jnp.concatenate(p_all, axis=1), jnp.concatenate(d_heads, axis=0))
        dq2 = jnp.concatenate(dq_parts, axis=0).T * factor
        dqs.append(
            (dq2 * cos_ref[0:rows, :] - swap_pairs(dq2) * sin_ref[0:rows, :]).astype(BF)
        )
        dks.append((dk2 * cos_ref[...] - swap_pairs(dk2) * sin_ref[...]).astype(BF))
        dvs.append(dv2.astype(BF))
    dq, dk, dv = (jnp.concatenate(v, axis=1) for v in (dqs, dks, dvs))
    store(0, nn(xm_turned[:, 0:rows], dq))
    store(1, nn(xm_turned[...], dk))
    store(2, nn(xm_turned[...], dv))
    return nt(jnp.concatenate([dk, dv], axis=1), wide(1, 3)), nt(dq, weight(0))


def back_kernel(
    S, T, I, cb,
    layer, all_a, grad_f, k_all, v_all, xm_all, dmid,
    frames_ref, q_ref, att_ref, lse_ref, mod_ref, db_ref, dmod_ref,
    cos_ref, sin_ref, mask_ref,
    layer_out, grads_out, rows_out, sum_a, sum_f,
    *scratch,
):
    nh, nq = grad_f.shape[0], all_a.shape[0]
    (xm_turned, db_turned, dx_sum, dx_ref, near, far, d_rows, ga_ref,
     w_stage, k_stage, v_stage, in_sem, send, recv, local, row_send, row_recv) = scratch[:17]
    rest = scratch[17:]
    p = Place(S, T, I)
    wires = Wires(send, recv, local)
    Q, _, rows, _ = xm_all.shape
    L = Q * 2 * rows
    steps, slots = nq * T, w_stage.shape[0]

    def fetch(n):
        j, t = divmod(n, T)
        slot = n % slots
        copies = [
            pltpu.make_async_copy(all_a.at[j, t], w_stage.at[slot], in_sem.at[0, slot]),
            pltpu.make_async_copy(k_all.at[n], k_stage.at[slot], in_sem.at[1, slot]),
            pltpu.make_async_copy(v_all.at[n], v_stage.at[slot], in_sem.at[2, slot]),
        ]
        for copy in copies:
            copy.start()
        return copies

    xm_copy = wires.move(xm_all, dx_ref)
    fetched = fetch(0)
    greet_all(p)
    chunks_f, chunks_a = [], []
    for j in range(nh):
        own, landing, rest = rest[0], rest[1:7], rest[7:]
        chunks_f.append(Reduce(p, wires, grad_f.at[j], sum_f.at[j], own, 0, landing))
    for j in range(nq):
        landing, rest = rest[:6], rest[6:]
        g = ga_ref.at[j]
        chunks_a.append(Reduce(p, wires, g, sum_a.at[j], g, p.c, landing))
    for chunk in chunks_f:
        chunk.phase0()
    xm_copy.wait()
    xm_turned[...] = dx_ref[...].reshape(L, D).T
    db_turned[...] = db_ref[...].T
    for chunk in chunks_f:
        chunk.phase1()
    layer_own, layer_in = swap_items(p, wires, layer, layer_out)

    plan = {n: [] for n in range(steps)}
    for m, chunk in enumerate(chunks_f):
        plan[min(m, steps - 1)].append(chunk.phase2)
        plan[min(m + 1, steps - 1)].append(chunk.phase3)
    for j, chunk in enumerate(chunks_a):
        plan[j * T + T - 1].insert(0, chunk.phase0)
        if j * T + T < steps:
            plan[j * T + T].append(chunk.phase1)

    for n in range(steps):
        j, t = divmod(n, T)
        slot = n % slots
        coming = fetch(n + 1) if slots == 2 and n + 1 < steps else None
        for copy in fetched:
            copy.wait()
        fetched = coming

        def store(b, value):
            ga_ref[j, t, :, :, :, :, b * cb : (b + 1) * cb] = value.astype(BF).reshape(
                ga_ref.shape[2:6] + (cb,)
            )

        dx, dx_own = attend_back_block(
            rows, cb,
            lambda b: w_stage[slot, :, b * cb : (b + 1) * cb],
            lambda b, e: w_stage[slot, :, b * cb : e * cb],
            db_ref, xm_turned, db_turned, cos_ref, sin_ref, mask_ref,
            q_ref.at[n], k_stage.at[slot], v_stage.at[slot], att_ref.at[n], lse_ref.at[n], store,
        )
        if n == 0:
            dx_sum[...] = dx
        else:
            dx_sum[...] += dx
        dx_sum[0:rows, :] += dx_own
        if slots == 1 and n + 1 < steps:
            fetched = fetch(n + 1)
        if n < steps - 1:
            for phase in plan[n]:
                phase()

    dx_ref[...] = dx_sum[...].astype(BF).reshape(dx_ref.shape)
    dmid_copy = wires.move(dmid, dx_sum.at[pl.ds(rows, rows)])
    core = wires.push(dx_ref.at[:, 1], near, p.group(0, 1 - p.c))
    for phase in plan[steps - 1]:
        phase()
    core.wait_recv()
    across = []
    for k in range(1, Q):
        dx_ref[k, 0] = dx_ref[k, 0] + near[k]
        across.append(wires.push(dx_ref.at[k, 0], far.at[k - 1], p.group(k)))
    for j, chunk in enumerate(chunks_a[:-1]):
        if j * T + T >= steps:
            chunk.phase1()
        chunk.phase2()
    chunks_a[-1].phase1()

    normed, inverse = layer_stats(frames_ref[...].reshape(rows, D).astype(F32))
    d_mod = dx_sum[0:rows, :] + near[0].astype(F32)
    for k in range(1, Q):
        across[k - 1].wait_recv()
        d_mod = d_mod + far[k - 1].astype(F32)
    incoming = layer_back(normed, inverse, d_mod * (1.0 + mod_ref[1:2, :]))
    dmid_copy.wait()
    fl = layer.shape[1]
    dx_ref[0, 0] = (dx_sum[rows : 2 * rows, :] + incoming).astype(BF)
    grads_own, grads_in = swap_items(
        p, wires, lambda n: dx_ref.at[0, 0, pl.ds(n * fl, fl)], grads_out
    )
    high = d_rows.shape[1]
    first = [
        jnp.sum(d_mod, axis=0, keepdims=True),
        jnp.sum(d_mod * normed.astype(BF).astype(F32), axis=0, keepdims=True),
    ]
    for t in range(T):
        for n in range(high):
            row, col = divmod((t * high + n) * 128, D)
            value = first[row] if row < 2 else dmod_ref[row : row + 1, :]
            d_rows[t, n : n + 1, :] = value[:, col : col + 128]
    rows_done = scatter_rows(
        p, row_send, row_recv, lambda s, t: (d_rows.at[t], rows_out.at[p.t, p.s])
    )
    rows_own = wires.move(d_rows.at[p.t], rows_out.at[p.t, p.s])
    for chunk in chunks_a[:-1]:
        chunk.phase3()
    chunks_a[-1].phase2()
    for chunk in chunks_f:
        chunk.phase4()
    chunks_a[-1].phase3()
    for chunk in chunks_a:
        chunk.phase4()
    for own in (grads_own, layer_own, rows_own):
        own.wait()
    landed(grads_in)
    landed(layer_in)
    rows_done()
    wires.close()


def back_call(
    S, T, I, cb, layer, all_a, grad_f, k, v, xm, d_mid,
    frames, q, att, lse, mod, d_branch, d_mod, cosine, sine, mask,
):
    nq, ca = all_a.shape[0], all_a.shape[3]
    nh, cf = grad_f.shape[0], grad_f.shape[6]
    rs = grad_f.shape[5]
    Z, Q, rows = S // 4, xm.shape[0], xm.shape[2]
    L = Q * 2 * rows
    high = 6 * D // T // 128
    slots = 2 if L <= 1024 else 1
    remote = 2 * (I - 1) + (nq + nh) * (Z + 2 * T + 2) + Q
    shape = jax.ShapeDtypeStruct
    dma = pltpu.SemaphoreType.DMA
    scratch = [
        pltpu.VMEM((D, L), BF),
        pltpu.VMEM((D, rows), BF),
        pltpu.VMEM((L, D), F32),
        pltpu.VMEM((Q, 2, rows, D), BF),
        pltpu.VMEM((Q, rows, D), BF),
        pltpu.VMEM((Q - 1, rows, D), BF),
        pltpu.VMEM((T, high, 128), F32),
        pltpu.VMEM((nq, T, Z, 2, 2, rs, ca), BF),
        pltpu.VMEM((slots, D, ca), BF),
        pltpu.VMEM((slots, L, cb), BF),
        pltpu.VMEM((slots, L, cb), BF),
        dma((3, slots)),
        dma((remote,)),
        dma((remote,)),
        dma((5 + nh,)),
        dma((S * T,)),
        dma((S * T,)),
    ]
    for _ in range(nh):
        scratch += [pltpu.VMEM((T, Z, 2, 1, rs, cf), BF)] + Reduce.landing(T, Z, rs, cf)
    for _ in range(nq):
        scratch += Reduce.landing(T, Z, rs, ca)
    return pl.pallas_call(
        partial(back_kernel, S, T, I, cb),
        out_shape=(
            shape(layer.shape, BF),
            shape(layer.shape, BF),
            shape((T, S, high, 128), F32),
            shape((nq, rs, ca), F32),
            shape((nh, rs, cf), F32),
        ),
        in_specs=[ANY] * 7 + [VMEM] * 10,
        out_specs=(ANY, ANY, ANY, VMEM, VMEM),
        scratch_shapes=scratch,
        compiler_params=pltpu.CompilerParams(
            collective_id=1, has_side_effects=True, vmem_limit_bytes=LIMIT
        ),
        name="backward",
    )(
        layer, all_a, grad_f, k, v, xm, d_mid,
        frames, q, att, lse, mod, d_branch, d_mod, cosine, sine, mask,
    )


def layer_stats(values):
    center = values - jnp.mean(values, axis=-1, keepdims=True)
    inverse = lax.rsqrt(jnp.mean(center * center, axis=-1, keepdims=True) + EPSILON)
    return center * inverse, inverse


def layer_back(normed, inverse, incoming):
    return inverse * (
        incoming
        - jnp.mean(incoming, axis=-1, keepdims=True)
        - normed * jnp.mean(incoming * normed, axis=-1, keepdims=True)
    )


def pack(blocks, width):
    rows = blocks[0].shape[0]
    cut = [b.reshape(rows, -1, width) for b in blocks]
    return jnp.concatenate(cut, axis=2).transpose(1, 0, 2)


def unpack(packed, count):
    steps, rows, wide = packed.shape
    cut = packed.reshape(steps, rows, count, wide // count)
    return [cut[:, :, n].transpose(1, 0, 2).reshape(rows, -1) for n in range(count)]


def per_device(
    S, T, frames, time_embed, lengths, w_query, w_key, w_value, w_out, w_up, w_down, w_mod, out_grad
):
    micro, rows_own, fl, _ = frames.shape
    batch = lengths.shape[1]
    I = micro * rows_own
    R = S // I
    Q = R // 2
    rs = w_query.shape[0]
    rows = I * fl
    L = R * rows
    cb = min(256, w_query.shape[1])
    hb = min(512, w_up.shape[1])
    s, t = lax.axis_index("seq"), lax.axis_index("tp")
    item = s // R
    place_r = s % R

    w_a = pack([w_query, w_key, w_value, w_out.T], cb)
    w_f = pack([w_up, w_down.T], hb)
    silu = jax.nn.silu(time_embed).astype(BF).reshape(micro * batch, D)
    silu_own = lax.dynamic_slice_in_dim(silu, s * rs, rs, 1)
    cols = w_mod.shape[1]
    parts = jnp.dot(silu_own, w_mod, preferred_element_type=F32)
    parts = parts.reshape(micro, T, rows_own, cols // 128, 128)
    parts = parts.transpose(1, 0, 2, 3, 4).reshape(T, I, cols // 128, 128)
    g = jnp.arange(R)
    r_of = (place_r // 2 + g // 2) % Q * 2 + (place_r % 2 + g % 2) % 2
    pos = fl * (jnp.arange(I)[None, :] * R + r_of[:, None])
    pos = (pos[:, :, None] + jnp.arange(fl)).reshape(L)
    length = lengths[item // rows_own, t * rows_own + item % rows_own]
    alive = pos < length
    live = alive[:rows].astype(F32)[:, None]
    lane = jnp.arange(128)
    mask = jnp.where((lane[None, :] == 0) & ~alive[:, None], NEGATIVE, 0.0).astype(BF)
    column = (lane % HEAD_DIM // 2).astype(F32)
    inverse = jnp.exp(column * (-2.0 * math.log(10000.0) / HEAD_DIM))
    angles = pos.astype(F32)[:, None] * inverse[None, :]
    cosine = jnp.cos(angles)
    sine = jnp.sin(angles) * jnp.where(lane % 2 == 0, -1.0, 1.0)

    (
        all_a, frames_in, xm, q, k, v, att, lse, mod, layer, grad_f, d_mid, d_branch, d_rows
    ) = front_call(
        S, T, I, cb, hb, frames.reshape(I, fl, D), out_grad.reshape(I, fl, D), parts,
        w_a, w_f, cosine, sine, mask, live,
    )
    layer_out, grad_input, mod_in, sum_a, sum_f = back_call(
        S, T, I, cb, layer, all_a.reshape(all_a.shape[:2] + (D, 4 * cb)),
        grad_f.reshape((grad_f.shape[0], T, S // 4, 2, 2, rs, 2 * hb)), k, v, xm, d_mid,
        frames_in, q, att, lse, mod, d_branch, d_rows, cosine, sine, mask,
    )
    mod_items = jnp.sum(mod_in.reshape(T, I, R, cols), axis=2).reshape(T * I, cols)
    silu_items = silu.reshape(micro, T, rows_own, D).transpose(1, 0, 2, 3).reshape(T * I, D)
    silu_items = lax.dynamic_slice_in_dim(silu_items, s * rs, rs, 1).astype(F32)
    grad_mod = jnp.dot(silu_items.T, mod_items, precision=HIGHEST)
    g_query, g_key, g_value, g_out = unpack(sum_a, 4)
    g_up, g_down = unpack(sum_f, 2)
    return (
        layer_out.reshape(frames.shape),
        grad_input.reshape(frames.shape),
        g_query,
        g_key,
        g_value,
        g_out.T,
        g_up,
        g_down.T,
        grad_mod,
    )


def solution(mesh):
    S, T = mesh.shape["seq"], mesh.shape["tp"]
    rows = P(None, "tp", "seq", None)
    return jax.shard_map(
        partial(per_device, S, T),
        mesh=mesh,
        in_specs=(
            rows,
            P(),
            P(),
            P("seq", "tp"),
            P("seq", "tp"),
            P("seq", "tp"),
            P("tp", "seq"),
            P("seq", "tp"),
            P("tp", "seq"),
            P("seq", "tp"),
            rows,
        ),
        out_specs=(
            rows,
            rows,
            P("seq", "tp"),
            P("seq", "tp"),
            P("seq", "tp"),
            P("tp", "seq"),
            P("seq", "tp"),
            P("tp", "seq"),
            P("seq", "tp"),
        ),
        check_vma=False,
    )
```

```python
from functools import partial
import math

import jax
import jax.numpy as jnp
from jax import lax
from jax.experimental import pallas as pl
from jax.experimental.pallas import tpu as pltpu
from jax.sharding import PartitionSpec as P

D = 1024
HEAD_DIM = 64
EPSILON = 1e-06
NEGATIVE = -1e30
BF = jnp.bfloat16
F32 = jnp.float32
HIGHEST = lax.Precision.HIGHEST
MESH = pl.DeviceIdType.MESH
ANY = pl.BlockSpec(memory_space=pl.ANY)
VMEM = pl.BlockSpec(memory_space=pltpu.VMEM)
LIMIT = 62 * 1024 * 1024


def nn(a, b):
    return lax.dot_general(a, b, (((1,), (0,)), ((), ())), preferred_element_type=F32)


def nt(a, b):
    return lax.dot_general(a, b, (((1,), (1,)), ((), ())), preferred_element_type=F32)


class Place:
    def __init__(self, S, T, I):
        self.S, self.T, self.I = S, T, I
        self.Z, self.R = S // 4, S // I
        self.Q = self.R // 2
        self.s, self.t = lax.axis_index("seq"), lax.axis_index("tp")
        self.z = lax.div(self.s, 4)
        self.x = lax.rem(lax.div(self.s, 2), 2)
        self.c = lax.rem(self.s, 2)
        self.i = lax.div(self.s, self.R)
        self.r = lax.rem(self.s, self.R)
        self.q = lax.div(self.r, 2)

    def at(self, z=None, x=None, c=None, t=None):
        z = self.z if z is None else z
        x = self.x if x is None else x
        c = self.c if c is None else c
        t = self.t if t is None else t
        return ((z * 2 + x) * 2 + c, t)

    def tp(self, k):
        return (self.s, lax.rem(self.t + k, self.T))

    def zs(self, k):
        return lax.rem(self.z + k, self.Z)

    def group(self, k, c=None):
        c = self.c if c is None else c
        return (self.i * self.R + lax.rem(self.q + k, self.Q) * 2 + c, self.t)


class Wires:
    def __init__(self, send, recv, local):
        self.send, self.recv, self.local = send, recv, local
        self.remote_count = self.local_count = 0
        self.sent = []

    def push(self, src, dst, device):
        n = self.remote_count
        self.remote_count += 1
        copy = pltpu.make_async_remote_copy(
            src_ref=src,
            dst_ref=dst,
            send_sem=self.send.at[n],
            recv_sem=self.recv.at[n],
            device_id=device,
            device_id_type=MESH,
        )
        copy.start()
        self.sent.append(copy)
        return copy

    def move(self, src, dst):
        n = self.local_count
        self.local_count += 1
        copy = pltpu.make_async_copy(src, dst, self.local.at[n])
        copy.start()
        return copy

    def close(self):
        for copy in self.sent:
            copy.wait_send()


def landed(copies):
    for copy in copies:
        copy.wait_recv()


def loop_group(place, first, body):
    total = place.R * place.T
    me = place.r * place.T + place.t

    def step(d, carry):
        other = lax.rem(me + d, total)
        body(d, place.i * place.R + lax.div(other, place.T), lax.rem(other, place.T))
        return carry

    lax.fori_loop(first, total, step, 0)


def greet(place):
    barrier = pltpu.get_barrier_semaphore()

    def signal(d, s, t):
        pl.semaphore_signal(barrier, inc=1, device_id=(s, t), device_id_type=MESH)

    for k in range(1, place.Z):
        signal(k, *place.at(z=place.zs(k)))
    loop_group(place, 1, signal)
    pl.semaphore_wait(barrier, place.Z - 1 + place.R * place.T - 1)


def spread_group(place, send, recv, src_of, dst):
    def copy(d, s, t):
        return pltpu.make_async_remote_copy(
            src_ref=src_of(t),
            dst_ref=dst.at[place.t, place.r],
            send_sem=send.at[d],
            recv_sem=recv.at[d],
            device_id=(s, t),
            device_id_type=MESH,
        )

    loop_group(place, 1, lambda d, s, t: copy(d, s, t).start())
    return lambda: loop_group(place, 1, lambda d, s, t: copy(d, s, t).wait())


class Phased:
    done = 0

    def upto(self, phase):
        while self.done <= phase:
            getattr(self, f"phase{self.done}")()
            self.done += 1


def split_rows(rs, quarters):
    upper = rs * quarters // 4 if rs * quarters // 4 % 16 == 0 else rs // 2
    return pl.ds(0, upper), pl.ds(upper, rs - upper)


class Gather(Phased):
    def __init__(self, place, wires, dst, quarters):
        self.p, self.w, self.dst = place, wires, dst
        self.upper, self.lower = split_rows(dst.shape[4], quarters)

    def phase0(self):
        p, w, dst = self.p, self.w, self.dst
        own = dst.at[0, p.z, p.x, p.c]
        self.along = [w.push(own, own, p.at(z=p.zs(k))) for k in range(1, p.Z)]

    def phase1(self):
        p, w, dst = self.p, self.w, self.dst
        landed(self.along)
        line = dst.at[0, :, p.x, p.c]
        self.sides = [
            w.push(
                dst.at[0, :, p.x, p.c, self.upper],
                dst.at[0, :, p.x, p.c, self.upper],
                p.at(x=1 - p.x),
            )
        ]
        for k in range(1, p.T):
            self.sides.append(
                w.push(
                    dst.at[0, :, p.x, p.c, self.lower],
                    dst.at[p.T - k, :, p.x, p.c, self.lower],
                    p.tp(k),
                )
            )
        self.cores = [w.push(line, line, p.at(c=1 - p.c))]

    def phase2(self):
        p, w, dst = self.p, self.w, self.dst
        landed(self.sides)
        self.last = []
        for k in range(1, p.T):
            self.last.append(
                w.push(
                    dst.at[0, :, :, p.c, self.upper],
                    dst.at[p.T - k, :, :, p.c, self.upper],
                    p.tp(k),
                )
            )
        part = dst.at[:, :, p.x, p.c, self.lower]
        self.last.append(w.push(part, part, p.at(x=1 - p.x)))
        part = dst.at[0, :, 1 - p.x, p.c, self.upper]
        self.cores.append(w.push(part, part, p.at(c=1 - p.c)))
        part = dst.at[pl.ds(1, p.T - 1), :, p.x, p.c, self.lower]
        self.cores.append(w.push(part, part, p.at(c=1 - p.c)))

    def phase3(self):
        p, w, dst = self.p, self.w, self.dst
        landed(self.last)
        part = dst.at[pl.ds(1, p.T - 1), :, :, p.c, self.upper]
        self.cores.append(w.push(part, part, p.at(c=1 - p.c)))
        part = dst.at[:, :, 1 - p.x, p.c, self.lower]
        self.cores.append(w.push(part, part, p.at(c=1 - p.c)))

    def phase4(self):
        landed(self.cores)


class Reduce(Phased):
    def __init__(self, place, wires, src, out, own, core_at, quarters, landing):
        self.p, self.w, self.src, self.out = place, wires, src, out
        self.own, self.core_at = own, core_at
        self.core, self.y_up, self.x_low, self.x_up, self.y_low, self.z_in = landing
        self.upper, self.lower = split_rows(own.shape[4], quarters)

    @staticmethod
    def landing(T, Z, rs, C, quarters):
        upper, lower = (part.size for part in split_rows(rs, quarters))
        return [
            pltpu.VMEM((T, Z, 2, rs, C), BF),
            pltpu.VMEM((T - 1, Z, 2, upper, C), BF),
            pltpu.VMEM((T, Z, lower, C), BF),
            pltpu.VMEM((Z, upper, C), BF),
            pltpu.VMEM((T - 1, Z, lower, C), BF),
            pltpu.VMEM((Z - 1, rs, C), BF),
        ]

    def phase0(self):
        p, w, src = self.p, self.w, self.src
        self.mine = None
        if self.own is not src:
            self.mine = w.move(src.at[:, :, :, pl.ds(p.c, 1)], self.own)
        self.pair = [w.push(src.at[:, :, :, 1 - p.c], self.core, p.at(c=1 - p.c))]

    def phase1(self):
        p, w, own, c = self.p, self.w, self.own, self.core_at
        if self.mine is not None:
            self.mine.wait()
        landed(self.pair)

        def add(n, carry):
            k, z = lax.div(n, p.Z), lax.rem(n, p.Z)
            for x in range(2):
                own[k, z, x, c] = own[k, z, x, c] + self.core[k, z, x]
            return carry

        lax.fori_loop(0, p.T * p.Z, add, 0)
        self.sides = [
            w.push(own.at[k, :, :, c, self.upper], self.y_up.at[k - 1], p.tp(k))
            for k in range(1, p.T)
        ]
        self.sides.append(
            w.push(own.at[:, :, 1 - p.x, c, self.lower], self.x_low, p.at(x=1 - p.x))
        )

    def phase2(self):
        p, w, own, c = self.p, self.w, self.own, self.core_at
        landed(self.sides)

        def add(z, carry):
            for x in range(2):
                total = own[0, z, x, c, self.upper].astype(F32)
                for k in range(1, p.T):
                    total = total + self.y_up[k - 1, z, x].astype(F32)
                own[0, z, x, c, self.upper] = total.astype(BF)
            for k in range(p.T):
                own[k, z, p.x, c, self.lower] = own[k, z, p.x, c, self.lower] + self.x_low[k, z]
            return carry

        lax.fori_loop(0, p.Z, add, 0)
        self.last = [w.push(own.at[0, :, 1 - p.x, c, self.upper], self.x_up, p.at(x=1 - p.x))]
        for k in range(1, p.T):
            self.last.append(
                w.push(own.at[k, :, p.x, c, self.lower], self.y_low.at[k - 1], p.tp(k))
            )

    def phase3(self):
        p, w, own, c = self.p, self.w, self.own, self.core_at
        landed(self.last)

        def add(z, carry):
            own[0, z, p.x, c, self.upper] = own[0, z, p.x, c, self.upper] + self.x_up[z]
            total = own[0, z, p.x, c, self.lower].astype(F32)
            for k in range(1, p.T):
                total = total + self.y_low[k - 1, z].astype(F32)
            own[0, z, p.x, c, self.lower] = total.astype(BF)
            return carry

        lax.fori_loop(0, p.Z, add, 0)
        self.along = [
            w.push(own.at[0, p.zs(k), p.x, c], self.z_in.at[k - 1], p.at(z=p.zs(k)))
            for k in range(1, p.Z)
        ]

    def phase4(self):
        p = self.p
        landed(self.along)
        total = self.own[0, p.z, p.x, self.core_at].astype(F32)
        for k in range(1, p.Z):
            total = total + self.z_in[k - 1].astype(F32)
        self.out[...] = total


def swap_items(place, wires, src, dst):
    p = place
    block = src if callable(src) else lambda n: src.at[n]
    own = wires.move(block(p.i), dst.at[p.i])
    copies = []
    for k in range(1, p.I):
        other = lax.rem(p.i + k, p.I)
        copies.append(wires.push(block(other), dst.at[p.i], (other * p.R + p.r, p.t)))
    return own, copies


def swap_pairs(v):
    lane = lax.broadcasted_iota(jnp.int32, v.shape, 1)
    return jnp.where(lax.rem(lane, 2) == 0, pltpu.roll(v, 127, 1), pltpu.roll(v, 1, 1))


def head_split(v):
    lane = lax.broadcasted_iota(jnp.int32, v.shape, 1)
    zero = jnp.zeros_like(v)
    return jnp.where(lane < HEAD_DIM, v, zero), jnp.where(lane < HEAD_DIM, zero, v)


def first_lane(rows):
    lane = lax.broadcasted_iota(jnp.int32, (rows, 128), 1)
    return jnp.where(lane == 0, 1.0, 0.0).astype(BF)


def attend_block(rows, cb, xm, weight, cos_ref, sin_ref, mask_ref, q_ref, k_ref, v_ref, att_ref, lse_ref):
    q_lin = nn(xm[0:rows, :], weight(0))
    k_lin = nn(xm, weight(1))
    v_ref[...] = nn(xm, weight(2)).astype(BF)
    ones = first_lane(rows)
    factor = HEAD_DIM**-0.5
    for p in range(cb // 128):
        lanes = slice(p * 128, p * 128 + 128)
        q2, k2 = q_lin[:, lanes], k_lin[:, lanes]
        q2 = (q2 * cos_ref[0:rows, :] + swap_pairs(q2) * sin_ref[0:rows, :]).astype(BF)
        q2 = q2 * jnp.asarray(factor, BF)
        k2 = (k2 * cos_ref[...] + swap_pairs(k2) * sin_ref[...]).astype(BF)
        q_ref[:, lanes] = q2
        k_ref[:, lanes] = k2
        k_long = jnp.concatenate([k2, mask_ref[...]], axis=1)
        v_turned = v_ref[:, lanes].T
        outs = []
        for h, q1 in enumerate(head_split(q2)):
            scores = nt(k_long, jnp.concatenate([q1, ones], axis=1))
            highest = jnp.max(scores, axis=0, keepdims=True)
            unnormed = jnp.exp(scores - highest)
            total = jnp.sum(unnormed, axis=0, keepdims=True)
            probs = (unnormed * (1.0 / total)).astype(BF)
            lse_ref[pl.ds(2 * p + h, 1), :] = highest + jnp.log(total)
            outs.append(nn(v_turned[h * HEAD_DIM : (h + 1) * HEAD_DIM], probs))
        att_ref[:, lanes] = jnp.concatenate(outs, axis=0).T.astype(BF)
    return nt(att_ref[...], weight(3))


def own_columns(place, time, rs):
    silu = (time / (1.0 + jnp.exp(-time))).astype(BF)
    feature = lax.broadcasted_iota(jnp.int32, (D, rs), 0)
    chosen = feature == lax.broadcasted_iota(jnp.int32, (D, rs), 1) + place.s * rs
    return nn(silu, jnp.where(chosen, 1.0, 0.0).astype(BF)).astype(BF)


def fill_tables(place, fl, length, cos_ref, sin_ref, mask_ref, live_ref):
    p = place
    lane = lax.broadcasted_iota(jnp.int32, (fl, 128), 1)
    row = lax.broadcasted_iota(jnp.int32, (fl, 128), 0)
    column = lax.div(lax.rem(lane, HEAD_DIM), 2).astype(F32)
    inverse = jnp.exp(column * (-2.0 * math.log(10000.0) / HEAD_DIM))
    sign = jnp.where(lax.rem(lane, 2) == 0, -1.0, 1.0)
    for g in range(p.R):
        r = lax.rem(p.q + g // 2, p.Q) * 2 + lax.rem(p.c + g % 2, 2)
        for n in range(p.I):
            at = pl.ds((g * p.I + n) * fl, fl)
            pos = row + fl * (n * p.R + r)
            angles = pos.astype(F32) * inverse
            cos_ref[at, :] = jnp.cos(angles)
            sin_ref[at, :] = jnp.sin(angles) * sign
            alive = pos < length
            mask_ref[at, :] = jnp.where((lane == 0) & ~alive, NEGATIVE, 0.0).astype(BF)
            if g == 0:
                live_ref[at, :] = jnp.where(alive, 1.0, 0.0)[:, 0:1]


def front_kernel(
    S, T, I, cb, hb,
    frames, cotangent, time_ref, lengths_ref, wq_ref, wk_ref, wv_ref, wo_ref, wu_ref, wd_ref, wm_ref,
    all_a, frames_in, xm_ref, q_ref, k_ref, v_ref, att_ref, lse_ref,
    mod_ref, layer_ref, grad_f, dmid_ref, dbranch_ref, dmod_ref, cos_ref, sin_ref, mask_ref,
    a_ref, f_ref, cot_in, parts, line_in, line_sum, parts_in, live_ref, branch_ref, mid_ref,
    normed_ref, mf_ref, mf_turned, db_ref, db_turned, out_sum, dmf_sum, stage,
    send, recv, local, row_send, row_recv, out_sem,
):
    p = Place(S, T, I)
    wires = Wires(send, recv, local)
    nq, nh = a_ref.shape[0], f_ref.shape[0]
    fl, rs = frames.shape[1], wq_ref.shape[0]
    rows, L = I * fl, I * fl * p.R
    micro, batch = lengths_ref.shape
    rows_own = I // micro
    for j in range(nq):
        cols = slice(j * cb, (j + 1) * cb)
        blocks = (wq_ref[:, cols], wk_ref[:, cols], wv_ref[:, cols], wo_ref[:, cols])
        a_ref[j, 0, p.z, p.x, p.c] = jnp.concatenate(blocks, axis=1)
    greet(p)
    chunks_a = [Gather(p, wires, a_ref.at[j], 2) for j in range(nq)]
    chunks_f = [Gather(p, wires, f_ref.at[j], 3) for j in range(nh)]
    chunks = chunks_a + chunks_f

    def upto(m, phase):
        if m < len(chunks):
            chunks[m].upto(phase)

    upto(0, 0)
    product = nn(own_columns(p, time_ref[...], rs), wm_ref[...])
    high = parts.shape[2]
    for item in range(micro * batch):
        m, b = divmod(item, batch)
        t, own = divmod(b, rows_own)
        for n in range(high):
            parts[t, m * rows_own + own, n : n + 1, :] = product[
                item : item + 1, n * 128 : (n + 1) * 128
            ]
    line = []
    for k in range(1, I):
        other = lax.rem(p.i + k, I)
        line.append(
            wires.push(parts.at[:, other], line_in.at[k - 1], (other * p.R + p.r, p.t))
        )
    for j in range(nh):
        cols = slice(j * hb, (j + 1) * hb)
        f_ref[j, 0, p.z, p.x, p.c] = jnp.concatenate([wu_ref[:, cols], wd_ref[:, cols]], axis=1)
    upto(0, 1)
    upto(1, 0)
    landed(line)
    for t in range(T):
        total = parts[t, p.i]
        for k in range(1, I):
            total = total + line_in[k - 1, t]
        line_sum[t] = total
    parts_in[p.t, p.r] = line_sum[p.t]
    group_done = spread_group(p, row_send, row_recv, lambda t: line_sum.at[t], parts_in)
    upto(0, 2)
    length = lengths_ref[lax.div(p.i, rows_own), p.t * rows_own + lax.rem(p.i, rows_own)]
    fill_tables(p, fl, length, cos_ref, sin_ref, mask_ref, live_ref)
    upto(1, 1)
    frames_own, frames_got = swap_items(p, wires, frames, frames_in)
    upto(0, 3)
    upto(1, 2)
    group_done()
    mod_ref[...] = jnp.zeros_like(mod_ref)
    for t in range(T):
        total = jnp.sum(parts_in[t], axis=0).astype(BF).astype(F32)
        for n in range(high):
            row, col = divmod((t * high + n) * 128, D)
            mod_ref[row : row + 1, col : col + 128] = total[n : n + 1]
    frames_own.wait()
    landed(frames_got)
    upto(2, 0)
    frame_rows = frames_in[...].reshape(rows, D).astype(F32)
    normed, _ = layer_stats(frame_rows)
    low = normed.astype(BF).astype(F32)
    xm_ref[0, 0] = (low * (1.0 + mod_ref[1:2, :]) + mod_ref[0:1, :]).astype(BF)
    sibling = p.group(0, 1 - p.c)
    across = [wires.push(xm_ref.at[0, 0], xm_ref.at[p.Q - k, 0], p.group(k)) for k in range(1, p.Q)]
    cores = [wires.push(xm_ref.at[0, 0], xm_ref.at[0, 1], sibling)]
    upto(2, 1)
    upto(3, 0)
    for k in range(1, p.Q):
        across[k - 1].wait_recv()
        cores.append(wires.push(xm_ref.at[p.Q - k, 0], xm_ref.at[p.Q - k, 1], sibling))
    upto(1, 3)
    landed(cores)

    cot_copies = []

    def ask_cotangent():
        own, got = swap_items(p, wires, cotangent, cot_in)
        cot_copies.extend([own, got])

    between = {
        0: lambda: (upto(2, 2), upto(3, 1), ask_cotangent()),
        1: lambda: (upto(3, 2),),
        2: lambda: (upto(2, 3),),
        3: lambda: (upto(3, 3),),
    }

    xm = xm_ref[...].reshape(L, D)
    copies = []
    for j in range(nq):
        chunks_a[j].upto(4)
        copies.append(wires.move(a_ref.at[j], all_a.at[j]))
        for t in range(T):
            n = j * T + t
            part = attend_block(
                rows, cb, xm,
                lambda b: a_ref[j, t, :, :, :, :, b * cb : (b + 1) * cb].reshape(D, cb),
                cos_ref, sin_ref, mask_ref,
                q_ref.at[n], k_ref.at[n], v_ref.at[n], att_ref.at[n], lse_ref.at[n],
            )
            if n == 0:
                branch_ref[...] = part
            else:
                branch_ref[...] += part
            between.get(n, tuple)()

    gate_attn, shift_ff = mod_ref[2:3, :], mod_ref[3:4, :]
    scale_ff, gate_ff = mod_ref[4:5, :], mod_ref[5:6, :]
    middle = (
        frames_in[...].reshape(rows, D).astype(F32)
        + gate_attn * live_ref[...] * branch_ref[...]
    )
    mid_ref[...] = middle
    normed, _ = layer_stats(middle)
    low = normed.astype(BF)
    normed_ref[...] = low
    modulated = (low.astype(F32) * (1.0 + scale_ff) + shift_ff).astype(BF)
    mf_ref[...] = modulated
    mf_turned[...] = modulated.T
    cot_copies[0].wait()
    landed(cot_copies[1])
    d_branch = (cot_in[...].reshape(rows, D).astype(F32) * gate_ff).astype(BF)
    db_ref[...] = d_branch
    db_turned[...] = d_branch.T

    pending = [None, None]
    for j in range(nh):
        chunks_f[j].upto(4)
        for t in range(T):
            n = j * T + t
            w_up = f_ref[j, t, :, :, :, :, 0:hb].reshape(D, hb)
            w_down = f_ref[j, t, :, :, :, :, hb : 2 * hb].reshape(D, hb)
            upper = nn(mf_ref[...], w_up)
            square = upper * upper
            slope = 0.7978845608
            tanh = jnp.tanh(slope * (upper + 0.044715 * upper * square))
            half = 0.5 * (1.0 + tanh)
            active = (upper * half).astype(BF)
            bend = half + 0.5 * upper * (1.0 - tanh * tanh) * (
                slope * (1.0 + 3 * 0.044715 * square)
            )
            d_upper = (nn(db_ref[...], w_down) * bend).astype(BF)
            if n == 0:
                out_sum[...] = nt(active, w_down)
                dmf_sum[...] = nt(d_upper, w_up)
            else:
                out_sum[...] += nt(active, w_down)
                dmf_sum[...] += nt(d_upper, w_up)
            slot = n % 2
            if pending[slot] is not None:
                pending[slot].wait()
            stage[slot, :, 0:hb] = nn(mf_turned[...], d_upper).astype(BF)
            stage[slot, :, hb : 2 * hb] = nn(db_turned[...], active).astype(BF)
            pending[slot] = pltpu.make_async_copy(stage.at[slot], grad_f.at[j, t], out_sem.at[slot])
            pending[slot].start()

    middle, branch_f = mid_ref[...], out_sum[...]
    layer_ref[...] = (middle + gate_ff * branch_f).astype(BF).reshape(layer_ref.shape)
    cot = cot_in[...].reshape(rows, D).astype(F32)
    normed, inverse = layer_stats(middle)
    dmf = dmf_sum[...]
    d_mid = cot + layer_back(normed, inverse, dmf * (1.0 + scale_ff))
    dmid_ref[...] = d_mid
    alive = d_mid * live_ref[...]
    dbranch_ref[...] = (alive * gate_attn).astype(BF)
    dmod_ref[...] = jnp.zeros_like(dmod_ref)
    dmod_ref[2:3, :] = jnp.sum(alive * branch_ref[...], axis=0, keepdims=True)
    dmod_ref[3:4, :] = jnp.sum(dmf, axis=0, keepdims=True)
    dmod_ref[4:5, :] = jnp.sum(dmf * normed_ref[...].astype(F32), axis=0, keepdims=True)
    dmod_ref[5:6, :] = jnp.sum(cot * branch_f, axis=0, keepdims=True)
    for copy in copies + [c for c in pending if c is not None]:
        copy.wait()
    wires.close()


def front_call(S, T, I, cb, hb, frames, cotangent, time, lengths, weights):
    w_query, w_up, w_mod = weights[0], weights[4], weights[6]
    rs = w_query.shape[0]
    nq, wide_a = w_query.shape[1] // cb, 4 * cb
    nh, wide_f = w_up.shape[1] // hb, 2 * hb
    fl = frames.shape[1]
    rows, Z, R = I * fl, S // 4, S // I
    Q, L, steps = R // 2, rows * R, nq * T
    high = w_mod.shape[1] // 128
    remote = 3 * (I - 1) + (nq + nh) * (Z + 2 * T + 4) + 2 * Q
    shape = jax.ShapeDtypeStruct
    vmem, dma = pltpu.VMEM, pltpu.SemaphoreType.DMA
    return pl.pallas_call(
        partial(front_kernel, S, T, I, cb, hb),
        out_shape=(
            shape((nq, T, Z, 2, 2, rs, wide_a), BF),
            shape(frames.shape, BF),
            shape((Q, 2, rows, D), BF),
            shape((steps, rows, cb), BF),
            shape((steps, L, cb), BF),
            shape((steps, L, cb), BF),
            shape((steps, rows, cb), BF),
            shape((steps, 8, rows), F32),
            shape((8, D), F32),
            shape(frames.shape, BF),
            shape((nh, T, D, wide_f), BF),
            shape((rows, D), F32),
            shape((rows, D), BF),
            shape((8, D), F32),
            shape((L, 128), F32),
            shape((L, 128), F32),
            shape((L, 128), BF),
        ),
        in_specs=[ANY] * 2 + [VMEM, pl.BlockSpec(memory_space=pltpu.SMEM)] + [VMEM] * 7,
        out_specs=(ANY,) + (VMEM,) * 9 + (ANY,) + (VMEM,) * 6,
        scratch_shapes=[
            vmem((nq, T, Z, 2, 2, rs, wide_a), BF),
            vmem((nh, T, Z, 2, 2, rs, wide_f), BF),
            vmem(frames.shape, BF),
            vmem((T, I, high, 128), F32),
            vmem((I - 1, T, high, 128), F32),
            vmem((T, high, 128), F32),
            vmem((T, R, high, 128), F32),
            vmem((rows, 1), F32),
            vmem((rows, D), F32),
            vmem((rows, D), F32),
            vmem((rows, D), BF),
            vmem((rows, D), BF),
            vmem((D, rows), BF),
            vmem((rows, D), BF),
            vmem((D, rows), BF),
            vmem((rows, D), F32),
            vmem((rows, D), F32),
            vmem((2, D, wide_f), BF),
            dma((remote,)),
            dma((remote,)),
            dma((2 + nq,)),
            dma((R * T,)),
            dma((R * T,)),
            dma((2,)),
        ],
        compiler_params=pltpu.CompilerParams(
            collective_id=0, has_side_effects=True, vmem_limit_bytes=LIMIT
        ),
        name="forward",
    )(frames, cotangent, time, lengths, *weights)


def attend_back_block(
    rows, cb, weight, wide, db_ref, xm_turned, db_turned, cos_ref, sin_ref, mask_ref,
    q_ref, k_ref, v_ref, att_ref, lse_ref, store,
):
    d_att = nn(db_ref[...], weight(3)).astype(BF)
    store(3, nn(db_turned[...], att_ref[...]))
    ones = first_lane(rows)
    factor = HEAD_DIM**-0.5
    dqs, dks, dvs = [], [], []
    for p in range(cb // 128):
        lanes = slice(p * 128, p * 128 + 128)
        q2, k2, v2 = q_ref[:, lanes], k_ref[:, lanes], v_ref[:, lanes]
        k_long = jnp.concatenate([k2, mask_ref[...]], axis=1)
        k_turned = k2.T
        dq_parts, ds_all, p_all = [], [], []
        q_heads, d_heads = head_split(q2), head_split(d_att[:, lanes])
        for h in range(2):
            scores = nt(k_long, jnp.concatenate([q_heads[h], ones], axis=1))
            probs = jnp.exp(scores - lse_ref[pl.ds(2 * p + h, 1), :])
            d_probs = nt(v2, d_heads[h])
            row_dot = jnp.sum(probs * d_probs, axis=0, keepdims=True)
            d_scores = (probs * (d_probs - row_dot)).astype(BF)
            dq_parts.append(nn(k_turned[h * HEAD_DIM : (h + 1) * HEAD_DIM], d_scores))
            ds_all.append(d_scores)
            p_all.append(probs.astype(BF))
        dk2 = nn(jnp.concatenate(ds_all, axis=1), jnp.concatenate(q_heads, axis=0))
        dv2 = nn(jnp.concatenate(p_all, axis=1), jnp.concatenate(d_heads, axis=0))
        dq2 = jnp.concatenate(dq_parts, axis=0).T * factor
        dqs.append(
            (dq2 * cos_ref[0:rows, :] - swap_pairs(dq2) * sin_ref[0:rows, :]).astype(BF)
        )
        dks.append((dk2 * cos_ref[...] - swap_pairs(dk2) * sin_ref[...]).astype(BF))
        dvs.append(dv2.astype(BF))
    dq, dk, dv = (jnp.concatenate(v, axis=1) for v in (dqs, dks, dvs))
    store(0, nn(xm_turned[:, 0:rows], dq))
    store(1, nn(xm_turned[...], dk))
    store(2, nn(xm_turned[...], dv))
    return nt(jnp.concatenate([dk, dv], axis=1), wide(1, 3)), nt(dq, weight(0))


def back_kernel(
    S, T, I, cb,
    layer, all_a, grad_f, k_all, v_all, xm_all, dmid, frames,
    q_ref, att_ref, lse_ref, mod_ref, db_ref, dmod_ref,
    cos_ref, sin_ref, mask_ref,
    layer_out, grads_out, rows_out, sum_a, sum_f,
    *scratch,
):
    nh, nq = grad_f.shape[0], all_a.shape[0]
    (xm_turned, db_turned, dx_sum, dx_ref, near, far, d_rows, group_in, group_sum, ga_ref,
     w_stage, k_stage, v_stage, in_sem, send, recv, local, row_send, row_recv) = scratch[:19]
    rest = scratch[19:]
    p = Place(S, T, I)
    wires = Wires(send, recv, local)
    Q, _, rows, _ = xm_all.shape
    L = Q * 2 * rows
    steps, slots = nq * T, w_stage.shape[0]

    def fetch(n):
        j, t = divmod(n, T)
        slot = n % slots
        copies = [
            pltpu.make_async_copy(all_a.at[j, t], w_stage.at[slot], in_sem.at[0, slot]),
            pltpu.make_async_copy(k_all.at[n], k_stage.at[slot], in_sem.at[1, slot]),
            pltpu.make_async_copy(v_all.at[n], v_stage.at[slot], in_sem.at[2, slot]),
        ]
        for copy in copies:
            copy.start()
        return copies

    xm_copy = wires.move(xm_all, dx_ref)
    fetched = fetch(0)
    greet(p)
    chunks_f, chunks_a = [], []
    for j in range(nh):
        own, landing, rest = rest[0], rest[1:7], rest[7:]
        chunks_f.append(Reduce(p, wires, grad_f.at[j], sum_f.at[j], own, 0, 2, landing))
    for j in range(nq):
        landing, rest = rest[:6], rest[6:]
        g = ga_ref.at[j]
        chunks_a.append(Reduce(p, wires, g, sum_a.at[j], g, p.c, 2, landing))
    chunks = chunks_f + chunks_a

    def upto(m, phase):
        if m < len(chunks):
            chunks[m].upto(phase)

    upto(0, 0)
    if nh > 1:
        upto(1, 0)
    xm_copy.wait()
    xm_turned[...] = dx_ref[...].reshape(L, D).T
    db_turned[...] = db_ref[...].T
    for m in range(nh):
        upto(m, 1)
    layer_own, layer_in = swap_items(p, wires, layer, layer_out)

    between = {
        0: lambda: None,
        1: lambda: (upto(nh, 0), upto(0, 2), upto(nh - 1, 2), upto(nh, 1)),
        2: lambda: (upto(0, 3), upto(nh - 1, 3)),
    }
    if nq == 1:
        between = {}

    for n in range(steps):
        j, t = divmod(n, T)
        slot = n % slots
        coming = fetch(n + 1) if slots == 2 and n + 1 < steps else None
        for copy in fetched:
            copy.wait()
        fetched = coming

        def store(b, value):
            ga_ref[j, t, :, :, :, :, b * cb : (b + 1) * cb] = value.astype(BF).reshape(
                ga_ref.shape[2:6] + (cb,)
            )

        dx, dx_own = attend_back_block(
            rows, cb,
            lambda b: w_stage[slot, :, b * cb : (b + 1) * cb],
            lambda b, e: w_stage[slot, :, b * cb : e * cb],
            db_ref, xm_turned, db_turned, cos_ref, sin_ref, mask_ref,
            q_ref.at[n], k_stage.at[slot], v_stage.at[slot], att_ref.at[n], lse_ref.at[n], store,
        )
        if n == 0:
            dx_sum[...] = dx
        else:
            dx_sum[...] += dx
        dx_sum[0:rows, :] += dx_own
        if slots == 1 and n + 1 < steps:
            fetched = fetch(n + 1)
        if n < steps - 1:
            between.get(n, tuple)()

    dx_ref[...] = dx_sum[...].astype(BF).reshape(dx_ref.shape)
    dmid_copy = wires.move(dmid, dx_sum.at[pl.ds(rows, rows)])
    fl = layer.shape[1]
    frame_copies = [
        wires.move(frames.at[n], xm_turned.at[pl.ds(n * fl, fl), pl.ds(0, D)]) for n in range(I)
    ]
    core = wires.push(dx_ref.at[:, 1], near, p.group(0, 1 - p.c))
    last = len(chunks) - 1
    upto(last, 0)
    core.wait_recv()
    across = []
    for k in range(1, Q):
        dx_ref[k, 0] = dx_ref[k, 0] + near[k]
        across.append(wires.push(dx_ref.at[k, 0], far.at[k - 1], p.group(k)))
    for m in range(last):
        upto(m, 2)
    upto(last, 1)
    for m in range(nh):
        upto(m, 3)

    for copy in frame_copies:
        copy.wait()
    normed, inverse = layer_stats(xm_turned[0:rows, 0:D].astype(F32))
    d_mod = dx_sum[0:rows, :] + near[0].astype(F32)
    for k in range(1, Q):
        across[k - 1].wait_recv()
        d_mod = d_mod + far[k - 1].astype(F32)
    incoming = layer_back(normed, inverse, d_mod * (1.0 + mod_ref[1:2, :]))
    dmid_copy.wait()
    dx_ref[0, 0] = (dx_sum[rows : 2 * rows, :] + incoming).astype(BF)
    grads_own, grads_in = swap_items(
        p, wires, lambda n: dx_ref.at[0, 0, pl.ds(n * fl, fl)], grads_out
    )
    high = d_rows.shape[1]
    first = [
        jnp.sum(d_mod, axis=0, keepdims=True),
        jnp.sum(d_mod * normed.astype(BF).astype(F32), axis=0, keepdims=True),
    ]
    for t in range(T):
        for n in range(high):
            row, col = divmod((t * high + n) * 128, D)
            value = first[row] if row < 2 else dmod_ref[row : row + 1, :]
            d_rows[t, n : n + 1, :] = value[:, col : col + 128]
    group_in[p.t, p.r] = d_rows[p.t]
    group_done = spread_group(p, row_send, row_recv, lambda t: d_rows.at[t], group_in)
    for m in range(last):
        upto(m, 3)
    group_done()
    for t in range(T):
        group_sum[t] = jnp.sum(group_in[t], axis=0)
    rows_own = wires.move(group_sum, rows_out.at[p.i])
    line = []
    for k in range(1, I):
        other = lax.rem(p.i + k, I)
        line.append(wires.push(group_sum, rows_out.at[p.i], (other * p.R + p.r, p.t)))
    upto(last, 2)
    for m in range(nh):
        upto(m, 4)
    upto(last, 3)
    for m in range(last + 1):
        upto(m, 4)
    landed(line)
    for own in (grads_own, layer_own, rows_own):
        own.wait()
    landed(grads_in)
    landed(layer_in)
    wires.close()


def back_call(
    S, T, I, cb, layer, all_a, grad_f, k, v, xm, d_mid, frames,
    q, att, lse, mod, d_branch, d_mod, cosine, sine, mask,
):
    nq, ca = all_a.shape[0], all_a.shape[3]
    nh, cf = grad_f.shape[0], grad_f.shape[6]
    rs = grad_f.shape[5]
    Z, Q, rows = S // 4, xm.shape[0], xm.shape[2]
    L = Q * 2 * rows
    high = 6 * D // T // 128
    slots = 2 if L <= 1024 else 1
    remote = 3 * (I - 1) + (nq + nh) * (Z + 2 * T + 2) + Q
    R = S // I
    shape = jax.ShapeDtypeStruct
    dma = pltpu.SemaphoreType.DMA
    scratch = [
        pltpu.VMEM((D, L), BF),
        pltpu.VMEM((D, rows), BF),
        pltpu.VMEM((L, D), F32),
        pltpu.VMEM((Q, 2, rows, D), BF),
        pltpu.VMEM((Q, rows, D), BF),
        pltpu.VMEM((Q - 1, rows, D), BF),
        pltpu.VMEM((T, high, 128), F32),
        pltpu.VMEM((T, R, high, 128), F32),
        pltpu.VMEM((T, high, 128), F32),
        pltpu.VMEM((nq, T, Z, 2, 2, rs, ca), BF),
        pltpu.VMEM((slots, D, ca), BF),
        pltpu.VMEM((slots, L, cb), BF),
        pltpu.VMEM((slots, L, cb), BF),
        dma((3, slots)),
        dma((remote,)),
        dma((remote,)),
        dma((5 + nh + I,)),
        dma((R * T,)),
        dma((R * T,)),
    ]
    for _ in range(nh):
        scratch += [pltpu.VMEM((T, Z, 2, 1, rs, cf), BF)] + Reduce.landing(T, Z, rs, cf, 2)
    for _ in range(nq):
        scratch += Reduce.landing(T, Z, rs, ca, 2)
    return pl.pallas_call(
        partial(back_kernel, S, T, I, cb),
        out_shape=(
            shape(layer.shape, BF),
            shape(layer.shape, BF),
            shape((I, T, high, 128), F32),
            shape((nq, rs, ca), F32),
            shape((nh, rs, cf), F32),
        ),
        in_specs=[ANY] * 8 + [VMEM] * 9,
        out_specs=(ANY, ANY, ANY, VMEM, VMEM),
        scratch_shapes=scratch,
        compiler_params=pltpu.CompilerParams(
            collective_id=1, has_side_effects=True, vmem_limit_bytes=LIMIT
        ),
        name="backward",
    )(
        layer, all_a, grad_f, k, v, xm, d_mid, frames,
        q, att, lse, mod, d_branch, d_mod, cosine, sine, mask,
    )


def layer_stats(values):
    center = values - jnp.mean(values, axis=-1, keepdims=True)
    inverse = lax.rsqrt(jnp.mean(center * center, axis=-1, keepdims=True) + EPSILON)
    return center * inverse, inverse


def layer_back(normed, inverse, incoming):
    return inverse * (
        incoming
        - jnp.mean(incoming, axis=-1, keepdims=True)
        - normed * jnp.mean(incoming * normed, axis=-1, keepdims=True)
    )


def finish_kernel(
    S, T, I, micro, time_ref, rows_ref, sum_a, sum_f, layer_in, grads_in,
    layer_ref, grads_ref, gq_ref, gk_ref, gv_ref, go_ref, gu_ref, gd_ref, gm_ref, items_ref,
):
    p = Place(S, T, I)
    nq, rs, wide_a = sum_a.shape
    nh, _, wide_f = sum_f.shape
    cb, hb = wide_a // 4, wide_f // 2
    layer_ref[...] = layer_in[...]
    grads_ref[...] = grads_in[...]
    for j in range(nq):
        for b, ref in enumerate((gq_ref, gk_ref, gv_ref, go_ref)):
            ref[:, j * cb : (j + 1) * cb] = sum_a[j, :, b * cb : (b + 1) * cb]
    for j in range(nh):
        gu_ref[:, j * hb : (j + 1) * hb] = sum_f[j, :, 0:hb]
        gd_ref[:, j * hb : (j + 1) * hb] = sum_f[j, :, hb : 2 * hb]
    high = rows_ref.shape[2]
    rows_own = I // micro
    for item in range(I * T):
        m, b = divmod(item, rows_own * T)
        i, t = m * rows_own + b % rows_own, b // rows_own
        for n in range(high):
            items_ref[item : item + 1, n * 128 : (n + 1) * 128] = rows_ref[i, t, n : n + 1, :]
    silu = own_columns(p, time_ref[...], rs).astype(F32)
    gm_ref[...] = lax.dot_general(
        silu, items_ref[...], (((0,), (0,)), ((), ())), precision=HIGHEST,
        preferred_element_type=F32,
    )


def finish_call(S, T, I, micro, time, rows, sum_a, sum_f, layer, grads, weights):
    shape = jax.ShapeDtypeStruct
    return pl.pallas_call(
        partial(finish_kernel, S, T, I, micro),
        out_shape=(shape(layer.shape, BF), shape(grads.shape, BF))
        + tuple(shape(w.shape, F32) for w in weights),
        in_specs=[VMEM] * 6,
        out_specs=(VMEM,) * 9,
        scratch_shapes=[pltpu.VMEM((I * T, weights[6].shape[1]), F32)],
        compiler_params=pltpu.CompilerParams(vmem_limit_bytes=LIMIT),
        name="finish",
    )(time, rows, sum_a, sum_f, layer, grads)


def per_device(
    S, T, frames, time_embed, lengths, w_query, w_key, w_value, w_out, w_up, w_down, w_mod, out_grad
):
    micro, rows_own, fl, _ = frames.shape
    batch = lengths.shape[1]
    I = micro * rows_own
    rs = w_query.shape[0]
    cb = min(256, w_query.shape[1])
    hb = min(512, w_up.shape[1])
    time = time_embed.reshape(micro * batch, D)
    weights = (w_query, w_key, w_value, w_out.T, w_up, w_down.T, w_mod)
    (
        all_a, frames_in, xm, q, k, v, att, lse, mod, layer, grad_f, d_mid, d_branch, d_rows,
        cosine, sine, mask,
    ) = front_call(
        S, T, I, cb, hb, frames.reshape(I, fl, D), out_grad.reshape(I, fl, D), time, lengths, weights
    )
    layer_out, grad_input, rows_in, sum_a, sum_f = back_call(
        S, T, I, cb, layer, all_a.reshape(all_a.shape[:2] + (D, 4 * cb)),
        grad_f.reshape((grad_f.shape[0], T, S // 4, 2, 2, rs, 2 * hb)), k, v, xm, d_mid,
        frames_in, q, att, lse, mod, d_branch, d_rows, cosine, sine, mask,
    )
    outs = finish_call(S, T, I, micro, time, rows_in, sum_a, sum_f, layer_out, grad_input, weights)
    layer_out, grad_input, g_query, g_key, g_value, g_out, g_up, g_down, g_mod = outs
    return (
        layer_out.reshape(frames.shape), grad_input.reshape(frames.shape),
        g_query, g_key, g_value, g_out.T, g_up, g_down.T, g_mod,
    )


def solution(mesh):
    S, T = mesh.shape["seq"], mesh.shape["tp"]
    rows = P(None, "tp", "seq", None)
    return jax.shard_map(
        partial(per_device, S, T),
        mesh=mesh,
        in_specs=(
            rows,
            P(),
            P(),
            P("seq", "tp"),
            P("seq", "tp"),
            P("seq", "tp"),
            P("tp", "seq"),
            P("seq", "tp"),
            P("tp", "seq"),
            P("seq", "tp"),
            rows,
        ),
        out_specs=(
            rows,
            rows,
            P("seq", "tp"),
            P("seq", "tp"),
            P("seq", "tp"),
            P("tp", "seq"),
            P("seq", "tp"),
            P("tp", "seq"),
            P("seq", "tp"),
        ),
        check_vma=False,
    )
```

```python
from functools import partial
import math

import jax
import jax.numpy as jnp
from jax import lax
from jax.experimental import pallas as pl
from jax.experimental.pallas import tpu as pltpu
from jax.sharding import PartitionSpec as P

D = 1024
HEAD_DIM = 64
EPSILON = 1e-06
NEGATIVE = -1e30
BF = jnp.bfloat16
F32 = jnp.float32
HIGHEST = lax.Precision.HIGHEST
MESH = pl.DeviceIdType.MESH
ANY = pl.BlockSpec(memory_space=pl.ANY)
VMEM = pl.BlockSpec(memory_space=pltpu.VMEM)
LIMIT = 62 * 1024 * 1024


def nn(a, b):
    return lax.dot_general(a, b, (((1,), (0,)), ((), ())), preferred_element_type=F32)


def nt(a, b):
    return lax.dot_general(a, b, (((1,), (1,)), ((), ())), preferred_element_type=F32)


class Place:
    def __init__(self, S, T, I):
        self.S, self.T, self.I = S, T, I
        self.Z, self.R = S // 4, S // I
        self.Q = self.R // 2
        self.s, self.t = lax.axis_index("seq"), lax.axis_index("tp")
        self.z = lax.div(self.s, 4)
        self.x = lax.rem(lax.div(self.s, 2), 2)
        self.c = lax.rem(self.s, 2)
        self.i = lax.div(self.s, self.R)
        self.r = lax.rem(self.s, self.R)
        self.q = lax.div(self.r, 2)

    def at(self, z=None, x=None, c=None, t=None):
        z = self.z if z is None else z
        x = self.x if x is None else x
        c = self.c if c is None else c
        t = self.t if t is None else t
        return ((z * 2 + x) * 2 + c, t)

    def tp(self, k):
        return (self.s, lax.rem(self.t + k, self.T))

    def zs(self, k):
        return lax.rem(self.z + k, self.Z)

    def group(self, k, c=None):
        c = self.c if c is None else c
        return (self.i * self.R + lax.rem(self.q + k, self.Q) * 2 + c, self.t)


class Wires:
    def __init__(self, send, recv, local):
        self.send, self.recv, self.local = send, recv, local
        self.remote_count = self.local_count = 0
        self.sent = []

    def push(self, src, dst, device):
        n = self.remote_count
        self.remote_count += 1
        copy = pltpu.make_async_remote_copy(
            src_ref=src,
            dst_ref=dst,
            send_sem=self.send.at[n],
            recv_sem=self.recv.at[n],
            device_id=device,
            device_id_type=MESH,
        )
        copy.start()
        self.sent.append(copy)
        return copy

    def move(self, src, dst):
        n = self.local_count
        self.local_count += 1
        copy = pltpu.make_async_copy(src, dst, self.local.at[n])
        copy.start()
        return copy

    def close(self):
        for copy in self.sent:
            copy.wait_send()


def landed(copies):
    for copy in copies:
        copy.wait_recv()


def loop_group(place, first, body):
    total = place.R * place.T
    me = place.r * place.T + place.t

    def step(d, carry):
        other = lax.rem(me + d, total)
        body(d, place.i * place.R + lax.div(other, place.T), lax.rem(other, place.T))
        return carry

    lax.fori_loop(first, total, step, 0)


def greet(place):
    barrier = pltpu.get_barrier_semaphore()

    def signal(d, s, t):
        pl.semaphore_signal(barrier, inc=1, device_id=(s, t), device_id_type=MESH)

    for k in range(1, place.Z):
        signal(k, *place.at(z=place.zs(k)))
    loop_group(place, 1, signal)
    pl.semaphore_wait(barrier, place.Z - 1 + place.R * place.T - 1)


def spread_group(place, send, recv, src_of, dst):
    def copy(d, s, t):
        return pltpu.make_async_remote_copy(
            src_ref=src_of(t),
            dst_ref=dst.at[place.t, place.r],
            send_sem=send.at[d],
            recv_sem=recv.at[d],
            device_id=(s, t),
            device_id_type=MESH,
        )

    loop_group(place, 1, lambda d, s, t: copy(d, s, t).start())
    return lambda: loop_group(place, 1, lambda d, s, t: copy(d, s, t).wait())


class Phased:
    done = 0

    def upto(self, phase):
        while self.done <= phase:
            getattr(self, f"phase{self.done}")()
            self.done += 1


def split_rows(rs, quarters):
    upper = rs * quarters // 4 if rs * quarters // 4 % 16 == 0 else rs // 2
    return pl.ds(0, upper), pl.ds(upper, rs - upper)


class Gather(Phased):
    def __init__(self, place, wires, dst, quarters):
        self.p, self.w, self.dst = place, wires, dst
        self.upper, self.lower = split_rows(dst.shape[4], quarters)

    def phase0(self):
        p, w, dst = self.p, self.w, self.dst
        own = dst.at[0, p.z, p.x, p.c]
        self.along = [w.push(own, own, p.at(z=p.zs(k))) for k in range(1, p.Z)]

    def phase1(self):
        p, w, dst = self.p, self.w, self.dst
        landed(self.along)
        line = dst.at[0, :, p.x, p.c]
        self.sides = [
            w.push(
                dst.at[0, :, p.x, p.c, self.upper],
                dst.at[0, :, p.x, p.c, self.upper],
                p.at(x=1 - p.x),
            )
        ]
        for k in range(1, p.T):
            self.sides.append(
                w.push(
                    dst.at[0, :, p.x, p.c, self.lower],
                    dst.at[p.T - k, :, p.x, p.c, self.lower],
                    p.tp(k),
                )
            )
        self.cores = [w.push(line, line, p.at(c=1 - p.c))]

    def phase2(self):
        p, w, dst = self.p, self.w, self.dst
        landed(self.sides)
        self.last = []
        for k in range(1, p.T):
            self.last.append(
                w.push(
                    dst.at[0, :, :, p.c, self.upper],
                    dst.at[p.T - k, :, :, p.c, self.upper],
                    p.tp(k),
                )
            )
        part = dst.at[:, :, p.x, p.c, self.lower]
        self.last.append(w.push(part, part, p.at(x=1 - p.x)))
        part = dst.at[0, :, 1 - p.x, p.c, self.upper]
        self.cores.append(w.push(part, part, p.at(c=1 - p.c)))
        part = dst.at[pl.ds(1, p.T - 1), :, p.x, p.c, self.lower]
        self.cores.append(w.push(part, part, p.at(c=1 - p.c)))

    def phase3(self):
        p, w, dst = self.p, self.w, self.dst
        landed(self.last)
        part = dst.at[pl.ds(1, p.T - 1), :, :, p.c, self.upper]
        self.cores.append(w.push(part, part, p.at(c=1 - p.c)))
        part = dst.at[:, :, 1 - p.x, p.c, self.lower]
        self.cores.append(w.push(part, part, p.at(c=1 - p.c)))

    def phase4(self):
        landed(self.cores)


class Reduce(Phased):
    def __init__(self, place, wires, src, out, own, core_at, quarters, landing):
        self.p, self.w, self.src, self.out = place, wires, src, out
        self.own, self.core_at = own, core_at
        self.core, self.y_up, self.x_low, self.x_up, self.y_low, self.z_in = landing
        self.upper, self.lower = split_rows(own.shape[4], quarters)

    @staticmethod
    def landing(T, Z, rs, C, quarters):
        upper, lower = (part.size for part in split_rows(rs, quarters))
        return [
            pltpu.VMEM((T, Z, 2, rs, C), BF),
            pltpu.VMEM((T - 1, Z, 2, upper, C), BF),
            pltpu.VMEM((T, Z, lower, C), BF),
            pltpu.VMEM((Z, upper, C), BF),
            pltpu.VMEM((T - 1, Z, lower, C), BF),
            pltpu.VMEM((Z - 1, rs, C), BF),
        ]

    def phase0(self):
        p, w, src = self.p, self.w, self.src
        self.mine = None
        if self.own is not src:
            self.mine = w.move(src.at[:, :, :, pl.ds(p.c, 1)], self.own)
        self.pair = [w.push(src.at[:, :, :, 1 - p.c], self.core, p.at(c=1 - p.c))]

    def phase1(self):
        p, w, own, c = self.p, self.w, self.own, self.core_at
        if self.mine is not None:
            self.mine.wait()
        landed(self.pair)

        def add(n, carry):
            k, z = lax.div(n, p.Z), lax.rem(n, p.Z)
            for x in range(2):
                own[k, z, x, c] = own[k, z, x, c] + self.core[k, z, x]
            return carry

        lax.fori_loop(0, p.T * p.Z, add, 0)
        self.sides = [
            w.push(own.at[k, :, :, c, self.upper], self.y_up.at[k - 1], p.tp(k))
            for k in range(1, p.T)
        ]
        self.sides.append(
            w.push(own.at[:, :, 1 - p.x, c, self.lower], self.x_low, p.at(x=1 - p.x))
        )

    def phase2(self):
        p, w, own, c = self.p, self.w, self.own, self.core_at
        landed(self.sides)

        def add(z, carry):
            for x in range(2):
                total = own[0, z, x, c, self.upper].astype(F32)
                for k in range(1, p.T):
                    total = total + self.y_up[k - 1, z, x].astype(F32)
                own[0, z, x, c, self.upper] = total.astype(BF)
            for k in range(p.T):
                own[k, z, p.x, c, self.lower] = own[k, z, p.x, c, self.lower] + self.x_low[k, z]
            return carry

        lax.fori_loop(0, p.Z, add, 0)
        self.last = [w.push(own.at[0, :, 1 - p.x, c, self.upper], self.x_up, p.at(x=1 - p.x))]
        for k in range(1, p.T):
            self.last.append(
                w.push(own.at[k, :, p.x, c, self.lower], self.y_low.at[k - 1], p.tp(k))
            )

    def phase3(self):
        p, w, own, c = self.p, self.w, self.own, self.core_at
        landed(self.last)

        def add(z, carry):
            own[0, z, p.x, c, self.upper] = own[0, z, p.x, c, self.upper] + self.x_up[z]
            total = own[0, z, p.x, c, self.lower].astype(F32)
            for k in range(1, p.T):
                total = total + self.y_low[k - 1, z].astype(F32)
            own[0, z, p.x, c, self.lower] = total.astype(BF)
            return carry

        lax.fori_loop(0, p.Z, add, 0)
        self.along = [
            w.push(own.at[0, p.zs(k), p.x, c], self.z_in.at[k - 1], p.at(z=p.zs(k)))
            for k in range(1, p.Z)
        ]

    def phase4(self):
        p = self.p
        landed(self.along)
        total = self.own[0, p.z, p.x, self.core_at].astype(F32)
        for k in range(1, p.Z):
            total = total + self.z_in[k - 1].astype(F32)
        self.out[...] = total


def swap_items(place, wires, src, dst):
    p = place
    block = src if callable(src) else lambda n: src.at[n]
    own = wires.move(block(p.i), dst.at[p.i])
    copies = []
    for k in range(1, p.I):
        other = lax.rem(p.i + k, p.I)
        copies.append(wires.push(block(other), dst.at[p.i], (other * p.R + p.r, p.t)))
    return own, copies


def swap_pairs(v):
    lane = lax.broadcasted_iota(jnp.int32, v.shape, 1)
    return jnp.where(lax.rem(lane, 2) == 0, pltpu.roll(v, 127, 1), pltpu.roll(v, 1, 1))


def head_split(v):
    lane = lax.broadcasted_iota(jnp.int32, v.shape, 1)
    zero = jnp.zeros_like(v)
    return jnp.where(lane < HEAD_DIM, v, zero), jnp.where(lane < HEAD_DIM, zero, v)


def first_lane(rows):
    lane = lax.broadcasted_iota(jnp.int32, (rows, 128), 1)
    return jnp.where(lane == 0, 1.0, 0.0).astype(BF)


def attend_block(rows, cb, xm, weight, cos_ref, sin_ref, mask_ref, q_ref, k_ref, v_ref, att_ref, lse_ref):
    q_lin = nn(xm[0:rows, :], weight(0))
    k_lin = nn(xm, weight(1))
    v_ref[...] = nn(xm, weight(2)).astype(BF)
    ones = first_lane(rows)
    factor = HEAD_DIM**-0.5
    for p in range(cb // 128):
        lanes = slice(p * 128, p * 128 + 128)
        q2, k2 = q_lin[:, lanes], k_lin[:, lanes]
        q2 = (q2 * cos_ref[0:rows, :] + swap_pairs(q2) * sin_ref[0:rows, :]).astype(BF)
        q2 = q2 * jnp.asarray(factor, BF)
        k2 = (k2 * cos_ref[...] + swap_pairs(k2) * sin_ref[...]).astype(BF)
        q_ref[:, lanes] = q2
        k_ref[:, lanes] = k2
        k_long = jnp.concatenate([k2, mask_ref[...]], axis=1)
        v_turned = v_ref[:, lanes].T
        outs = []
        for h, q1 in enumerate(head_split(q2)):
            scores = nt(k_long, jnp.concatenate([q1, ones], axis=1))
            highest = jnp.max(scores, axis=0, keepdims=True)
            unnormed = jnp.exp(scores - highest)
            total = jnp.sum(unnormed, axis=0, keepdims=True)
            probs = (unnormed * (1.0 / total)).astype(BF)
            lse_ref[pl.ds(2 * p + h, 1), :] = highest + jnp.log(total)
            outs.append(nn(v_turned[h * HEAD_DIM : (h + 1) * HEAD_DIM], probs))
        att_ref[:, lanes] = jnp.concatenate(outs, axis=0).T.astype(BF)
    return nt(att_ref[...], weight(3))


def own_columns(place, time, rs):
    silu = (time / (1.0 + jnp.exp(-time))).astype(BF)
    feature = lax.broadcasted_iota(jnp.int32, (D, rs), 0)
    chosen = feature == lax.broadcasted_iota(jnp.int32, (D, rs), 1) + place.s * rs
    return nn(silu, jnp.where(chosen, 1.0, 0.0).astype(BF)).astype(BF)


def fill_tables(place, fl, length, cos_ref, sin_ref, mask_ref, live_ref):
    p = place
    lane = lax.broadcasted_iota(jnp.int32, (fl, 128), 1)
    row = lax.broadcasted_iota(jnp.int32, (fl, 128), 0)
    column = lax.div(lax.rem(lane, HEAD_DIM), 2).astype(F32)
    inverse = jnp.exp(column * (-2.0 * math.log(10000.0) / HEAD_DIM))
    sign = jnp.where(lax.rem(lane, 2) == 0, -1.0, 1.0)
    for g in range(p.R):
        r = lax.rem(p.q + g // 2, p.Q) * 2 + lax.rem(p.c + g % 2, 2)
        for n in range(p.I):
            at = pl.ds((g * p.I + n) * fl, fl)
            pos = row + fl * (n * p.R + r)
            angles = pos.astype(F32) * inverse
            cos_ref[at, :] = jnp.cos(angles)
            sin_ref[at, :] = jnp.sin(angles) * sign
            alive = pos < length
            mask_ref[at, :] = jnp.where((lane == 0) & ~alive, NEGATIVE, 0.0).astype(BF)
            if g == 0:
                live_ref[at, :] = jnp.where(alive, 1.0, 0.0)[:, 0:1]


def front_kernel(
    S, T, I, cb, hb,
    frames, cotangent, time_ref, lengths_ref, wq_ref, wk_ref, wv_ref, wo_ref, wu_ref, wd_ref, wm_ref,
    all_a, xm_out, q_out, k_out, v_out, att_out, lse_out, grad_f, cos_out, sin_out, mask_out,
    frames_in, mod_ref, layer_ref, dmid_ref, dbranch_ref, dmod_ref,
    xm_ref, q_ref, k_ref, v_ref, att_ref, lse_ref, cos_ref, sin_ref, mask_ref,
    a_ref, f_ref, cot_in, parts, line_in, line_sum, parts_in, live_ref, branch_ref, mid_ref,
    normed_ref, mf_ref, mf_turned, db_ref, db_turned, out_sum, dmf_sum, stage,
    send, recv, local, row_send, row_recv, out_sem,
):
    p = Place(S, T, I)
    wires = Wires(send, recv, local)
    nq, nh = a_ref.shape[0], f_ref.shape[0]
    fl, rs = frames.shape[1], wq_ref.shape[0]
    rows, L = I * fl, I * fl * p.R
    micro, batch = lengths_ref.shape
    rows_own = I // micro
    for j in range(nq):
        cols = slice(j * cb, (j + 1) * cb)
        blocks = (wq_ref[:, cols], wk_ref[:, cols], wv_ref[:, cols], wo_ref[:, cols])
        a_ref[j, 0, p.z, p.x, p.c] = jnp.concatenate(blocks, axis=1)
    greet(p)
    chunks_a = [Gather(p, wires, a_ref.at[j], 2) for j in range(nq)]
    chunks_f = [Gather(p, wires, f_ref.at[j], 2) for j in range(nh)]
    chunks = chunks_a + chunks_f

    def upto(m, phase):
        if m < len(chunks):
            chunks[m].upto(phase)

    upto(0, 0)
    product = nn(own_columns(p, time_ref[...], rs), wm_ref[...])
    high = parts.shape[2]
    for item in range(micro * batch):
        m, b = divmod(item, batch)
        t, own = divmod(b, rows_own)
        for n in range(high):
            parts[t, m * rows_own + own, n : n + 1, :] = product[
                item : item + 1, n * 128 : (n + 1) * 128
            ]
    line = []
    for k in range(1, I):
        other = lax.rem(p.i + k, I)
        line.append(
            wires.push(parts.at[:, other], line_in.at[k - 1], (other * p.R + p.r, p.t))
        )
    for j in range(nh):
        cols = slice(j * hb, (j + 1) * hb)
        f_ref[j, 0, p.z, p.x, p.c] = jnp.concatenate([wu_ref[:, cols], wd_ref[:, cols]], axis=1)
    upto(0, 1)
    frames_own, frames_got = swap_items(p, wires, frames, frames_in)
    landed(line)
    for t in range(T):
        total = parts[t, p.i]
        for k in range(1, I):
            total = total + line_in[k - 1, t]
        line_sum[t] = total
    parts_in[p.t, p.r] = line_sum[p.t]
    group_done = spread_group(p, row_send, row_recv, lambda t: line_sum.at[t], parts_in)
    upto(0, 2)
    length = lengths_ref[lax.div(p.i, rows_own), p.t * rows_own + lax.rem(p.i, rows_own)]
    fill_tables(p, fl, length, cos_ref, sin_ref, mask_ref, live_ref)
    group_done()
    mod_ref[...] = jnp.zeros_like(mod_ref)
    for t in range(T):
        total = jnp.sum(parts_in[t], axis=0).astype(BF).astype(F32)
        for n in range(high):
            row, col = divmod((t * high + n) * 128, D)
            mod_ref[row : row + 1, col : col + 128] = total[n : n + 1]
    frames_own.wait()
    landed(frames_got)
    upto(1, 0)
    frame_rows = frames_in[...].reshape(rows, D).astype(F32)
    normed, _ = layer_stats(frame_rows)
    low = normed.astype(BF).astype(F32)
    xm_ref[0, 0] = (low * (1.0 + mod_ref[1:2, :]) + mod_ref[0:1, :]).astype(BF)
    sibling = p.group(0, 1 - p.c)
    across = [wires.push(xm_ref.at[0, 0], xm_ref.at[p.Q - k, 0], p.group(k)) for k in range(1, p.Q)]
    cores = [wires.push(xm_ref.at[0, 0], xm_ref.at[0, 1], sibling)]
    upto(0, 3)
    upto(1, 1)
    upto(2, 0)
    for k in range(1, p.Q):
        across[k - 1].wait_recv()
        cores.append(wires.push(xm_ref.at[p.Q - k, 0], xm_ref.at[p.Q - k, 1], sibling))
    upto(1, 2)
    upto(2, 1)
    upto(3, 0)
    landed(cores)

    cot_copies, steps = [], nq * T

    def ask_cotangent():
        own, got = swap_items(p, wires, cotangent, cot_in)
        cot_copies.extend([own, got])

    between = {
        0: lambda: (upto(1, 3), upto(2, 2), upto(3, 1), upto(4, 0)),
        1: lambda: (upto(2, 3), upto(3, 2), upto(4, 1), upto(5, 0)),
        2: lambda: (upto(3, 3), upto(4, 2), upto(5, 1), ask_cotangent()),
        3: lambda: (upto(4, 3), upto(5, 2)),
        steps: lambda: (upto(5, 3),),
    }
    if len(chunks) < 4:
        between = {}

    xm = xm_ref[...].reshape(L, D)
    copies = [
        wires.move(xm_ref, xm_out),
        wires.move(cos_ref, cos_out),
        wires.move(sin_ref, sin_out),
        wires.move(mask_ref, mask_out),
    ]
    for j in range(nq):
        chunks_a[j].upto(4)
        copies.append(wires.move(a_ref.at[j], all_a.at[j]))
        for t in range(T):
            n = j * T + t
            part = attend_block(
                rows, cb, xm,
                lambda b: a_ref[j, t, :, :, :, :, b * cb : (b + 1) * cb].reshape(D, cb),
                cos_ref, sin_ref, mask_ref,
                q_ref.at[n], k_ref.at[n], v_ref.at[n], att_ref.at[n], lse_ref.at[n],
            )
            if n == 0:
                branch_ref[...] = part
            else:
                branch_ref[...] += part
            between.get(n, tuple)()
    if not cot_copies:
        ask_cotangent()

    for src, dst in (
        (q_ref, q_out), (k_ref, k_out), (v_ref, v_out), (att_ref, att_out), (lse_ref, lse_out)
    ):
        copies.append(wires.move(src, dst))
    gate_attn, shift_ff = mod_ref[2:3, :], mod_ref[3:4, :]
    scale_ff, gate_ff = mod_ref[4:5, :], mod_ref[5:6, :]
    middle = (
        frames_in[...].reshape(rows, D).astype(F32)
        + gate_attn * live_ref[...] * branch_ref[...]
    )
    mid_ref[...] = middle
    normed, _ = layer_stats(middle)
    low = normed.astype(BF)
    normed_ref[...] = low
    modulated = (low.astype(F32) * (1.0 + scale_ff) + shift_ff).astype(BF)
    mf_ref[...] = modulated
    mf_turned[...] = modulated.T
    cot_copies[0].wait()
    landed(cot_copies[1])
    d_branch = (cot_in[...].reshape(rows, D).astype(F32) * gate_ff).astype(BF)
    db_ref[...] = d_branch
    db_turned[...] = d_branch.T

    pending = [None, None]
    for j in range(nh):
        chunks_f[j].upto(4)
        for t in range(T):
            n = j * T + t
            w_up = f_ref[j, t, :, :, :, :, 0:hb].reshape(D, hb)
            w_down = f_ref[j, t, :, :, :, :, hb : 2 * hb].reshape(D, hb)
            upper = nn(mf_ref[...], w_up)
            square = upper * upper
            slope = 0.7978845608
            tanh = jnp.tanh(slope * (upper + 0.044715 * upper * square))
            half = 0.5 * (1.0 + tanh)
            active = (upper * half).astype(BF)
            bend = half + 0.5 * upper * (1.0 - tanh * tanh) * (
                slope * (1.0 + 3 * 0.044715 * square)
            )
            d_upper = (nn(db_ref[...], w_down) * bend).astype(BF)
            if n == 0:
                out_sum[...] = nt(active, w_down)
                dmf_sum[...] = nt(d_upper, w_up)
            else:
                out_sum[...] += nt(active, w_down)
                dmf_sum[...] += nt(d_upper, w_up)
            slot = n % 2
            if pending[slot] is not None:
                pending[slot].wait()
            stage[slot, :, 0:hb] = nn(mf_turned[...], d_upper).astype(BF)
            stage[slot, :, hb : 2 * hb] = nn(db_turned[...], active).astype(BF)
            pending[slot] = pltpu.make_async_copy(stage.at[slot], grad_f.at[j, t], out_sem.at[slot])
            pending[slot].start()
            between.get(steps + n, tuple)()

    middle, branch_f = mid_ref[...], out_sum[...]
    layer_ref[...] = (middle + gate_ff * branch_f).astype(BF).reshape(layer_ref.shape)
    cot = cot_in[...].reshape(rows, D).astype(F32)
    normed, inverse = layer_stats(middle)
    dmf = dmf_sum[...]
    d_mid = cot + layer_back(normed, inverse, dmf * (1.0 + scale_ff))
    dmid_ref[...] = d_mid
    alive = d_mid * live_ref[...]
    dbranch_ref[...] = (alive * gate_attn).astype(BF)
    dmod_ref[...] = jnp.zeros_like(dmod_ref)
    dmod_ref[2:3, :] = jnp.sum(alive * branch_ref[...], axis=0, keepdims=True)
    dmod_ref[3:4, :] = jnp.sum(dmf, axis=0, keepdims=True)
    dmod_ref[4:5, :] = jnp.sum(dmf * normed_ref[...].astype(F32), axis=0, keepdims=True)
    dmod_ref[5:6, :] = jnp.sum(cot * branch_f, axis=0, keepdims=True)
    for copy in copies + [c for c in pending if c is not None]:
        copy.wait()
    wires.close()


def front_call(S, T, I, cb, hb, frames, cotangent, time, lengths, weights):
    w_query, w_up, w_mod = weights[0], weights[4], weights[6]
    rs = w_query.shape[0]
    nq, wide_a = w_query.shape[1] // cb, 4 * cb
    nh, wide_f = w_up.shape[1] // hb, 2 * hb
    fl = frames.shape[1]
    rows, Z, R = I * fl, S // 4, S // I
    Q, L, steps = R // 2, rows * R, nq * T
    high = w_mod.shape[1] // 128
    remote = 3 * (I - 1) + (nq + nh) * (Z + 2 * T + 4) + 2 * Q
    shape = jax.ShapeDtypeStruct
    vmem, dma = pltpu.VMEM, pltpu.SemaphoreType.DMA
    kept = [
        ((Q, 2, rows, D), BF),
        ((steps, rows, cb), BF),
        ((steps, L, cb), BF),
        ((steps, L, cb), BF),
        ((steps, rows, cb), BF),
        ((steps, 8, rows), F32),
        ((L, 128), F32),
        ((L, 128), F32),
        ((L, 128), BF),
    ]
    return pl.pallas_call(
        partial(front_kernel, S, T, I, cb, hb),
        out_shape=tuple(shape(*x) for x in [((nq, T, Z, 2, 2, rs, wide_a), BF)] + kept[:6])
        + (shape((nh, T, D, wide_f), BF),)
        + tuple(shape(*x) for x in kept[6:])
        + (
            shape(frames.shape, BF),
            shape((8, D), F32),
            shape(frames.shape, BF),
            shape((rows, D), F32),
            shape((rows, D), BF),
            shape((8, D), F32),
        ),
        in_specs=[ANY] * 2 + [VMEM, pl.BlockSpec(memory_space=pltpu.SMEM)] + [VMEM] * 7,
        out_specs=(ANY,) * 11 + (VMEM,) * 6,
        scratch_shapes=[vmem(*x) for x in kept]
        + [
            vmem((nq, T, Z, 2, 2, rs, wide_a), BF),
            vmem((nh, T, Z, 2, 2, rs, wide_f), BF),
            vmem(frames.shape, BF),
            vmem((T, I, high, 128), F32),
            vmem((I - 1, T, high, 128), F32),
            vmem((T, high, 128), F32),
            vmem((T, R, high, 128), F32),
            vmem((rows, 1), F32),
            vmem((rows, D), F32),
            vmem((rows, D), F32),
            vmem((rows, D), BF),
            vmem((rows, D), BF),
            vmem((D, rows), BF),
            vmem((rows, D), BF),
            vmem((D, rows), BF),
            vmem((rows, D), F32),
            vmem((rows, D), F32),
            vmem((2, D, wide_f), BF),
            dma((remote,)),
            dma((remote,)),
            dma((11 + nq,)),
            dma((R * T,)),
            dma((R * T,)),
            dma((2,)),
        ],
        compiler_params=pltpu.CompilerParams(
            collective_id=0, has_side_effects=True, vmem_limit_bytes=LIMIT
        ),
        name="forward",
    )(frames, cotangent, time, lengths, *weights)


def attend_back_block(
    rows, cb, weight, wide, db_ref, xm_turned, db_turned, cos_ref, sin_ref, mask_ref,
    q_ref, k_ref, v_ref, att_ref, lse_ref, store,
):
    d_att = nn(db_ref[...], weight(3)).astype(BF)
    store(3, nn(db_turned[...], att_ref[...]))
    ones = first_lane(rows)
    factor = HEAD_DIM**-0.5
    dqs, dks, dvs = [], [], []
    for p in range(cb // 128):
        lanes = slice(p * 128, p * 128 + 128)
        q2, k2, v2 = q_ref[:, lanes], k_ref[:, lanes], v_ref[:, lanes]
        k_long = jnp.concatenate([k2, mask_ref[...]], axis=1)
        k_turned = k2.T
        dq_parts, ds_all, p_all = [], [], []
        q_heads, d_heads = head_split(q2), head_split(d_att[:, lanes])
        for h in range(2):
            scores = nt(k_long, jnp.concatenate([q_heads[h], ones], axis=1))
            probs = jnp.exp(scores - lse_ref[pl.ds(2 * p + h, 1), :])
            d_probs = nt(v2, d_heads[h])
            row_dot = jnp.sum(probs * d_probs, axis=0, keepdims=True)
            d_scores = (probs * (d_probs - row_dot)).astype(BF)
            dq_parts.append(nn(k_turned[h * HEAD_DIM : (h + 1) * HEAD_DIM], d_scores))
            ds_all.append(d_scores)
            p_all.append(probs.astype(BF))
        dk2 = nn(jnp.concatenate(ds_all, axis=1), jnp.concatenate(q_heads, axis=0))
        dv2 = nn(jnp.concatenate(p_all, axis=1), jnp.concatenate(d_heads, axis=0))
        dq2 = jnp.concatenate(dq_parts, axis=0).T * factor
        dqs.append(
            (dq2 * cos_ref[0:rows, :] - swap_pairs(dq2) * sin_ref[0:rows, :]).astype(BF)
        )
        dks.append((dk2 * cos_ref[...] - swap_pairs(dk2) * sin_ref[...]).astype(BF))
        dvs.append(dv2.astype(BF))
    dq, dk, dv = (jnp.concatenate(v, axis=1) for v in (dqs, dks, dvs))
    store(0, nn(xm_turned[:, 0:rows], dq))
    store(1, nn(xm_turned[...], dk))
    store(2, nn(xm_turned[...], dv))
    return nt(jnp.concatenate([dk, dv], axis=1), wide(1, 3)), nt(dq, weight(0))


def back_kernel(
    S, T, I, cb,
    layer, all_a, grad_f, k_all, v_all, xm_all, dmid, frames,
    q_ref, att_ref, lse_ref, mod_ref, db_ref, dmod_ref,
    cos_ref, sin_ref, mask_ref,
    layer_out, grads_out, rows_out, sum_a, sum_f,
    *scratch,
):
    nh, nq = grad_f.shape[0], all_a.shape[0]
    (xm_turned, db_turned, dx_sum, dx_ref, near, far, d_rows, group_in, group_sum, ga_ref,
     w_stage, k_stage, v_stage, in_sem, send, recv, local, row_send, row_recv) = scratch[:19]
    rest = scratch[19:]
    p = Place(S, T, I)
    wires = Wires(send, recv, local)
    Q, _, rows, _ = xm_all.shape
    L = Q * 2 * rows
    steps, slots = nq * T, w_stage.shape[0]

    def fetch(n):
        j, t = divmod(n, T)
        slot = n % slots
        copies = [
            pltpu.make_async_copy(all_a.at[j, t], w_stage.at[slot], in_sem.at[0, slot]),
            pltpu.make_async_copy(k_all.at[n], k_stage.at[slot], in_sem.at[1, slot]),
            pltpu.make_async_copy(v_all.at[n], v_stage.at[slot], in_sem.at[2, slot]),
        ]
        for copy in copies:
            copy.start()
        return copies

    xm_copy = wires.move(xm_all, dx_ref)
    fetched = fetch(0)
    greet(p)
    chunks_f, chunks_a = [], []
    for j in range(nh):
        own, landing, rest = rest[0], rest[1:7], rest[7:]
        chunks_f.append(Reduce(p, wires, grad_f.at[j], sum_f.at[j], own, 0, 2, landing))
    for j in range(nq):
        for h in (1, 0):
            landing, rest = rest[:6], rest[6:]
            cols = pl.ds(2 * cb * h, 2 * cb)
            g = ga_ref.at[j, :, :, :, :, :, cols]
            chunks_a.append(Reduce(p, wires, g, sum_a.at[j, :, cols], g, p.c, 2, landing))
    chunks = chunks_f + chunks_a

    def upto(m, phase):
        if m < len(chunks):
            chunks[m].upto(phase)

    upto(0, 0)
    if nh > 1:
        upto(1, 0)
    xm_copy.wait()
    db_turned[...] = db_ref[...].T
    upto(0, 1)
    for m in range(2, nh):
        upto(m, 0)
    xm_turned[...] = dx_ref[...].reshape(L, D).T
    for m in range(1, nh):
        upto(m, 1)
    layer_own, layer_in = swap_items(p, wires, layer, layer_out)

    between = {}
    if nq == 2 and T == 2 and nh == 4:
        between = {
            0: lambda: (upto(0, 2), upto(1, 2)),
            1: lambda: (upto(4, 0), upto(5, 0), upto(2, 2), upto(3, 2), upto(4, 1), upto(5, 1)),
            2: lambda: (upto(0, 3), upto(1, 3), upto(2, 3), upto(3, 3)),
        }

    for n in range(steps):
        j, t = divmod(n, T)
        slot = n % slots
        coming = fetch(n + 1) if slots == 2 and n + 1 < steps else None
        for copy in fetched:
            copy.wait()
        fetched = coming

        def store(b, value):
            ga_ref[j, t, :, :, :, :, b * cb : (b + 1) * cb] = value.astype(BF).reshape(
                ga_ref.shape[2:6] + (cb,)
            )

        dx, dx_own = attend_back_block(
            rows, cb,
            lambda b: w_stage[slot, :, b * cb : (b + 1) * cb],
            lambda b, e: w_stage[slot, :, b * cb : e * cb],
            db_ref, xm_turned, db_turned, cos_ref, sin_ref, mask_ref,
            q_ref.at[n], k_stage.at[slot], v_stage.at[slot], att_ref.at[n], lse_ref.at[n], store,
        )
        if n == 0:
            dx_sum[...] = dx
        else:
            dx_sum[...] += dx
        dx_sum[0:rows, :] += dx_own
        if slots == 1 and n + 1 < steps:
            fetched = fetch(n + 1)
        if n < steps - 1:
            between.get(n, tuple)()

    dx_ref[...] = dx_sum[...].astype(BF).reshape(dx_ref.shape)
    dmid_copy = wires.move(dmid, dx_sum.at[pl.ds(rows, rows)])
    fl = layer.shape[1]
    frame_copies = [
        wires.move(frames.at[n], xm_turned.at[pl.ds(n * fl, fl), pl.ds(0, D)]) for n in range(I)
    ]
    core = wires.push(dx_ref.at[:, 1], near, p.group(0, 1 - p.c))
    last = len(chunks) - 1
    upto(last - 1, 0)
    upto(last, 0)
    core.wait_recv()
    across = []
    for k in range(1, Q):
        dx_ref[k, 0] = dx_ref[k, 0] + near[k]
        across.append(wires.push(dx_ref.at[k, 0], far.at[k - 1], p.group(k)))
    for m in range(last - 1):
        upto(m, 2)
    upto(last - 1, 1)
    upto(last, 1)
    for m in range(nh):
        upto(m, 3)

    for copy in frame_copies:
        copy.wait()
    normed, inverse = layer_stats(xm_turned[0:rows, 0:D].astype(F32))
    d_mod = dx_sum[0:rows, :] + near[0].astype(F32)
    for k in range(1, Q):
        across[k - 1].wait_recv()
        d_mod = d_mod + far[k - 1].astype(F32)
    incoming = layer_back(normed, inverse, d_mod * (1.0 + mod_ref[1:2, :]))
    dmid_copy.wait()
    dx_ref[0, 0] = (dx_sum[rows : 2 * rows, :] + incoming).astype(BF)
    grads_own, grads_in = swap_items(
        p, wires, lambda n: dx_ref.at[0, 0, pl.ds(n * fl, fl)], grads_out
    )
    high = d_rows.shape[1]
    first = [
        jnp.sum(d_mod, axis=0, keepdims=True),
        jnp.sum(d_mod * normed.astype(BF).astype(F32), axis=0, keepdims=True),
    ]
    for t in range(T):
        for n in range(high):
            row, col = divmod((t * high + n) * 128, D)
            value = first[row] if row < 2 else dmod_ref[row : row + 1, :]
            d_rows[t, n : n + 1, :] = value[:, col : col + 128]
    group_in[p.t, p.r] = d_rows[p.t]
    group_done = spread_group(p, row_send, row_recv, lambda t: d_rows.at[t], group_in)
    for m in range(last - 1):
        upto(m, 3)
    group_done()
    for t in range(T):
        group_sum[t] = jnp.sum(group_in[t], axis=0)
    rows_own = wires.move(group_sum, rows_out.at[p.i])
    line = []
    for k in range(1, I):
        other = lax.rem(p.i + k, I)
        line.append(wires.push(group_sum, rows_out.at[p.i], (other * p.R + p.r, p.t)))
    upto(last - 1, 2)
    upto(last, 2)
    for m in range(nh):
        upto(m, 4)
    upto(last - 1, 3)
    upto(last, 3)
    for m in range(last + 1):
        upto(m, 4)
    landed(line)
    for own in (grads_own, layer_own, rows_own):
        own.wait()
    landed(grads_in)
    landed(layer_in)
    wires.close()


def back_call(
    S, T, I, cb, layer, all_a, grad_f, k, v, xm, d_mid, frames,
    q, att, lse, mod, d_branch, d_mod, cosine, sine, mask,
):
    nq, ca = all_a.shape[0], all_a.shape[3]
    nh, cf = grad_f.shape[0], grad_f.shape[6]
    rs = grad_f.shape[5]
    Z, Q, rows = S // 4, xm.shape[0], xm.shape[2]
    L = Q * 2 * rows
    high = 6 * D // T // 128
    slots = 2 if L <= 1024 else 1
    remote = 3 * (I - 1) + (2 * nq + nh) * (Z + 2 * T + 2) + Q
    R = S // I
    shape = jax.ShapeDtypeStruct
    dma = pltpu.SemaphoreType.DMA
    scratch = [
        pltpu.VMEM((D, L), BF),
        pltpu.VMEM((D, rows), BF),
        pltpu.VMEM((L, D), F32),
        pltpu.VMEM((Q, 2, rows, D), BF),
        pltpu.VMEM((Q, rows, D), BF),
        pltpu.VMEM((Q - 1, rows, D), BF),
        pltpu.VMEM((T, high, 128), F32),
        pltpu.VMEM((T, R, high, 128), F32),
        pltpu.VMEM((T, high, 128), F32),
        pltpu.VMEM((nq, T, Z, 2, 2, rs, ca), BF),
        pltpu.VMEM((slots, D, ca), BF),
        pltpu.VMEM((slots, L, cb), BF),
        pltpu.VMEM((slots, L, cb), BF),
        dma((3, slots)),
        dma((remote,)),
        dma((remote,)),
        dma((5 + nh + I,)),
        dma((R * T,)),
        dma((R * T,)),
    ]
    for _ in range(nh):
        scratch += [pltpu.VMEM((T, Z, 2, 1, rs, cf), BF)] + Reduce.landing(T, Z, rs, cf, 2)
    for _ in range(2 * nq):
        scratch += Reduce.landing(T, Z, rs, ca // 2, 2)
    return pl.pallas_call(
        partial(back_kernel, S, T, I, cb),
        out_shape=(
            shape(layer.shape, BF),
            shape(layer.shape, BF),
            shape((I, T, high, 128), F32),
            shape((nq, rs, ca), F32),
            shape((nh, rs, cf), F32),
        ),
        in_specs=[ANY] * 8 + [VMEM] * 9,
        out_specs=(ANY, ANY, ANY, VMEM, VMEM),
        scratch_shapes=scratch,
        compiler_params=pltpu.CompilerParams(
            collective_id=1, has_side_effects=True, vmem_limit_bytes=LIMIT
        ),
        name="backward",
    )(
        layer, all_a, grad_f, k, v, xm, d_mid, frames,
        q, att, lse, mod, d_branch, d_mod, cosine, sine, mask,
    )


def layer_stats(values):
    center = values - jnp.mean(values, axis=-1, keepdims=True)
    inverse = lax.rsqrt(jnp.mean(center * center, axis=-1, keepdims=True) + EPSILON)
    return center * inverse, inverse


def layer_back(normed, inverse, incoming):
    return inverse * (
        incoming
        - jnp.mean(incoming, axis=-1, keepdims=True)
        - normed * jnp.mean(incoming * normed, axis=-1, keepdims=True)
    )


def finish_kernel(
    S, T, I, micro, time_ref, rows_ref, sum_a, sum_f, layer_in, grads_in,
    layer_ref, grads_ref, gq_ref, gk_ref, gv_ref, go_ref, gu_ref, gd_ref, gm_ref, items_ref,
):
    p = Place(S, T, I)
    nq, rs, wide_a = sum_a.shape
    nh, _, wide_f = sum_f.shape
    cb, hb = wide_a // 4, wide_f // 2
    layer_ref[...] = layer_in[...]
    grads_ref[...] = grads_in[...]
    for j in range(nq):
        for b, ref in enumerate((gq_ref, gk_ref, gv_ref, go_ref)):
            ref[:, j * cb : (j + 1) * cb] = sum_a[j, :, b * cb : (b + 1) * cb]
    for j in range(nh):
        gu_ref[:, j * hb : (j + 1) * hb] = sum_f[j, :, 0:hb]
        gd_ref[:, j * hb : (j + 1) * hb] = sum_f[j, :, hb : 2 * hb]
    high = rows_ref.shape[2]
    rows_own = I // micro
    for item in range(I * T):
        m, b = divmod(item, rows_own * T)
        i, t = m * rows_own + b % rows_own, b // rows_own
        for n in range(high):
            items_ref[item : item + 1, n * 128 : (n + 1) * 128] = rows_ref[i, t, n : n + 1, :]
    silu = own_columns(p, time_ref[...], rs).astype(F32)
    gm_ref[...] = lax.dot_general(
        silu, items_ref[...], (((0,), (0,)), ((), ())), precision=HIGHEST,
        preferred_element_type=F32,
    )


def finish_call(S, T, I, micro, time, rows, sum_a, sum_f, layer, grads, weights):
    shape = jax.ShapeDtypeStruct
    return pl.pallas_call(
        partial(finish_kernel, S, T, I, micro),
        out_shape=(shape(layer.shape, BF), shape(grads.shape, BF))
        + tuple(shape(w.shape, F32) for w in weights),
        in_specs=[VMEM] * 6,
        out_specs=(VMEM,) * 9,
        scratch_shapes=[pltpu.VMEM((I * T, weights[6].shape[1]), F32)],
        compiler_params=pltpu.CompilerParams(vmem_limit_bytes=LIMIT),
        name="finish",
    )(time, rows, sum_a, sum_f, layer, grads)


def per_device(
    S, T, frames, time_embed, lengths, w_query, w_key, w_value, w_out, w_up, w_down, w_mod, out_grad
):
    micro, rows_own, fl, _ = frames.shape
    batch = lengths.shape[1]
    I = micro * rows_own
    rs = w_query.shape[0]
    cb = min(256, w_query.shape[1])
    hb = min(256, w_up.shape[1])
    time = time_embed.reshape(micro * batch, D)
    weights = (w_query, w_key, w_value, w_out.T, w_up, w_down.T, w_mod)
    (
        all_a, xm, q, k, v, att, lse, grad_f, cosine, sine, mask,
        frames_in, mod, layer, d_mid, d_branch, d_rows,
    ) = front_call(
        S, T, I, cb, hb, frames.reshape(I, fl, D), out_grad.reshape(I, fl, D), time, lengths, weights
    )
    layer_out, grad_input, rows_in, sum_a, sum_f = back_call(
        S, T, I, cb, layer, all_a.reshape(all_a.shape[:2] + (D, 4 * cb)),
        grad_f.reshape((grad_f.shape[0], T, S // 4, 2, 2, rs, 2 * hb)), k, v, xm, d_mid,
        frames_in, q, att, lse, mod, d_branch, d_rows, cosine, sine, mask,
    )
    outs = finish_call(S, T, I, micro, time, rows_in, sum_a, sum_f, layer_out, grad_input, weights)
    layer_out, grad_input, g_query, g_key, g_value, g_out, g_up, g_down, g_mod = outs
    return (
        layer_out.reshape(frames.shape), grad_input.reshape(frames.shape),
        g_query, g_key, g_value, g_out.T, g_up, g_down.T, g_mod,
    )


def solution(mesh):
    S, T = mesh.shape["seq"], mesh.shape["tp"]
    rows = P(None, "tp", "seq", None)
    return jax.shard_map(
        partial(per_device, S, T),
        mesh=mesh,
        in_specs=(
            rows,
            P(),
            P(),
            P("seq", "tp"),
            P("seq", "tp"),
            P("seq", "tp"),
            P("tp", "seq"),
            P("seq", "tp"),
            P("tp", "seq"),
            P("seq", "tp"),
            rows,
        ),
        out_specs=(
            rows,
            rows,
            P("seq", "tp"),
            P("seq", "tp"),
            P("seq", "tp"),
            P("tp", "seq"),
            P("seq", "tp"),
            P("tp", "seq"),
            P("seq", "tp"),
        ),
        check_vma=False,
    )
```

```python
from functools import partial
import math

import jax
import jax.numpy as jnp
from jax import lax
from jax.experimental import pallas as pl
from jax.experimental.pallas import tpu as pltpu
from jax.sharding import PartitionSpec as P

D = 1024
HEAD_DIM = 64
EPSILON = 1e-06
NEGATIVE = -1e30
BF = jnp.bfloat16
F32 = jnp.float32
HIGHEST = lax.Precision.HIGHEST
MESH = pl.DeviceIdType.MESH
ANY = pl.BlockSpec(memory_space=pl.ANY)
VMEM = pl.BlockSpec(memory_space=pltpu.VMEM)
LIMIT = 62 * 1024 * 1024


def nn(a, b):
    return lax.dot_general(a, b, (((1,), (0,)), ((), ())), preferred_element_type=F32)


def nt(a, b):
    return lax.dot_general(a, b, (((1,), (1,)), ((), ())), preferred_element_type=F32)


class Place:
    def __init__(self, S, T, I):
        self.S, self.T, self.I = S, T, I
        self.Z, self.R = S // 4, S // I
        self.Q = self.R // 2
        self.s, self.t = lax.axis_index("seq"), lax.axis_index("tp")
        self.z = lax.div(self.s, 4)
        self.x = lax.rem(lax.div(self.s, 2), 2)
        self.c = lax.rem(self.s, 2)
        self.i = lax.div(self.s, self.R)
        self.r = lax.rem(self.s, self.R)
        self.q = lax.div(self.r, 2)

    def at(self, z=None, x=None, c=None, t=None):
        z = self.z if z is None else z
        x = self.x if x is None else x
        c = self.c if c is None else c
        t = self.t if t is None else t
        return ((z * 2 + x) * 2 + c, t)

    def tp(self, k):
        return (self.s, lax.rem(self.t + k, self.T))

    def zs(self, k):
        return lax.rem(self.z + k, self.Z)

    def group(self, k, c=None):
        c = self.c if c is None else c
        return (self.i * self.R + lax.rem(self.q + k, self.Q) * 2 + c, self.t)


class Wires:
    def __init__(self, send, recv, local):
        self.send, self.recv, self.local = send, recv, local
        self.remote_count = self.local_count = 0
        self.sent = []

    def push(self, src, dst, device):
        n = self.remote_count
        self.remote_count += 1
        copy = pltpu.make_async_remote_copy(
            src_ref=src,
            dst_ref=dst,
            send_sem=self.send.at[n],
            recv_sem=self.recv.at[n],
            device_id=device,
            device_id_type=MESH,
        )
        copy.start()
        self.sent.append(copy)
        return copy

    def move(self, src, dst):
        n = self.local_count
        self.local_count += 1
        copy = pltpu.make_async_copy(src, dst, self.local.at[n])
        copy.start()
        return copy

    def close(self):
        for copy in self.sent:
            copy.wait_send()


def landed(copies):
    for copy in copies:
        copy.wait_recv()


def loop_group(place, first, body):
    total = place.R * place.T
    me = place.r * place.T + place.t

    def step(d, carry):
        other = lax.rem(me + d, total)
        body(d, place.i * place.R + lax.div(other, place.T), lax.rem(other, place.T))
        return carry

    lax.fori_loop(first, total, step, 0)


def greet(place):
    barrier = pltpu.get_barrier_semaphore()

    def signal(d, s, t):
        pl.semaphore_signal(barrier, inc=1, device_id=(s, t), device_id_type=MESH)

    for k in range(1, place.Z):
        signal(k, *place.at(z=place.zs(k)))
    loop_group(place, 1, signal)
    pl.semaphore_wait(barrier, place.Z - 1 + place.R * place.T - 1)


def spread_group(place, send, recv, src_of, dst):
    def copy(d, s, t):
        return pltpu.make_async_remote_copy(
            src_ref=src_of(t),
            dst_ref=dst.at[place.t, place.r],
            send_sem=send.at[d],
            recv_sem=recv.at[d],
            device_id=(s, t),
            device_id_type=MESH,
        )

    loop_group(place, 1, lambda d, s, t: copy(d, s, t).start())
    return lambda: loop_group(place, 1, lambda d, s, t: copy(d, s, t).wait())


class Phased:
    done = 0

    def upto(self, phase):
        while self.done <= phase:
            getattr(self, f"phase{self.done}")()
            self.done += 1


def split_rows(rs, quarters):
    upper = rs * quarters // 4 if rs * quarters // 4 % 16 == 0 else rs // 2
    return pl.ds(0, upper), pl.ds(upper, rs - upper)


class Gather(Phased):
    def __init__(self, place, wires, dst, quarters):
        self.p, self.w, self.dst = place, wires, dst
        self.upper, self.lower = split_rows(dst.shape[4], quarters)

    def phase0(self):
        p, w, dst = self.p, self.w, self.dst
        own = dst.at[0, p.z, p.x, p.c]
        self.along = [w.push(own, own, p.at(z=p.zs(k))) for k in range(1, p.Z)]

    def phase1(self):
        p, w, dst = self.p, self.w, self.dst
        landed(self.along)
        line = dst.at[0, :, p.x, p.c]
        self.sides = [
            w.push(
                dst.at[0, :, p.x, p.c, self.upper],
                dst.at[0, :, p.x, p.c, self.upper],
                p.at(x=1 - p.x),
            )
        ]
        for k in range(1, p.T):
            self.sides.append(
                w.push(
                    dst.at[0, :, p.x, p.c, self.lower],
                    dst.at[p.T - k, :, p.x, p.c, self.lower],
                    p.tp(k),
                )
            )
        self.cores = [w.push(line, line, p.at(c=1 - p.c))]

    def phase2(self):
        p, w, dst = self.p, self.w, self.dst
        landed(self.sides)
        self.last = []
        for k in range(1, p.T):
            self.last.append(
                w.push(
                    dst.at[0, :, :, p.c, self.upper],
                    dst.at[p.T - k, :, :, p.c, self.upper],
                    p.tp(k),
                )
            )
        part = dst.at[:, :, p.x, p.c, self.lower]
        self.last.append(w.push(part, part, p.at(x=1 - p.x)))
        part = dst.at[0, :, 1 - p.x, p.c, self.upper]
        self.cores.append(w.push(part, part, p.at(c=1 - p.c)))
        part = dst.at[pl.ds(1, p.T - 1), :, p.x, p.c, self.lower]
        self.cores.append(w.push(part, part, p.at(c=1 - p.c)))

    def phase3(self):
        p, w, dst = self.p, self.w, self.dst
        landed(self.last)
        part = dst.at[pl.ds(1, p.T - 1), :, :, p.c, self.upper]
        self.cores.append(w.push(part, part, p.at(c=1 - p.c)))
        part = dst.at[:, :, 1 - p.x, p.c, self.lower]
        self.cores.append(w.push(part, part, p.at(c=1 - p.c)))

    def phase4(self):
        landed(self.cores)


class Reduce(Phased):
    def __init__(self, place, wires, src, out, own, core_at, quarters, landing):
        self.p, self.w, self.src, self.out = place, wires, src, out
        self.own, self.core_at = own, core_at
        self.core, self.y_up, self.x_low, self.x_up, self.y_low, self.z_in = landing
        self.upper, self.lower = split_rows(own.shape[4], quarters)

    @staticmethod
    def landing(T, Z, rs, C, quarters):
        upper, lower = (part.size for part in split_rows(rs, quarters))
        return [
            pltpu.VMEM((T, Z, 2, rs, C), BF),
            pltpu.VMEM((T - 1, Z, 2, upper, C), BF),
            pltpu.VMEM((T, Z, lower, C), BF),
            pltpu.VMEM((Z, upper, C), BF),
            pltpu.VMEM((T - 1, Z, lower, C), BF),
            pltpu.VMEM((Z - 1, rs, C), BF),
        ]

    def phase0(self):
        p, w, src = self.p, self.w, self.src
        self.mine = None
        if self.own is not src:
            self.mine = w.move(src.at[:, :, :, pl.ds(p.c, 1)], self.own)
        self.pair = [w.push(src.at[:, :, :, 1 - p.c], self.core, p.at(c=1 - p.c))]

    def phase1(self):
        p, w, own, c = self.p, self.w, self.own, self.core_at
        if self.mine is not None:
            self.mine.wait()
        landed(self.pair)

        def add(n, carry):
            k, z = lax.div(n, p.Z), lax.rem(n, p.Z)
            for x in range(2):
                own[k, z, x, c] = own[k, z, x, c] + self.core[k, z, x]
            return carry

        lax.fori_loop(0, p.T * p.Z, add, 0)
        self.sides = [
            w.push(own.at[k, :, :, c, self.upper], self.y_up.at[k - 1], p.tp(k))
            for k in range(1, p.T)
        ]
        self.sides.append(
            w.push(own.at[:, :, 1 - p.x, c, self.lower], self.x_low, p.at(x=1 - p.x))
        )

    def phase2(self):
        p, w, own, c = self.p, self.w, self.own, self.core_at
        landed(self.sides)

        def add(z, carry):
            for x in range(2):
                total = own[0, z, x, c, self.upper].astype(F32)
                for k in range(1, p.T):
                    total = total + self.y_up[k - 1, z, x].astype(F32)
                own[0, z, x, c, self.upper] = total.astype(BF)
            for k in range(p.T):
                own[k, z, p.x, c, self.lower] = own[k, z, p.x, c, self.lower] + self.x_low[k, z]
            return carry

        lax.fori_loop(0, p.Z, add, 0)
        self.last = [w.push(own.at[0, :, 1 - p.x, c, self.upper], self.x_up, p.at(x=1 - p.x))]
        for k in range(1, p.T):
            self.last.append(
                w.push(own.at[k, :, p.x, c, self.lower], self.y_low.at[k - 1], p.tp(k))
            )

    def phase3(self):
        p, w, own, c = self.p, self.w, self.own, self.core_at
        landed(self.last)

        def add(z, carry):
            own[0, z, p.x, c, self.upper] = own[0, z, p.x, c, self.upper] + self.x_up[z]
            total = own[0, z, p.x, c, self.lower].astype(F32)
            for k in range(1, p.T):
                total = total + self.y_low[k - 1, z].astype(F32)
            own[0, z, p.x, c, self.lower] = total.astype(BF)
            return carry

        lax.fori_loop(0, p.Z, add, 0)
        self.along = [
            w.push(own.at[0, p.zs(k), p.x, c], self.z_in.at[k - 1], p.at(z=p.zs(k)))
            for k in range(1, p.Z)
        ]

    def phase4(self):
        p = self.p
        landed(self.along)
        total = self.own[0, p.z, p.x, self.core_at].astype(F32)
        for k in range(1, p.Z):
            total = total + self.z_in[k - 1].astype(F32)
        self.out[...] = total


def swap_items(place, wires, src, dst):
    p = place
    block = src if callable(src) else lambda n: src.at[n]
    own = wires.move(block(p.i), dst.at[p.i])
    copies = []
    for k in range(1, p.I):
        other = lax.rem(p.i + k, p.I)
        copies.append(wires.push(block(other), dst.at[p.i], (other * p.R + p.r, p.t)))
    return own, copies


def swap_pairs(v):
    lane = lax.broadcasted_iota(jnp.int32, v.shape, 1)
    return jnp.where(lax.rem(lane, 2) == 0, pltpu.roll(v, 127, 1), pltpu.roll(v, 1, 1))


def head_split(v):
    lane = lax.broadcasted_iota(jnp.int32, v.shape, 1)
    zero = jnp.zeros_like(v)
    return jnp.where(lane < HEAD_DIM, v, zero), jnp.where(lane < HEAD_DIM, zero, v)


def first_lane(rows):
    lane = lax.broadcasted_iota(jnp.int32, (rows, 128), 1)
    return jnp.where(lane == 0, 1.0, 0.0).astype(BF)


def attend_block(rows, cb, xm, weight, cos_ref, sin_ref, mask_ref, q_ref, k_ref, v_ref, att_ref, lse_ref):
    q_lin = nn(xm[0:rows, :], weight(0))
    k_lin = nn(xm, weight(1))
    v_ref[...] = nn(xm, weight(2)).astype(BF)
    ones = first_lane(rows)
    factor = HEAD_DIM**-0.5
    for p in range(cb // 128):
        lanes = slice(p * 128, p * 128 + 128)
        q2, k2 = q_lin[:, lanes], k_lin[:, lanes]
        q2 = (q2 * cos_ref[0:rows, :] + swap_pairs(q2) * sin_ref[0:rows, :]).astype(BF)
        q2 = q2 * jnp.asarray(factor, BF)
        k2 = (k2 * cos_ref[...] + swap_pairs(k2) * sin_ref[...]).astype(BF)
        q_ref[:, lanes] = q2
        k_ref[:, lanes] = k2
        k_long = jnp.concatenate([k2, mask_ref[...]], axis=1)
        v_turned = v_ref[:, lanes].T
        outs = []
        for h, q1 in enumerate(head_split(q2)):
            scores = nt(k_long, jnp.concatenate([q1, ones], axis=1))
            highest = jnp.max(scores, axis=0, keepdims=True)
            unnormed = jnp.exp(scores - highest)
            total = jnp.sum(unnormed, axis=0, keepdims=True)
            probs = (unnormed * (1.0 / total)).astype(BF)
            lse_ref[pl.ds(2 * p + h, 1), :] = highest + jnp.log(total)
            outs.append(nn(v_turned[h * HEAD_DIM : (h + 1) * HEAD_DIM], probs))
        att_ref[:, lanes] = jnp.concatenate(outs, axis=0).T.astype(BF)
    return nt(att_ref[...], weight(3))


def own_columns(place, time, rs):
    time = jnp.concatenate([time[m] for m in range(time.shape[0])], axis=0)
    silu = (time / (1.0 + jnp.exp(-time))).astype(BF)
    feature = lax.broadcasted_iota(jnp.int32, (D, rs), 0)
    chosen = feature == lax.broadcasted_iota(jnp.int32, (D, rs), 1) + place.s * rs
    return nn(silu, jnp.where(chosen, 1.0, 0.0).astype(BF)).astype(BF)


def fill_tables(place, fl, length, cos_ref, sin_ref, mask_ref, live_ref):
    p = place
    lane = lax.broadcasted_iota(jnp.int32, (fl, 128), 1)
    row = lax.broadcasted_iota(jnp.int32, (fl, 128), 0)
    column = lax.div(lax.rem(lane, HEAD_DIM), 2).astype(F32)
    inverse = jnp.exp(column * (-2.0 * math.log(10000.0) / HEAD_DIM))
    sign = jnp.where(lax.rem(lane, 2) == 0, -1.0, 1.0)
    for g in range(p.R):
        r = lax.rem(p.q + g // 2, p.Q) * 2 + lax.rem(p.c + g % 2, 2)
        for n in range(p.I):
            at = pl.ds((g * p.I + n) * fl, fl)
            pos = row + fl * (n * p.R + r)
            angles = pos.astype(F32) * inverse
            cos_ref[at, :] = jnp.cos(angles)
            sin_ref[at, :] = jnp.sin(angles) * sign
            alive = pos < length
            mask_ref[at, :] = jnp.where((lane == 0) & ~alive, NEGATIVE, 0.0).astype(BF)
            if g == 0:
                live_ref[at, :] = jnp.where(alive, 1.0, 0.0)[:, 0:1]


def front_kernel(
    S, T, I, cb, hb,
    frames, cotangent, time_ref, lengths_ref, wq_ref, wk_ref, wv_ref, wo_ref, wu_ref, wd_ref, wm_ref,
    all_a, xm_out, q_out, k_out, v_out, att_out, lse_out, grad_f, cos_out, sin_out, mask_out,
    frames_in, mod_ref, layer_ref, dmid_ref, dbranch_ref, dmod_ref,
    xm_ref, q_ref, k_ref, v_ref, att_ref, lse_ref, cos_ref, sin_ref, mask_ref,
    a_ref, f_ref, cot_in, parts, line_in, line_sum, parts_in, live_ref, branch_ref, mid_ref,
    normed_ref, mf_ref, mf_turned, db_ref, db_turned, out_sum, dmf_sum, stage,
    send, recv, local, row_send, row_recv, out_sem,
):
    p = Place(S, T, I)
    wires = Wires(send, recv, local)
    nq, nh = a_ref.shape[0], f_ref.shape[0]
    fl, rs = frames.shape[1], wq_ref.shape[0]
    rows, L = I * fl, I * fl * p.R
    micro, batch = lengths_ref.shape
    rows_own = I // micro
    for j in range(nq):
        cols = slice(j * cb, (j + 1) * cb)
        blocks = (wq_ref[:, cols], wk_ref[:, cols], wv_ref[:, cols], wo_ref[:, cols])
        a_ref[j, 0, p.z, p.x, p.c] = jnp.concatenate(blocks, axis=1)
    greet(p)
    chunks_a = [Gather(p, wires, a_ref.at[j], 2) for j in range(nq)]
    chunks_f = [Gather(p, wires, f_ref.at[j], 2) for j in range(nh)]
    chunks = chunks_a + chunks_f

    def upto(m, phase):
        if m < len(chunks):
            chunks[m].upto(phase)

    upto(0, 0)
    product = nn(own_columns(p, time_ref[...], rs), wm_ref[...])
    high = parts.shape[2]
    for item in range(micro * batch):
        m, b = divmod(item, batch)
        t, own = divmod(b, rows_own)
        for n in range(high):
            parts[t, m * rows_own + own, n : n + 1, :] = product[
                item : item + 1, n * 128 : (n + 1) * 128
            ]
    line = []
    for k in range(1, I):
        other = lax.rem(p.i + k, I)
        line.append(
            wires.push(parts.at[:, other], line_in.at[k - 1], (other * p.R + p.r, p.t))
        )
    for j in range(nh):
        cols = slice(j * hb, (j + 1) * hb)
        f_ref[j, 0, p.z, p.x, p.c] = jnp.concatenate([wu_ref[:, cols], wd_ref[:, cols]], axis=1)
    upto(0, 1)
    frames_own, frames_got = swap_items(p, wires, frames, frames_in)
    landed(line)
    for t in range(T):
        total = parts[t, p.i]
        for k in range(1, I):
            total = total + line_in[k - 1, t]
        line_sum[t] = total
    parts_in[p.t, p.r] = line_sum[p.t]
    group_done = spread_group(p, row_send, row_recv, lambda t: line_sum.at[t], parts_in)
    upto(0, 2)
    length = lengths_ref[lax.div(p.i, rows_own), p.t * rows_own + lax.rem(p.i, rows_own)]
    fill_tables(p, fl, length, cos_ref, sin_ref, mask_ref, live_ref)
    group_done()
    mod_ref[...] = jnp.zeros_like(mod_ref)
    for t in range(T):
        total = jnp.sum(parts_in[t], axis=0).astype(BF).astype(F32)
        for n in range(high):
            row, col = divmod((t * high + n) * 128, D)
            mod_ref[row : row + 1, col : col + 128] = total[n : n + 1]
    frames_own.wait()
    landed(frames_got)
    upto(1, 0)
    frame_rows = frames_in[...].reshape(rows, D).astype(F32)
    normed, _ = layer_stats(frame_rows)
    low = normed.astype(BF).astype(F32)
    xm_ref[0, 0] = (low * (1.0 + mod_ref[1:2, :]) + mod_ref[0:1, :]).astype(BF)
    sibling = p.group(0, 1 - p.c)
    across = [wires.push(xm_ref.at[0, 0], xm_ref.at[p.Q - k, 0], p.group(k)) for k in range(1, p.Q)]
    cores = [wires.push(xm_ref.at[0, 0], xm_ref.at[0, 1], sibling)]
    upto(0, 3)
    upto(1, 1)
    upto(2, 0)
    for k in range(1, p.Q):
        across[k - 1].wait_recv()
        cores.append(wires.push(xm_ref.at[p.Q - k, 0], xm_ref.at[p.Q - k, 1], sibling))
    upto(1, 2)
    upto(2, 1)
    upto(3, 0)
    landed(cores)

    cot_copies, steps = [], nq * T

    def ask_cotangent():
        own, got = swap_items(p, wires, cotangent, cot_in)
        cot_copies.extend([own, got])

    between = {
        0: lambda: (upto(1, 3), upto(2, 2), upto(3, 1), upto(4, 0),),
        1: lambda: (upto(2, 3), upto(3, 2), upto(4, 1), upto(5, 0),),
        2: lambda: (upto(3, 3), upto(4, 2), upto(5, 1), ask_cotangent(),),
        4: lambda: (upto(4, 3), upto(5, 2),),
        7: lambda: (upto(5, 3),),
    }
    if len(chunks) < 4:
        between = {}

    xm = xm_ref[...].reshape(L, D)
    copies = [
        wires.move(xm_ref, xm_out),
        wires.move(cos_ref, cos_out),
        wires.move(sin_ref, sin_out),
        wires.move(mask_ref, mask_out),
    ]
    for j in range(nq):
        chunks_a[j].upto(4)
        copies.append(wires.move(a_ref.at[j], all_a.at[j]))
        for t in range(T):
            n = j * T + t
            part = attend_block(
                rows, cb, xm,
                lambda b: a_ref[j, t, :, :, :, :, b * cb : (b + 1) * cb].reshape(D, cb),
                cos_ref, sin_ref, mask_ref,
                q_ref.at[n], k_ref.at[n], v_ref.at[n], att_ref.at[n], lse_ref.at[n],
            )
            if n == 0:
                branch_ref[...] = part
            else:
                branch_ref[...] += part
            between.get(n, tuple)()
    if not cot_copies:
        ask_cotangent()

    for src, dst in (
        (q_ref, q_out), (k_ref, k_out), (v_ref, v_out), (att_ref, att_out), (lse_ref, lse_out)
    ):
        copies.append(wires.move(src, dst))
    gate_attn, shift_ff = mod_ref[2:3, :], mod_ref[3:4, :]
    scale_ff, gate_ff = mod_ref[4:5, :], mod_ref[5:6, :]
    middle = (
        frames_in[...].reshape(rows, D).astype(F32)
        + gate_attn * live_ref[...] * branch_ref[...]
    )
    mid_ref[...] = middle
    normed, _ = layer_stats(middle)
    low = normed.astype(BF)
    normed_ref[...] = low
    modulated = (low.astype(F32) * (1.0 + scale_ff) + shift_ff).astype(BF)
    mf_ref[...] = modulated
    mf_turned[...] = modulated.T
    cot_copies[0].wait()
    landed(cot_copies[1])
    d_branch = (cot_in[...].reshape(rows, D).astype(F32) * gate_ff).astype(BF)
    db_ref[...] = d_branch
    db_turned[...] = d_branch.T

    pending = [None, None]
    for j in range(nh):
        chunks_f[j].upto(4)
        for t in range(T):
            n = j * T + t
            w_up = f_ref[j, t, :, :, :, :, 0:hb].reshape(D, hb)
            w_down = f_ref[j, t, :, :, :, :, hb : 2 * hb].reshape(D, hb)
            upper = nn(mf_ref[...], w_up)
            square = upper * upper
            slope = 0.7978845608
            tanh = jnp.tanh(slope * (upper + 0.044715 * upper * square))
            half = 0.5 * (1.0 + tanh)
            active = (upper * half).astype(BF)
            bend = half + 0.5 * upper * (1.0 - tanh * tanh) * (
                slope * (1.0 + 3 * 0.044715 * square)
            )
            d_upper = (nn(db_ref[...], w_down) * bend).astype(BF)
            if n == 0:
                out_sum[...] = nt(active, w_down)
                dmf_sum[...] = nt(d_upper, w_up)
            else:
                out_sum[...] += nt(active, w_down)
                dmf_sum[...] += nt(d_upper, w_up)
            slot = n % 2
            if pending[slot] is not None:
                pending[slot].wait()
            stage[slot, :, 0:hb] = nn(mf_turned[...], d_upper).astype(BF)
            stage[slot, :, hb : 2 * hb] = nn(db_turned[...], active).astype(BF)
            pending[slot] = pltpu.make_async_copy(stage.at[slot], grad_f.at[j, t], out_sem.at[slot])
            pending[slot].start()
            between.get(steps + n, tuple)()

    middle, branch_f = mid_ref[...], out_sum[...]
    layer_ref[...] = (middle + gate_ff * branch_f).astype(BF).reshape(layer_ref.shape)
    cot = cot_in[...].reshape(rows, D).astype(F32)
    normed, inverse = layer_stats(middle)
    dmf = dmf_sum[...]
    d_mid = cot + layer_back(normed, inverse, dmf * (1.0 + scale_ff))
    dmid_ref[...] = d_mid
    alive = d_mid * live_ref[...]
    dbranch_ref[...] = (alive * gate_attn).astype(BF)
    dmod_ref[...] = jnp.zeros_like(dmod_ref)
    dmod_ref[2:3, :] = jnp.sum(alive * branch_ref[...], axis=0, keepdims=True)
    dmod_ref[3:4, :] = jnp.sum(dmf, axis=0, keepdims=True)
    dmod_ref[4:5, :] = jnp.sum(dmf * normed_ref[...].astype(F32), axis=0, keepdims=True)
    dmod_ref[5:6, :] = jnp.sum(cot * branch_f, axis=0, keepdims=True)
    for copy in copies + [c for c in pending if c is not None]:
        copy.wait()
    wires.close()


def front_call(S, T, I, cb, hb, frames, cotangent, time, lengths, weights):
    w_query, w_up, w_mod = weights[0], weights[4], weights[6]
    rs = w_query.shape[0]
    nq, wide_a = w_query.shape[1] // cb, 4 * cb
    nh, wide_f = w_up.shape[1] // hb, 2 * hb
    fl = frames.shape[1]
    rows, Z, R = I * fl, S // 4, S // I
    Q, L, steps = R // 2, rows * R, nq * T
    high = w_mod.shape[1] // 128
    remote = 3 * (I - 1) + (nq + nh) * (Z + 2 * T + 4) + 2 * Q
    shape = jax.ShapeDtypeStruct
    vmem, dma = pltpu.VMEM, pltpu.SemaphoreType.DMA
    kept = [
        ((Q, 2, rows, D), BF),
        ((steps, rows, cb), BF),
        ((steps, L, cb), BF),
        ((steps, L, cb), BF),
        ((steps, rows, cb), BF),
        ((steps, 8, rows), F32),
        ((L, 128), F32),
        ((L, 128), F32),
        ((L, 128), BF),
    ]
    return pl.pallas_call(
        partial(front_kernel, S, T, I, cb, hb),
        out_shape=tuple(shape(*x) for x in [((nq, T, Z, 2, 2, rs, wide_a), BF)] + kept[:6])
        + (shape((nh, T, D, wide_f), BF),)
        + tuple(shape(*x) for x in kept[6:])
        + (
            shape(frames.shape, BF),
            shape((8, D), F32),
            shape(frames.shape, BF),
            shape((rows, D), F32),
            shape((rows, D), BF),
            shape((8, D), F32),
        ),
        in_specs=[ANY] * 2 + [VMEM, pl.BlockSpec(memory_space=pltpu.SMEM)] + [VMEM] * 7,
        out_specs=(ANY,) * 11 + (VMEM,) * 6,
        scratch_shapes=[vmem(*x) for x in kept]
        + [
            vmem((nq, T, Z, 2, 2, rs, wide_a), BF),
            vmem((nh, T, Z, 2, 2, rs, wide_f), BF),
            vmem(frames.shape, BF),
            vmem((T, I, high, 128), F32),
            vmem((I - 1, T, high, 128), F32),
            vmem((T, high, 128), F32),
            vmem((T, R, high, 128), F32),
            vmem((rows, 1), F32),
            vmem((rows, D), F32),
            vmem((rows, D), F32),
            vmem((rows, D), BF),
            vmem((rows, D), BF),
            vmem((D, rows), BF),
            vmem((rows, D), BF),
            vmem((D, rows), BF),
            vmem((rows, D), F32),
            vmem((rows, D), F32),
            vmem((2, D, wide_f), BF),
            dma((remote,)),
            dma((remote,)),
            dma((11 + nq,)),
            dma((R * T,)),
            dma((R * T,)),
            dma((2,)),
        ],
        compiler_params=pltpu.CompilerParams(
            collective_id=0, has_side_effects=True, vmem_limit_bytes=LIMIT
        ),
        name="forward",
    )(frames, cotangent, time, lengths, *weights)


def attend_back_block(
    rows, cb, weight, wide, db_ref, xm_turned, db_turned, cos_ref, sin_ref, mask_ref,
    q_ref, k_ref, v_ref, att_ref, lse_ref, store,
):
    d_att = nn(db_ref[...], weight(3)).astype(BF)
    store(3, nn(db_turned[...], att_ref[...]))
    ones = first_lane(rows)
    factor = HEAD_DIM**-0.5
    dqs, dks, dvs = [], [], []
    for p in range(cb // 128):
        lanes = slice(p * 128, p * 128 + 128)
        q2, k2, v2 = q_ref[:, lanes], k_ref[:, lanes], v_ref[:, lanes]
        k_long = jnp.concatenate([k2, mask_ref[...]], axis=1)
        k_turned = k2.T
        dq_parts, ds_all, p_all = [], [], []
        q_heads, d_heads = head_split(q2), head_split(d_att[:, lanes])
        for h in range(2):
            scores = nt(k_long, jnp.concatenate([q_heads[h], ones], axis=1))
            probs = jnp.exp(scores - lse_ref[pl.ds(2 * p + h, 1), :])
            d_probs = nt(v2, d_heads[h])
            row_dot = jnp.sum(probs * d_probs, axis=0, keepdims=True)
            d_scores = (probs * (d_probs - row_dot)).astype(BF)
            dq_parts.append(nn(k_turned[h * HEAD_DIM : (h + 1) * HEAD_DIM], d_scores))
            ds_all.append(d_scores)
            p_all.append(probs.astype(BF))
        dk2 = nn(jnp.concatenate(ds_all, axis=1), jnp.concatenate(q_heads, axis=0))
        dv2 = nn(jnp.concatenate(p_all, axis=1), jnp.concatenate(d_heads, axis=0))
        dq2 = jnp.concatenate(dq_parts, axis=0).T * factor
        dqs.append(
            (dq2 * cos_ref[0:rows, :] - swap_pairs(dq2) * sin_ref[0:rows, :]).astype(BF)
        )
        dks.append((dk2 * cos_ref[...] - swap_pairs(dk2) * sin_ref[...]).astype(BF))
        dvs.append(dv2.astype(BF))
    dq, dk, dv = (jnp.concatenate(v, axis=1) for v in (dqs, dks, dvs))
    store(0, nn(xm_turned[:, 0:rows], dq))
    store(1, nn(xm_turned[...], dk))
    store(2, nn(xm_turned[...], dv))
    return nt(jnp.concatenate([dk, dv], axis=1), wide(1, 3)), nt(dq, weight(0))


def back_kernel(
    S, T, I, cb,
    layer, all_a, grad_f, k_all, v_all, xm_all, dmid, frames,
    q_ref, att_ref, lse_ref, mod_ref, db_ref, dmod_ref,
    cos_ref, sin_ref, mask_ref,
    layer_out, grads_out, rows_out, sum_a, sum_f,
    *scratch,
):
    nh, nq = grad_f.shape[0], all_a.shape[0]
    (xm_turned, db_turned, dx_sum, dx_ref, near, far, d_rows, group_in, group_sum, ga_ref,
     w_stage, k_stage, v_stage, in_sem, send, recv, local, row_send, row_recv) = scratch[:19]
    rest = scratch[19:]
    p = Place(S, T, I)
    wires = Wires(send, recv, local)
    Q, _, rows, _ = xm_all.shape
    L = Q * 2 * rows
    steps, slots = nq * T, w_stage.shape[0]

    def fetch(n):
        j, t = divmod(n, T)
        slot = n % slots
        copies = [
            pltpu.make_async_copy(all_a.at[j, t], w_stage.at[slot], in_sem.at[0, slot]),
            pltpu.make_async_copy(k_all.at[n], k_stage.at[slot], in_sem.at[1, slot]),
            pltpu.make_async_copy(v_all.at[n], v_stage.at[slot], in_sem.at[2, slot]),
        ]
        for copy in copies:
            copy.start()
        return copies

    xm_copy = wires.move(xm_all, dx_ref)
    fetched = fetch(0)
    greet(p)
    chunks_f, chunks_a = [], []
    for j in range(nh):
        own, landing, rest = rest[0], rest[1:7], rest[7:]
        chunks_f.append(Reduce(p, wires, grad_f.at[j], sum_f.at[j], own, 0, 2, landing))
    for j in range(nq):
        for h in (1, 0):
            landing, rest = rest[:6], rest[6:]
            cols = pl.ds(2 * cb * h, 2 * cb)
            g = ga_ref.at[j, :, :, :, :, :, cols]
            chunks_a.append(Reduce(p, wires, g, sum_a.at[j, :, cols], g, p.c, 3 if j == 1 else 2, landing))
    chunks = chunks_f + chunks_a

    def upto(m, phase):
        if m < len(chunks):
            chunks[m].upto(phase)

    upto(0, 0)
    if nh > 1:
        upto(1, 0)
    xm_copy.wait()
    db_turned[...] = db_ref[...].T
    upto(0, 1)
    for m in range(2, nh):
        upto(m, 0)
    xm_turned[...] = dx_ref[...].reshape(L, D).T
    for m in range(1, nh):
        upto(m, 1)
    layer_own, layer_in = swap_items(p, wires, layer, layer_out)

    between = {}
    if nq == 2 and T == 2 and nh == 4:
        between = {
            0: lambda: (upto(0, 2), upto(1, 2)),
            1: lambda: (upto(4, 0), upto(5, 0), upto(2, 2), upto(3, 2), upto(4, 1), upto(5, 1)),
            2: lambda: (upto(0, 3), upto(1, 3), upto(2, 3), upto(3, 3)),
        }

    for n in range(steps):
        j, t = divmod(n, T)
        slot = n % slots
        coming = fetch(n + 1) if slots == 2 and n + 1 < steps else None
        for copy in fetched:
            copy.wait()
        fetched = coming

        def store(b, value):
            ga_ref[j, t, :, :, :, :, b * cb : (b + 1) * cb] = value.astype(BF).reshape(
                ga_ref.shape[2:6] + (cb,)
            )

        dx, dx_own = attend_back_block(
            rows, cb,
            lambda b: w_stage[slot, :, b * cb : (b + 1) * cb],
            lambda b, e: w_stage[slot, :, b * cb : e * cb],
            db_ref, xm_turned, db_turned, cos_ref, sin_ref, mask_ref,
            q_ref.at[n], k_stage.at[slot], v_stage.at[slot], att_ref.at[n], lse_ref.at[n], store,
        )
        if n == 0:
            dx_sum[...] = dx
        else:
            dx_sum[...] += dx
        dx_sum[0:rows, :] += dx_own
        if slots == 1 and n + 1 < steps:
            fetched = fetch(n + 1)
        if n < steps - 1:
            between.get(n, tuple)()

    dx_ref[...] = dx_sum[...].astype(BF).reshape(dx_ref.shape)
    dmid_copy = wires.move(dmid, dx_sum.at[pl.ds(rows, rows)])
    fl = layer.shape[1]
    frame_copies = [
        wires.move(frames.at[n], xm_turned.at[pl.ds(n * fl, fl), pl.ds(0, D)]) for n in range(I)
    ]
    core = wires.push(dx_ref.at[:, 1], near, p.group(0, 1 - p.c))
    last = len(chunks) - 1
    upto(last - 1, 0)
    upto(last, 0)
    core.wait_recv()
    across = []
    for k in range(1, Q):
        dx_ref[k, 0] = dx_ref[k, 0] + near[k]
        across.append(wires.push(dx_ref.at[k, 0], far.at[k - 1], p.group(k)))
    for m in range(last - 1):
        upto(m, 2)
    upto(last - 1, 1)
    upto(last, 1)
    for m in range(nh):
        upto(m, 3)

    for copy in frame_copies:
        copy.wait()
    normed, inverse = layer_stats(xm_turned[0:rows, 0:D].astype(F32))
    d_mod = dx_sum[0:rows, :] + near[0].astype(F32)
    for k in range(1, Q):
        across[k - 1].wait_recv()
        d_mod = d_mod + far[k - 1].astype(F32)
    incoming = layer_back(normed, inverse, d_mod * (1.0 + mod_ref[1:2, :]))
    dmid_copy.wait()
    dx_ref[0, 0] = (dx_sum[rows : 2 * rows, :] + incoming).astype(BF)
    grads_own, grads_in = swap_items(
        p, wires, lambda n: dx_ref.at[0, 0, pl.ds(n * fl, fl)], grads_out
    )
    high = d_rows.shape[1]
    first = [
        jnp.sum(d_mod, axis=0, keepdims=True),
        jnp.sum(d_mod * normed.astype(BF).astype(F32), axis=0, keepdims=True),
    ]
    for t in range(T):
        for n in range(high):
            row, col = divmod((t * high + n) * 128, D)
            value = first[row] if row < 2 else dmod_ref[row : row + 1, :]
            d_rows[t, n : n + 1, :] = value[:, col : col + 128]
    group_in[p.t, p.r] = d_rows[p.t]
    group_done = spread_group(p, row_send, row_recv, lambda t: d_rows.at[t], group_in)
    for m in range(last - 1):
        upto(m, 3)
    group_done()
    for t in range(T):
        group_sum[t] = jnp.sum(group_in[t], axis=0)
    rows_own = wires.move(group_sum, rows_out.at[p.i])
    line = []
    for k in range(1, I):
        other = lax.rem(p.i + k, I)
        line.append(wires.push(group_sum, rows_out.at[p.i], (other * p.R + p.r, p.t)))
    upto(last - 1, 2)
    upto(last, 2)
    for m in range(nh):
        upto(m, 4)
    upto(last - 1, 3)
    upto(last, 3)
    for m in range(last + 1):
        upto(m, 4)
    landed(line)
    for own in (grads_own, layer_own, rows_own):
        own.wait()
    landed(grads_in)
    landed(layer_in)
    wires.close()


def back_call(
    S, T, I, cb, layer, all_a, grad_f, k, v, xm, d_mid, frames,
    q, att, lse, mod, d_branch, d_mod, cosine, sine, mask,
):
    nq, ca = all_a.shape[0], all_a.shape[3]
    nh, cf = grad_f.shape[0], grad_f.shape[6]
    rs = grad_f.shape[5]
    Z, Q, rows = S // 4, xm.shape[0], xm.shape[2]
    L = Q * 2 * rows
    high = 6 * D // T // 128
    slots = 2 if L <= 1024 else 1
    remote = 3 * (I - 1) + (2 * nq + nh) * (Z + 2 * T + 2) + Q
    R = S // I
    shape = jax.ShapeDtypeStruct
    dma = pltpu.SemaphoreType.DMA
    scratch = [
        pltpu.VMEM((D, L), BF),
        pltpu.VMEM((D, rows), BF),
        pltpu.VMEM((L, D), F32),
        pltpu.VMEM((Q, 2, rows, D), BF),
        pltpu.VMEM((Q, rows, D), BF),
        pltpu.VMEM((Q - 1, rows, D), BF),
        pltpu.VMEM((T, high, 128), F32),
        pltpu.VMEM((T, R, high, 128), F32),
        pltpu.VMEM((T, high, 128), F32),
        pltpu.VMEM((nq, T, Z, 2, 2, rs, ca), BF),
        pltpu.VMEM((slots, D, ca), BF),
        pltpu.VMEM((slots, L, cb), BF),
        pltpu.VMEM((slots, L, cb), BF),
        dma((3, slots)),
        dma((remote,)),
        dma((remote,)),
        dma((5 + nh + I,)),
        dma((R * T,)),
        dma((R * T,)),
    ]
    for _ in range(nh):
        scratch += [pltpu.VMEM((T, Z, 2, 1, rs, cf), BF)] + Reduce.landing(T, Z, rs, cf, 2)
    for j in range(2 * nq):
        scratch += Reduce.landing(T, Z, rs, ca // 2, 3 if j // 2 == 1 else 2)
    return pl.pallas_call(
        partial(back_kernel, S, T, I, cb),
        out_shape=(
            shape(layer.shape, BF),
            shape(layer.shape, BF),
            shape((I, T, high, 128), F32),
            shape((nq, rs, ca), F32),
            shape((nh, rs, cf), F32),
        ),
        in_specs=[ANY] * 8 + [VMEM] * 9,
        out_specs=(ANY, ANY, ANY, VMEM, VMEM),
        scratch_shapes=scratch,
        compiler_params=pltpu.CompilerParams(
            collective_id=1, has_side_effects=True, vmem_limit_bytes=LIMIT
        ),
        name="backward",
    )(
        layer, all_a, grad_f, k, v, xm, d_mid, frames,
        q, att, lse, mod, d_branch, d_mod, cosine, sine, mask,
    )


def layer_stats(values):
    center = values - jnp.mean(values, axis=-1, keepdims=True)
    inverse = lax.rsqrt(jnp.mean(center * center, axis=-1, keepdims=True) + EPSILON)
    return center * inverse, inverse


def layer_back(normed, inverse, incoming):
    return inverse * (
        incoming
        - jnp.mean(incoming, axis=-1, keepdims=True)
        - normed * jnp.mean(incoming * normed, axis=-1, keepdims=True)
    )


def finish_kernel(
    S, T, I, micro, time_ref, rows_ref, sum_a, sum_f, layer_in, grads_in,
    layer_ref, grads_ref, gq_ref, gk_ref, gv_ref, go_ref, gu_ref, gd_ref, gm_ref, items_ref,
):
    p = Place(S, T, I)
    nq, rs, wide_a = sum_a.shape
    nh, _, wide_f = sum_f.shape
    cb, hb = wide_a // 4, wide_f // 2
    layer_ref[...] = layer_in[...]
    grads_ref[...] = grads_in[...]
    for j in range(nq):
        for b, ref in enumerate((gq_ref, gk_ref, gv_ref, go_ref)):
            ref[:, j * cb : (j + 1) * cb] = sum_a[j, :, b * cb : (b + 1) * cb]
    for j in range(nh):
        gu_ref[:, j * hb : (j + 1) * hb] = sum_f[j, :, 0:hb]
        gd_ref[:, j * hb : (j + 1) * hb] = sum_f[j, :, hb : 2 * hb]
    high = rows_ref.shape[2]
    rows_own = I // micro
    for item in range(I * T):
        m, b = divmod(item, rows_own * T)
        i, t = m * rows_own + b % rows_own, b // rows_own
        for n in range(high):
            items_ref[item : item + 1, n * 128 : (n + 1) * 128] = rows_ref[i, t, n : n + 1, :]
    silu = own_columns(p, time_ref[...], rs).astype(F32)
    gm_ref[...] = lax.dot_general(
        silu, items_ref[...], (((0,), (0,)), ((), ())), precision=HIGHEST,
        preferred_element_type=F32,
    )


def finish_call(S, T, I, micro, time, rows, sum_a, sum_f, layer, grads, weights):
    shape = jax.ShapeDtypeStruct
    return pl.pallas_call(
        partial(finish_kernel, S, T, I, micro),
        out_shape=(shape(layer.shape, BF), shape(grads.shape, BF))
        + tuple(shape(w.shape, F32) for w in weights),
        in_specs=[VMEM] * 6,
        out_specs=(VMEM,) * 9,
        scratch_shapes=[pltpu.VMEM((I * T, weights[6].shape[1]), F32)],
        compiler_params=pltpu.CompilerParams(vmem_limit_bytes=LIMIT),
        name="finish",
    )(time, rows, sum_a, sum_f, layer, grads)


def per_device(
    S, T, frames, time_embed, lengths, w_query, w_key, w_value, w_out, w_up, w_down, w_mod, out_grad
):
    micro, rows_own, fl, _ = frames.shape
    batch = lengths.shape[1]
    I = micro * rows_own
    rs = w_query.shape[0]
    cb = min(256, w_query.shape[1])
    hb = min(256, w_up.shape[1])
    time = time_embed
    weights = (w_query, w_key, w_value, w_out.T, w_up, w_down.T, w_mod)
    (
        all_a, xm, q, k, v, att, lse, grad_f, cosine, sine, mask,
        frames_in, mod, layer, d_mid, d_branch, d_rows,
    ) = front_call(
        S, T, I, cb, hb, frames.reshape(I, fl, D), out_grad.reshape(I, fl, D), time, lengths, weights
    )
    layer_out, grad_input, rows_in, sum_a, sum_f = back_call(
        S, T, I, cb, layer, all_a.reshape(all_a.shape[:2] + (D, 4 * cb)),
        grad_f.reshape((grad_f.shape[0], T, S // 4, 2, 2, rs, 2 * hb)), k, v, xm, d_mid,
        frames_in, q, att, lse, mod, d_branch, d_rows, cosine, sine, mask,
    )
    outs = finish_call(S, T, I, micro, time, rows_in, sum_a, sum_f, layer_out, grad_input, weights)
    layer_out, grad_input, g_query, g_key, g_value, g_out, g_up, g_down, g_mod = outs
    return (
        layer_out.reshape(frames.shape), grad_input.reshape(frames.shape),
        g_query, g_key, g_value, g_out.T, g_up, g_down.T, g_mod,
    )


def solution(mesh):
    S, T = mesh.shape["seq"], mesh.shape["tp"]
    rows = P(None, "tp", "seq", None)
    return jax.shard_map(
        partial(per_device, S, T),
        mesh=mesh,
        in_specs=(
            rows,
            P(),
            P(),
            P("seq", "tp"),
            P("seq", "tp"),
            P("seq", "tp"),
            P("tp", "seq"),
            P("seq", "tp"),
            P("tp", "seq"),
            P("seq", "tp"),
            rows,
        ),
        out_specs=(
            rows,
            rows,
            P("seq", "tp"),
            P("seq", "tp"),
            P("seq", "tp"),
            P("tp", "seq"),
            P("seq", "tp"),
            P("tp", "seq"),
            P("seq", "tp"),
        ),
        check_vma=False,
    )
```

```python
from functools import partial
import math

import jax
import jax.numpy as jnp
from jax import lax
from jax.experimental import pallas as pl
from jax.experimental.pallas import tpu as pltpu
from jax.sharding import PartitionSpec as P

D = 1024
HEAD_DIM = 64
EPSILON = 1e-06
NEGATIVE = -1e30
BF = jnp.bfloat16
F32 = jnp.float32
HIGHEST = lax.Precision.HIGHEST
MESH = pl.DeviceIdType.MESH
ANY = pl.BlockSpec(memory_space=pl.ANY)
VMEM = pl.BlockSpec(memory_space=pltpu.VMEM)
LIMIT = 62 * 1024 * 1024


def nn(a, b):
    return lax.dot_general(a, b, (((1,), (0,)), ((), ())), preferred_element_type=F32)


def nt(a, b):
    return lax.dot_general(a, b, (((1,), (1,)), ((), ())), preferred_element_type=F32)


class Place:
    def __init__(self, S, T, I):
        self.S, self.T, self.I = S, T, I
        self.Z, self.R = S // 4, S // I
        self.Q = self.R // 2
        self.s, self.t = lax.axis_index("seq"), lax.axis_index("tp")
        self.z = lax.div(self.s, 4)
        self.x = lax.rem(lax.div(self.s, 2), 2)
        self.c = lax.rem(self.s, 2)
        self.i = lax.div(self.s, self.R)
        self.r = lax.rem(self.s, self.R)
        self.q = lax.div(self.r, 2)

    def at(self, z=None, x=None, c=None, t=None):
        z = self.z if z is None else z
        x = self.x if x is None else x
        c = self.c if c is None else c
        t = self.t if t is None else t
        return ((z * 2 + x) * 2 + c, t)

    def tp(self, k):
        return (self.s, lax.rem(self.t + k, self.T))

    def zs(self, k):
        return lax.rem(self.z + k, self.Z)

    def group(self, k, c=None):
        c = self.c if c is None else c
        return (self.i * self.R + lax.rem(self.q + k, self.Q) * 2 + c, self.t)


class Wires:
    def __init__(self, send, recv, local):
        self.send, self.recv, self.local = send, recv, local
        self.remote_count = self.local_count = 0
        self.sent = []

    def push(self, src, dst, device):
        n = self.remote_count
        self.remote_count += 1
        copy = pltpu.make_async_remote_copy(
            src_ref=src,
            dst_ref=dst,
            send_sem=self.send.at[n],
            recv_sem=self.recv.at[n],
            device_id=device,
            device_id_type=MESH,
        )
        copy.start()
        self.sent.append(copy)
        return copy

    def move(self, src, dst):
        n = self.local_count
        self.local_count += 1
        copy = pltpu.make_async_copy(src, dst, self.local.at[n])
        copy.start()
        return copy

    def close(self):
        for copy in self.sent:
            copy.wait_send()


def landed(copies):
    for copy in copies:
        copy.wait_recv()


def loop_group(place, first, body):
    total = place.R * place.T
    me = place.r * place.T + place.t

    def step(d, carry):
        other = lax.rem(me + d, total)
        body(d, place.i * place.R + lax.div(other, place.T), lax.rem(other, place.T))
        return carry

    lax.fori_loop(first, total, step, 0)


def greet(place):
    barrier = pltpu.get_barrier_semaphore()

    def signal(d, s, t):
        pl.semaphore_signal(barrier, inc=1, device_id=(s, t), device_id_type=MESH)

    for k in range(1, place.Z):
        signal(k, *place.at(z=place.zs(k)))
    loop_group(place, 1, signal)
    pl.semaphore_wait(barrier, place.Z - 1 + place.R * place.T - 1)


def spread_group(place, send, recv, src_of, dst):
    def copy(d, s, t):
        return pltpu.make_async_remote_copy(
            src_ref=src_of(t),
            dst_ref=dst.at[place.t, place.r],
            send_sem=send.at[d],
            recv_sem=recv.at[d],
            device_id=(s, t),
            device_id_type=MESH,
        )

    loop_group(place, 1, lambda d, s, t: copy(d, s, t).start())
    return lambda: loop_group(place, 1, lambda d, s, t: copy(d, s, t).wait())


class Phased:
    done = 0

    def upto(self, phase):
        while self.done <= phase:
            getattr(self, f"phase{self.done}")()
            self.done += 1


def split_rows(rs, quarters):
    upper = rs * quarters // 4 if rs * quarters // 4 % 16 == 0 else rs // 2
    return pl.ds(0, upper), pl.ds(upper, rs - upper)


class Gather(Phased):
    def __init__(self, place, wires, dst, quarters):
        self.p, self.w, self.dst = place, wires, dst
        self.upper, self.lower = split_rows(dst.shape[4], quarters)

    def phase0(self):
        p, w, dst = self.p, self.w, self.dst
        own = dst.at[0, p.z, p.x, p.c]
        self.along = [w.push(own, own, p.at(z=p.zs(k))) for k in range(1, p.Z)]

    def phase1(self):
        p, w, dst = self.p, self.w, self.dst
        landed(self.along)
        line = dst.at[0, :, p.x, p.c]
        self.sides = [
            w.push(
                dst.at[0, :, p.x, p.c, self.upper],
                dst.at[0, :, p.x, p.c, self.upper],
                p.at(x=1 - p.x),
            )
        ]
        for k in range(1, p.T):
            self.sides.append(
                w.push(
                    dst.at[0, :, p.x, p.c, self.lower],
                    dst.at[p.T - k, :, p.x, p.c, self.lower],
                    p.tp(k),
                )
            )
        self.cores = [w.push(line, line, p.at(c=1 - p.c))]

    def phase2(self):
        p, w, dst = self.p, self.w, self.dst
        landed(self.sides)
        self.last = []
        for k in range(1, p.T):
            self.last.append(
                w.push(
                    dst.at[0, :, :, p.c, self.upper],
                    dst.at[p.T - k, :, :, p.c, self.upper],
                    p.tp(k),
                )
            )
        part = dst.at[:, :, p.x, p.c, self.lower]
        self.last.append(w.push(part, part, p.at(x=1 - p.x)))
        part = dst.at[0, :, 1 - p.x, p.c, self.upper]
        self.cores.append(w.push(part, part, p.at(c=1 - p.c)))
        part = dst.at[pl.ds(1, p.T - 1), :, p.x, p.c, self.lower]
        self.cores.append(w.push(part, part, p.at(c=1 - p.c)))

    def phase3(self):
        p, w, dst = self.p, self.w, self.dst
        landed(self.last)
        part = dst.at[pl.ds(1, p.T - 1), :, :, p.c, self.upper]
        self.cores.append(w.push(part, part, p.at(c=1 - p.c)))
        part = dst.at[:, :, 1 - p.x, p.c, self.lower]
        self.cores.append(w.push(part, part, p.at(c=1 - p.c)))

    def phase4(self):
        landed(self.cores)


class Reduce(Phased):
    def __init__(self, place, wires, src, out, own, core_at, quarters, landing):
        self.p, self.w, self.src, self.out = place, wires, src, out
        self.own, self.core_at = own, core_at
        self.core, self.y_up, self.x_low, self.x_up, self.y_low, self.z_in = landing
        self.upper, self.lower = split_rows(own.shape[4], quarters)

    @staticmethod
    def landing(T, Z, rs, C, quarters):
        upper, lower = (part.size for part in split_rows(rs, quarters))
        return [
            pltpu.VMEM((T, Z, 2, rs, C), BF),
            pltpu.VMEM((T - 1, Z, 2, upper, C), BF),
            pltpu.VMEM((T, Z, lower, C), BF),
            pltpu.VMEM((Z, upper, C), BF),
            pltpu.VMEM((T - 1, Z, lower, C), BF),
            pltpu.VMEM((Z - 1, rs, C), BF),
        ]

    def phase0(self):
        p, w, src = self.p, self.w, self.src
        self.mine = None
        if self.own is not src:
            self.mine = w.move(src.at[:, :, :, pl.ds(p.c, 1)], self.own)
        self.pair = [w.push(src.at[:, :, :, 1 - p.c], self.core, p.at(c=1 - p.c))]

    def phase1(self):
        p, w, own, c = self.p, self.w, self.own, self.core_at
        if self.mine is not None:
            self.mine.wait()
        landed(self.pair)

        def add(n, carry):
            k, z = lax.div(n, p.Z), lax.rem(n, p.Z)
            for x in range(2):
                own[k, z, x, c] = own[k, z, x, c] + self.core[k, z, x]
            return carry

        lax.fori_loop(0, p.T * p.Z, add, 0)
        self.sides = [
            w.push(own.at[k, :, :, c, self.upper], self.y_up.at[k - 1], p.tp(k))
            for k in range(1, p.T)
        ]
        self.sides.append(
            w.push(own.at[:, :, 1 - p.x, c, self.lower], self.x_low, p.at(x=1 - p.x))
        )

    def phase2(self):
        p, w, own, c = self.p, self.w, self.own, self.core_at
        landed(self.sides)

        def add(z, carry):
            for x in range(2):
                total = own[0, z, x, c, self.upper].astype(F32)
                for k in range(1, p.T):
                    total = total + self.y_up[k - 1, z, x].astype(F32)
                own[0, z, x, c, self.upper] = total.astype(BF)
            for k in range(p.T):
                own[k, z, p.x, c, self.lower] = own[k, z, p.x, c, self.lower] + self.x_low[k, z]
            return carry

        lax.fori_loop(0, p.Z, add, 0)
        self.last = [w.push(own.at[0, :, 1 - p.x, c, self.upper], self.x_up, p.at(x=1 - p.x))]
        for k in range(1, p.T):
            self.last.append(
                w.push(own.at[k, :, p.x, c, self.lower], self.y_low.at[k - 1], p.tp(k))
            )

    def phase3(self):
        p, w, own, c = self.p, self.w, self.own, self.core_at
        landed(self.last)

        def add(z, carry):
            own[0, z, p.x, c, self.upper] = own[0, z, p.x, c, self.upper] + self.x_up[z]
            total = own[0, z, p.x, c, self.lower].astype(F32)
            for k in range(1, p.T):
                total = total + self.y_low[k - 1, z].astype(F32)
            own[0, z, p.x, c, self.lower] = total.astype(BF)
            return carry

        lax.fori_loop(0, p.Z, add, 0)
        if p.Z == 4:
            near = p.z + 1 - 2 * lax.rem(p.z, 2)
            self.along = [
                w.push(own.at[0, near, p.x, c], self.z_in.at[0], p.at(z=near)),
                w.push(own.at[0, 3 - p.z, p.x, c], self.z_in.at[1], p.at(z=near)),
            ]
        else:
            self.along = [
                w.push(own.at[0, p.zs(k), p.x, c], self.z_in.at[k - 1], p.at(z=p.zs(k)))
                for k in range(1, p.Z)
            ]

    def phase4(self):
        p, w, own, c = self.p, self.w, self.own, self.core_at
        landed(self.along)
        self.across = []
        if p.Z == 4:
            far = p.zs(2)
            own[0, far, p.x, c] = own[0, far, p.x, c] + self.z_in[1]
            self.across.append(w.push(own.at[0, far, p.x, c], self.z_in.at[2], p.at(z=far)))

    def phase5(self):
        p = self.p
        landed(self.across)
        blocks = (0, 2) if p.Z == 4 else range(p.Z - 1)
        total = self.own[0, p.z, p.x, self.core_at].astype(F32)
        for k in blocks:
            total = total + self.z_in[k].astype(F32)
        self.out[...] = total


def swap_items(place, wires, src, dst):
    p = place
    block = src if callable(src) else lambda n: src.at[n]
    own = wires.move(block(p.i), dst.at[p.i])
    copies = []
    for k in range(1, p.I):
        other = lax.rem(p.i + k, p.I)
        copies.append(wires.push(block(other), dst.at[p.i], (other * p.R + p.r, p.t)))
    return own, copies


def swap_pairs(v):
    lane = lax.broadcasted_iota(jnp.int32, v.shape, 1)
    return jnp.where(lax.rem(lane, 2) == 0, pltpu.roll(v, 127, 1), pltpu.roll(v, 1, 1))


def head_split(v):
    lane = lax.broadcasted_iota(jnp.int32, v.shape, 1)
    zero = jnp.zeros_like(v)
    return jnp.where(lane < HEAD_DIM, v, zero), jnp.where(lane < HEAD_DIM, zero, v)


def first_lane(rows):
    lane = lax.broadcasted_iota(jnp.int32, (rows, 128), 1)
    return jnp.where(lane == 0, 1.0, 0.0).astype(BF)


def attend_block(rows, cb, xm, weight, cos_ref, sin_ref, mask_ref, q_ref, k_ref, v_ref, att_ref, lse_ref):
    q_lin = nn(xm[0:rows, :], weight(0))
    k_lin = nn(xm, weight(1))
    v_ref[...] = nn(xm, weight(2)).astype(BF)
    ones = first_lane(rows)
    factor = HEAD_DIM**-0.5
    for p in range(cb // 128):
        lanes = slice(p * 128, p * 128 + 128)
        q2, k2 = q_lin[:, lanes], k_lin[:, lanes]
        q2 = (q2 * cos_ref[0:rows, :] + swap_pairs(q2) * sin_ref[0:rows, :]).astype(BF)
        q2 = q2 * jnp.asarray(factor, BF)
        k2 = (k2 * cos_ref[...] + swap_pairs(k2) * sin_ref[...]).astype(BF)
        q_ref[:, lanes] = q2
        k_ref[:, lanes] = k2
        k_long = jnp.concatenate([k2, mask_ref[...]], axis=1)
        v_turned = v_ref[:, lanes].T
        outs = []
        for h, q1 in enumerate(head_split(q2)):
            scores = nt(k_long, jnp.concatenate([q1, ones], axis=1))
            highest = jnp.max(scores, axis=0, keepdims=True)
            unnormed = jnp.exp(scores - highest)
            total = jnp.sum(unnormed, axis=0, keepdims=True)
            probs = (unnormed * (1.0 / total)).astype(BF)
            lse_ref[pl.ds(2 * p + h, 1), :] = highest + jnp.log(total)
            outs.append(nn(v_turned[h * HEAD_DIM : (h + 1) * HEAD_DIM], probs))
        att_ref[:, lanes] = jnp.concatenate(outs, axis=0).T.astype(BF)
    return nt(att_ref[...], weight(3))


def own_columns(place, time, rs):
    time = jnp.concatenate([time[m] for m in range(time.shape[0])], axis=0)
    silu = (time / (1.0 + jnp.exp(-time))).astype(BF)
    feature = lax.broadcasted_iota(jnp.int32, (D, rs), 0)
    chosen = feature == lax.broadcasted_iota(jnp.int32, (D, rs), 1) + place.s * rs
    return nn(silu, jnp.where(chosen, 1.0, 0.0).astype(BF)).astype(BF)


def fill_tables(place, fl, length, cos_ref, sin_ref, mask_ref, live_ref):
    p = place
    lane = lax.broadcasted_iota(jnp.int32, (fl, 128), 1)
    row = lax.broadcasted_iota(jnp.int32, (fl, 128), 0)
    column = lax.div(lax.rem(lane, HEAD_DIM), 2).astype(F32)
    inverse = jnp.exp(column * (-2.0 * math.log(10000.0) / HEAD_DIM))
    sign = jnp.where(lax.rem(lane, 2) == 0, -1.0, 1.0)
    for g in range(p.R):
        r = lax.rem(p.q + g // 2, p.Q) * 2 + lax.rem(p.c + g % 2, 2)
        for n in range(p.I):
            at = pl.ds((g * p.I + n) * fl, fl)
            pos = row + fl * (n * p.R + r)
            angles = pos.astype(F32) * inverse
            cos_ref[at, :] = jnp.cos(angles)
            sin_ref[at, :] = jnp.sin(angles) * sign
            alive = pos < length
            mask_ref[at, :] = jnp.where((lane == 0) & ~alive, NEGATIVE, 0.0).astype(BF)
            if g == 0:
                live_ref[at, :] = jnp.where(alive, 1.0, 0.0)[:, 0:1]


def front_kernel(
    S, T, I, cb, hb,
    frames, cotangent, time_ref, lengths_ref, wq_ref, wk_ref, wv_ref, wo_ref, wu_ref, wd_ref, wm_ref,
    all_a, xm_out, q_out, k_out, v_out, att_out, lse_out, grad_f, cos_out, sin_out, mask_out,
    frames_in, mod_ref, layer_ref, dmid_ref, dbranch_ref, dmod_ref,
    xm_ref, q_ref, k_ref, v_ref, att_ref, lse_ref, cos_ref, sin_ref, mask_ref,
    a_ref, f_ref, cot_in, parts, line_in, line_sum, parts_in, live_ref, branch_ref, mid_ref,
    normed_ref, mf_ref, mf_turned, db_ref, db_turned, out_sum, dmf_sum, stage,
    send, recv, local, row_send, row_recv, out_sem,
):
    p = Place(S, T, I)
    wires = Wires(send, recv, local)
    nq, nh = a_ref.shape[0], f_ref.shape[0]
    fl, rs = frames.shape[1], wq_ref.shape[0]
    rows, L = I * fl, I * fl * p.R
    micro, batch = lengths_ref.shape
    rows_own = I // micro
    for j in range(nq):
        cols = slice(j * cb, (j + 1) * cb)
        blocks = (wq_ref[:, cols], wk_ref[:, cols], wv_ref[:, cols], wo_ref[:, cols])
        a_ref[j, 0, p.z, p.x, p.c] = jnp.concatenate(blocks, axis=1)
    greet(p)
    chunks_a = [Gather(p, wires, a_ref.at[j], 2) for j in range(nq)]
    chunks_f = [Gather(p, wires, f_ref.at[j], 2) for j in range(nh)]
    chunks = chunks_a + chunks_f

    def upto(m, phase):
        if m < len(chunks):
            chunks[m].upto(phase)

    upto(0, 0)
    product = nn(own_columns(p, time_ref[...], rs), wm_ref[...])
    high = parts.shape[2]
    for item in range(micro * batch):
        m, b = divmod(item, batch)
        t, own = divmod(b, rows_own)
        for n in range(high):
            parts[t, m * rows_own + own, n : n + 1, :] = product[
                item : item + 1, n * 128 : (n + 1) * 128
            ]
    line = []
    for k in range(1, I):
        other = lax.rem(p.i + k, I)
        line.append(
            wires.push(parts.at[:, other], line_in.at[k - 1], (other * p.R + p.r, p.t))
        )
    for j in range(nh):
        cols = slice(j * hb, (j + 1) * hb)
        f_ref[j, 0, p.z, p.x, p.c] = jnp.concatenate([wu_ref[:, cols], wd_ref[:, cols]], axis=1)
    upto(0, 1)
    frames_own, frames_got = swap_items(p, wires, frames, frames_in)
    landed(line)
    for t in range(T):
        total = parts[t, p.i]
        for k in range(1, I):
            total = total + line_in[k - 1, t]
        line_sum[t] = total
    parts_in[p.t, p.r] = line_sum[p.t]
    group_done = spread_group(p, row_send, row_recv, lambda t: line_sum.at[t], parts_in)
    upto(0, 2)
    length = lengths_ref[lax.div(p.i, rows_own), p.t * rows_own + lax.rem(p.i, rows_own)]
    fill_tables(p, fl, length, cos_ref, sin_ref, mask_ref, live_ref)
    group_done()
    mod_ref[...] = jnp.zeros_like(mod_ref)
    for t in range(T):
        total = jnp.sum(parts_in[t], axis=0).astype(BF).astype(F32)
        for n in range(high):
            row, col = divmod((t * high + n) * 128, D)
            mod_ref[row : row + 1, col : col + 128] = total[n : n + 1]
    frames_own.wait()
    landed(frames_got)
    upto(1, 0)
    frame_rows = frames_in[...].reshape(rows, D).astype(F32)
    normed, _ = layer_stats(frame_rows)
    low = normed.astype(BF).astype(F32)
    xm_ref[0, 0] = (low * (1.0 + mod_ref[1:2, :]) + mod_ref[0:1, :]).astype(BF)
    sibling = p.group(0, 1 - p.c)
    across = [wires.push(xm_ref.at[0, 0], xm_ref.at[p.Q - k, 0], p.group(k)) for k in range(1, p.Q)]
    cores = [wires.push(xm_ref.at[0, 0], xm_ref.at[0, 1], sibling)]
    upto(0, 3)
    upto(1, 1)
    upto(2, 0)
    for k in range(1, p.Q):
        across[k - 1].wait_recv()
        cores.append(wires.push(xm_ref.at[p.Q - k, 0], xm_ref.at[p.Q - k, 1], sibling))
    upto(1, 2)
    upto(2, 1)
    upto(3, 0)
    landed(cores)

    cot_copies, steps = [], nq * T

    def ask_cotangent():
        own, got = swap_items(p, wires, cotangent, cot_in)
        cot_copies.extend([own, got])

    between = {
        0: lambda: (upto(1, 3), upto(2, 2), upto(3, 1), upto(4, 0),),
        1: lambda: (upto(2, 3), upto(3, 2), upto(4, 1), upto(5, 0),),
        2: lambda: (upto(3, 3), upto(4, 2), upto(5, 1), ask_cotangent(),),
        4: lambda: (upto(4, 3), upto(5, 2),),
        7: lambda: (upto(5, 3),),
    }
    if len(chunks) < 4:
        between = {}

    xm = xm_ref[...].reshape(L, D)
    copies = [
        wires.move(xm_ref, xm_out),
        wires.move(cos_ref, cos_out),
        wires.move(sin_ref, sin_out),
        wires.move(mask_ref, mask_out),
    ]
    for j in range(nq):
        chunks_a[j].upto(4)
        copies.append(wires.move(a_ref.at[j], all_a.at[j]))
        for t in range(T):
            n = j * T + t
            part = attend_block(
                rows, cb, xm,
                lambda b: a_ref[j, t, :, :, :, :, b * cb : (b + 1) * cb].reshape(D, cb),
                cos_ref, sin_ref, mask_ref,
                q_ref.at[n], k_ref.at[n], v_ref.at[n], att_ref.at[n], lse_ref.at[n],
            )
            if n == 0:
                branch_ref[...] = part
            else:
                branch_ref[...] += part
            between.get(n, tuple)()
    if not cot_copies:
        ask_cotangent()

    for src, dst in (
        (q_ref, q_out), (k_ref, k_out), (v_ref, v_out), (att_ref, att_out), (lse_ref, lse_out)
    ):
        copies.append(wires.move(src, dst))
    gate_attn, shift_ff = mod_ref[2:3, :], mod_ref[3:4, :]
    scale_ff, gate_ff = mod_ref[4:5, :], mod_ref[5:6, :]
    middle = (
        frames_in[...].reshape(rows, D).astype(F32)
        + gate_attn * live_ref[...] * branch_ref[...]
    )
    mid_ref[...] = middle
    normed, _ = layer_stats(middle)
    low = normed.astype(BF)
    normed_ref[...] = low
    modulated = (low.astype(F32) * (1.0 + scale_ff) + shift_ff).astype(BF)
    mf_ref[...] = modulated
    mf_turned[...] = modulated.T
    cot_copies[0].wait()
    landed(cot_copies[1])
    d_branch = (cot_in[...].reshape(rows, D).astype(F32) * gate_ff).astype(BF)
    db_ref[...] = d_branch
    db_turned[...] = d_branch.T

    pending = [None, None]
    for j in range(nh):
        chunks_f[j].upto(4)
        for t in range(T):
            n = j * T + t
            w_up = f_ref[j, t, :, :, :, :, 0:hb].reshape(D, hb)
            w_down = f_ref[j, t, :, :, :, :, hb : 2 * hb].reshape(D, hb)
            upper = nn(mf_ref[...], w_up)
            square = upper * upper
            slope = 0.7978845608
            tanh = jnp.tanh(slope * (upper + 0.044715 * upper * square))
            half = 0.5 * (1.0 + tanh)
            active = (upper * half).astype(BF)
            bend = half + 0.5 * upper * (1.0 - tanh * tanh) * (
                slope * (1.0 + 3 * 0.044715 * square)
            )
            d_upper = (nn(db_ref[...], w_down) * bend).astype(BF)
            if n == 0:
                out_sum[...] = nt(active, w_down)
                dmf_sum[...] = nt(d_upper, w_up)
            else:
                out_sum[...] += nt(active, w_down)
                dmf_sum[...] += nt(d_upper, w_up)
            slot = n % 2
            if pending[slot] is not None:
                pending[slot].wait()
            stage[slot, :, 0:hb] = nn(mf_turned[...], d_upper).astype(BF)
            stage[slot, :, hb : 2 * hb] = nn(db_turned[...], active).astype(BF)
            pending[slot] = pltpu.make_async_copy(stage.at[slot], grad_f.at[j, t], out_sem.at[slot])
            pending[slot].start()
            between.get(steps + n, tuple)()

    middle, branch_f = mid_ref[...], out_sum[...]
    layer_ref[...] = (middle + gate_ff * branch_f).astype(BF).reshape(layer_ref.shape)
    cot = cot_in[...].reshape(rows, D).astype(F32)
    normed, inverse = layer_stats(middle)
    dmf = dmf_sum[...]
    d_mid = cot + layer_back(normed, inverse, dmf * (1.0 + scale_ff))
    dmid_ref[...] = d_mid
    alive = d_mid * live_ref[...]
    dbranch_ref[...] = (alive * gate_attn).astype(BF)
    dmod_ref[...] = jnp.zeros_like(dmod_ref)
    dmod_ref[2:3, :] = jnp.sum(alive * branch_ref[...], axis=0, keepdims=True)
    dmod_ref[3:4, :] = jnp.sum(dmf, axis=0, keepdims=True)
    dmod_ref[4:5, :] = jnp.sum(dmf * normed_ref[...].astype(F32), axis=0, keepdims=True)
    dmod_ref[5:6, :] = jnp.sum(cot * branch_f, axis=0, keepdims=True)
    for copy in copies + [c for c in pending if c is not None]:
        copy.wait()
    wires.close()


def front_call(S, T, I, cb, hb, frames, cotangent, time, lengths, weights):
    w_query, w_up, w_mod = weights[0], weights[4], weights[6]
    rs = w_query.shape[0]
    nq, wide_a = w_query.shape[1] // cb, 4 * cb
    nh, wide_f = w_up.shape[1] // hb, 2 * hb
    fl = frames.shape[1]
    rows, Z, R = I * fl, S // 4, S // I
    Q, L, steps = R // 2, rows * R, nq * T
    high = w_mod.shape[1] // 128
    remote = 3 * (I - 1) + (nq + nh) * (Z + 2 * T + 4) + 2 * Q
    shape = jax.ShapeDtypeStruct
    vmem, dma = pltpu.VMEM, pltpu.SemaphoreType.DMA
    kept = [
        ((Q, 2, rows, D), BF),
        ((steps, rows, cb), BF),
        ((steps, L, cb), BF),
        ((steps, L, cb), BF),
        ((steps, rows, cb), BF),
        ((steps, 8, rows), F32),
        ((L, 128), F32),
        ((L, 128), F32),
        ((L, 128), BF),
    ]
    return pl.pallas_call(
        partial(front_kernel, S, T, I, cb, hb),
        out_shape=tuple(shape(*x) for x in [((nq, T, Z, 2, 2, rs, wide_a), BF)] + kept[:6])
        + (shape((nh, T, D, wide_f), BF),)
        + tuple(shape(*x) for x in kept[6:])
        + (
            shape(frames.shape, BF),
            shape((8, D), F32),
            shape(frames.shape, BF),
            shape((rows, D), F32),
            shape((rows, D), BF),
            shape((8, D), F32),
        ),
        in_specs=[ANY] * 2 + [VMEM, pl.BlockSpec(memory_space=pltpu.SMEM)] + [VMEM] * 7,
        out_specs=(ANY,) * 11 + (VMEM,) * 6,
        scratch_shapes=[vmem(*x) for x in kept]
        + [
            vmem((nq, T, Z, 2, 2, rs, wide_a), BF),
            vmem((nh, T, Z, 2, 2, rs, wide_f), BF),
            vmem(frames.shape, BF),
            vmem((T, I, high, 128), F32),
            vmem((I - 1, T, high, 128), F32),
            vmem((T, high, 128), F32),
            vmem((T, R, high, 128), F32),
            vmem((rows, 1), F32),
            vmem((rows, D), F32),
            vmem((rows, D), F32),
            vmem((rows, D), BF),
            vmem((rows, D), BF),
            vmem((D, rows), BF),
            vmem((rows, D), BF),
            vmem((D, rows), BF),
            vmem((rows, D), F32),
            vmem((rows, D), F32),
            vmem((2, D, wide_f), BF),
            dma((remote,)),
            dma((remote,)),
            dma((11 + nq,)),
            dma((R * T,)),
            dma((R * T,)),
            dma((2,)),
        ],
        compiler_params=pltpu.CompilerParams(
            collective_id=0, has_side_effects=True, vmem_limit_bytes=LIMIT
        ),
        name="forward",
    )(frames, cotangent, time, lengths, *weights)


def attend_back_block(
    rows, cb, weight, wide, db_ref, xm_turned, db_turned, cos_ref, sin_ref, mask_ref,
    q_ref, k_ref, v_ref, att_ref, lse_ref, store,
):
    d_att = nn(db_ref[...], weight(3)).astype(BF)
    store(3, nn(db_turned[...], att_ref[...]))
    ones = first_lane(rows)
    factor = HEAD_DIM**-0.5
    dqs, dks, dvs = [], [], []
    for p in range(cb // 128):
        lanes = slice(p * 128, p * 128 + 128)
        q2, k2, v2 = q_ref[:, lanes], k_ref[:, lanes], v_ref[:, lanes]
        k_long = jnp.concatenate([k2, mask_ref[...]], axis=1)
        k_turned = k2.T
        dq_parts, ds_all, p_all = [], [], []
        q_heads, d_heads = head_split(q2), head_split(d_att[:, lanes])
        for h in range(2):
            scores = nt(k_long, jnp.concatenate([q_heads[h], ones], axis=1))
            probs = jnp.exp(scores - lse_ref[pl.ds(2 * p + h, 1), :])
            d_probs = nt(v2, d_heads[h])
            row_dot = jnp.sum(probs * d_probs, axis=0, keepdims=True)
            d_scores = (probs * (d_probs - row_dot)).astype(BF)
            dq_parts.append(nn(k_turned[h * HEAD_DIM : (h + 1) * HEAD_DIM], d_scores))
            ds_all.append(d_scores)
            p_all.append(probs.astype(BF))
        dk2 = nn(jnp.concatenate(ds_all, axis=1), jnp.concatenate(q_heads, axis=0))
        dv2 = nn(jnp.concatenate(p_all, axis=1), jnp.concatenate(d_heads, axis=0))
        dq2 = jnp.concatenate(dq_parts, axis=0).T * factor
        dqs.append(
            (dq2 * cos_ref[0:rows, :] - swap_pairs(dq2) * sin_ref[0:rows, :]).astype(BF)
        )
        dks.append((dk2 * cos_ref[...] - swap_pairs(dk2) * sin_ref[...]).astype(BF))
        dvs.append(dv2.astype(BF))
    dq, dk, dv = (jnp.concatenate(v, axis=1) for v in (dqs, dks, dvs))
    store(0, nn(xm_turned[:, 0:rows], dq))
    store(1, nn(xm_turned[...], dk))
    store(2, nn(xm_turned[...], dv))
    return nt(jnp.concatenate([dk, dv], axis=1), wide(1, 3)), nt(dq, weight(0))


def back_kernel(
    S, T, I, cb,
    layer, all_a, grad_f, k_all, v_all, xm_all, dmid, frames,
    q_ref, att_ref, lse_ref, mod_ref, db_ref, dmod_ref,
    cos_ref, sin_ref, mask_ref,
    layer_out, grads_out, rows_out, sum_a, sum_f,
    *scratch,
):
    nh, nq = grad_f.shape[0], all_a.shape[0]
    (xm_turned, db_turned, dx_sum, dx_ref, near, far, d_rows, group_in, group_sum, ga_ref,
     w_stage, k_stage, v_stage, in_sem, send, recv, local, row_send, row_recv) = scratch[:19]
    rest = scratch[19:]
    p = Place(S, T, I)
    wires = Wires(send, recv, local)
    Q, _, rows, _ = xm_all.shape
    L = Q * 2 * rows
    steps, slots = nq * T, w_stage.shape[0]

    def fetch(n):
        j, t = divmod(n, T)
        slot = n % slots
        copies = [
            pltpu.make_async_copy(all_a.at[j, t], w_stage.at[slot], in_sem.at[0, slot]),
            pltpu.make_async_copy(k_all.at[n], k_stage.at[slot], in_sem.at[1, slot]),
            pltpu.make_async_copy(v_all.at[n], v_stage.at[slot], in_sem.at[2, slot]),
        ]
        for copy in copies:
            copy.start()
        return copies

    xm_copy = wires.move(xm_all, dx_ref)
    fetched = fetch(0)
    greet(p)
    chunks_f, chunks_a = [], []
    for j in range(nh):
        own, landing, rest = rest[0], rest[1:7], rest[7:]
        chunks_f.append(Reduce(p, wires, grad_f.at[j], sum_f.at[j], own, 0, 2, landing))
    for j in range(nq):
        for h in (1, 0):
            landing, rest = rest[:6], rest[6:]
            cols = pl.ds(2 * cb * h, 2 * cb)
            g = ga_ref.at[j, :, :, :, :, :, cols]
            chunks_a.append(Reduce(p, wires, g, sum_a.at[j, :, cols], g, p.c, 3 if j == 1 else 2, landing))
    chunks = chunks_f + chunks_a

    def upto(m, phase):
        if m < len(chunks):
            chunks[m].upto(phase)

    upto(0, 0)
    if nh > 1:
        upto(1, 0)
    xm_copy.wait()
    db_turned[...] = db_ref[...].T
    upto(0, 1)
    for m in range(2, nh):
        upto(m, 0)
    xm_turned[...] = dx_ref[...].reshape(L, D).T
    for m in range(1, nh):
        upto(m, 1)
    layer_own, layer_in = swap_items(p, wires, layer, layer_out)

    between = {}
    if nq == 2 and T == 2 and nh == 4:
        between = {
            0: lambda: (upto(0, 2), upto(1, 2)),
            1: lambda: (upto(4, 0), upto(5, 0), upto(2, 2), upto(3, 2), upto(4, 1), upto(5, 1)),
            2: lambda: (upto(0, 3), upto(1, 3), upto(2, 3), upto(3, 3)),
        }

    for n in range(steps):
        j, t = divmod(n, T)
        slot = n % slots
        coming = fetch(n + 1) if slots == 2 and n + 1 < steps else None
        for copy in fetched:
            copy.wait()
        fetched = coming

        def store(b, value):
            ga_ref[j, t, :, :, :, :, b * cb : (b + 1) * cb] = value.astype(BF).reshape(
                ga_ref.shape[2:6] + (cb,)
            )

        dx, dx_own = attend_back_block(
            rows, cb,
            lambda b: w_stage[slot, :, b * cb : (b + 1) * cb],
            lambda b, e: w_stage[slot, :, b * cb : e * cb],
            db_ref, xm_turned, db_turned, cos_ref, sin_ref, mask_ref,
            q_ref.at[n], k_stage.at[slot], v_stage.at[slot], att_ref.at[n], lse_ref.at[n], store,
        )
        if n == 0:
            dx_sum[...] = dx
        else:
            dx_sum[...] += dx
        dx_sum[0:rows, :] += dx_own
        if slots == 1 and n + 1 < steps:
            fetched = fetch(n + 1)
        if n < steps - 1:
            between.get(n, tuple)()

    dx_ref[...] = dx_sum[...].astype(BF).reshape(dx_ref.shape)
    dmid_copy = wires.move(dmid, dx_sum.at[pl.ds(rows, rows)])
    fl = layer.shape[1]
    frame_copies = [
        wires.move(frames.at[n], xm_turned.at[pl.ds(n * fl, fl), pl.ds(0, D)]) for n in range(I)
    ]
    core = wires.push(dx_ref.at[:, 1], near, p.group(0, 1 - p.c))
    last = len(chunks) - 1
    upto(last - 1, 0)
    upto(last, 0)
    core.wait_recv()
    across = []
    for k in range(1, Q):
        dx_ref[k, 0] = dx_ref[k, 0] + near[k]
        across.append(wires.push(dx_ref.at[k, 0], far.at[k - 1], p.group(k)))
    for m in range(last - 1):
        upto(m, 2)
    upto(last - 1, 1)
    upto(last, 1)
    for m in range(nh):
        upto(m, 4)

    for copy in frame_copies:
        copy.wait()
    normed, inverse = layer_stats(xm_turned[0:rows, 0:D].astype(F32))
    d_mod = dx_sum[0:rows, :] + near[0].astype(F32)
    for k in range(1, Q):
        across[k - 1].wait_recv()
        d_mod = d_mod + far[k - 1].astype(F32)
    incoming = layer_back(normed, inverse, d_mod * (1.0 + mod_ref[1:2, :]))
    dmid_copy.wait()
    dx_ref[0, 0] = (dx_sum[rows : 2 * rows, :] + incoming).astype(BF)
    grads_own, grads_in = swap_items(
        p, wires, lambda n: dx_ref.at[0, 0, pl.ds(n * fl, fl)], grads_out
    )
    high = d_rows.shape[1]
    first = [
        jnp.sum(d_mod, axis=0, keepdims=True),
        jnp.sum(d_mod * normed.astype(BF).astype(F32), axis=0, keepdims=True),
    ]
    for t in range(T):
        for n in range(high):
            row, col = divmod((t * high + n) * 128, D)
            value = first[row] if row < 2 else dmod_ref[row : row + 1, :]
            d_rows[t, n : n + 1, :] = value[:, col : col + 128]
    group_in[p.t, p.r] = d_rows[p.t]
    group_done = spread_group(p, row_send, row_recv, lambda t: d_rows.at[t], group_in)
    for m in range(last - 1):
        upto(m, 3)
    group_done()
    for t in range(T):
        group_sum[t] = jnp.sum(group_in[t], axis=0)
    rows_own = wires.move(group_sum, rows_out.at[p.i])
    line = []
    for k in range(1, I):
        other = lax.rem(p.i + k, I)
        line.append(wires.push(group_sum, rows_out.at[p.i], (other * p.R + p.r, p.t)))
    upto(last - 1, 2)
    upto(last, 2)
    for m in range(last - 1):
        upto(m, 4)
    upto(last - 1, 3)
    upto(last, 3)
    upto(last - 1, 4)
    upto(last, 4)
    for m in range(last + 1):
        upto(m, 5)
    landed(line)
    for own in (grads_own, layer_own, rows_own):
        own.wait()
    landed(grads_in)
    landed(layer_in)
    wires.close()


def back_call(
    S, T, I, cb, layer, all_a, grad_f, k, v, xm, d_mid, frames,
    q, att, lse, mod, d_branch, d_mod, cosine, sine, mask,
):
    nq, ca = all_a.shape[0], all_a.shape[3]
    nh, cf = grad_f.shape[0], grad_f.shape[6]
    rs = grad_f.shape[5]
    Z, Q, rows = S // 4, xm.shape[0], xm.shape[2]
    L = Q * 2 * rows
    high = 6 * D // T // 128
    slots = 2 if L <= 1024 else 1
    remote = 3 * (I - 1) + (2 * nq + nh) * (Z + 2 * T + 2) + Q
    R = S // I
    shape = jax.ShapeDtypeStruct
    dma = pltpu.SemaphoreType.DMA
    scratch = [
        pltpu.VMEM((D, L), BF),
        pltpu.VMEM((D, rows), BF),
        pltpu.VMEM((L, D), F32),
        pltpu.VMEM((Q, 2, rows, D), BF),
        pltpu.VMEM((Q, rows, D), BF),
        pltpu.VMEM((Q - 1, rows, D), BF),
        pltpu.VMEM((T, high, 128), F32),
        pltpu.VMEM((T, R, high, 128), F32),
        pltpu.VMEM((T, high, 128), F32),
        pltpu.VMEM((nq, T, Z, 2, 2, rs, ca), BF),
        pltpu.VMEM((slots, D, ca), BF),
        pltpu.VMEM((slots, L, cb), BF),
        pltpu.VMEM((slots, L, cb), BF),
        dma((3, slots)),
        dma((remote,)),
        dma((remote,)),
        dma((5 + nh + I,)),
        dma((R * T,)),
        dma((R * T,)),
    ]
    for _ in range(nh):
        scratch += [pltpu.VMEM((T, Z, 2, 1, rs, cf), BF)] + Reduce.landing(T, Z, rs, cf, 2)
    for j in range(2 * nq):
        scratch += Reduce.landing(T, Z, rs, ca // 2, 3 if j // 2 == 1 else 2)
    return pl.pallas_call(
        partial(back_kernel, S, T, I, cb),
        out_shape=(
            shape(layer.shape, BF),
            shape(layer.shape, BF),
            shape((I, T, high, 128), F32),
            shape((nq, rs, ca), F32),
            shape((nh, rs, cf), F32),
        ),
        in_specs=[ANY] * 8 + [VMEM] * 9,
        out_specs=(ANY, ANY, ANY, VMEM, VMEM),
        scratch_shapes=scratch,
        compiler_params=pltpu.CompilerParams(
            collective_id=1, has_side_effects=True, vmem_limit_bytes=LIMIT
        ),
        name="backward",
    )(
        layer, all_a, grad_f, k, v, xm, d_mid, frames,
        q, att, lse, mod, d_branch, d_mod, cosine, sine, mask,
    )


def layer_stats(values):
    center = values - jnp.mean(values, axis=-1, keepdims=True)
    inverse = lax.rsqrt(jnp.mean(center * center, axis=-1, keepdims=True) + EPSILON)
    return center * inverse, inverse


def layer_back(normed, inverse, incoming):
    return inverse * (
        incoming
        - jnp.mean(incoming, axis=-1, keepdims=True)
        - normed * jnp.mean(incoming * normed, axis=-1, keepdims=True)
    )


def finish_kernel(
    S, T, I, micro, time_ref, rows_ref, sum_a, sum_f, layer_in, grads_in,
    layer_ref, grads_ref, gq_ref, gk_ref, gv_ref, go_ref, gu_ref, gd_ref, gm_ref, items_ref,
):
    p = Place(S, T, I)
    nq, rs, wide_a = sum_a.shape
    nh, _, wide_f = sum_f.shape
    cb, hb = wide_a // 4, wide_f // 2
    layer_ref[...] = layer_in[...]
    grads_ref[...] = grads_in[...]
    for j in range(nq):
        for b, ref in enumerate((gq_ref, gk_ref, gv_ref, go_ref)):
            ref[:, j * cb : (j + 1) * cb] = sum_a[j, :, b * cb : (b + 1) * cb]
    for j in range(nh):
        gu_ref[:, j * hb : (j + 1) * hb] = sum_f[j, :, 0:hb]
        gd_ref[:, j * hb : (j + 1) * hb] = sum_f[j, :, hb : 2 * hb]
    high = rows_ref.shape[2]
    rows_own = I // micro
    for item in range(I * T):
        m, b = divmod(item, rows_own * T)
        i, t = m * rows_own + b % rows_own, b // rows_own
        for n in range(high):
            items_ref[item : item + 1, n * 128 : (n + 1) * 128] = rows_ref[i, t, n : n + 1, :]
    silu = own_columns(p, time_ref[...], rs).astype(F32)
    gm_ref[...] = lax.dot_general(
        silu, items_ref[...], (((0,), (0,)), ((), ())), precision=HIGHEST,
        preferred_element_type=F32,
    )


def finish_call(S, T, I, micro, time, rows, sum_a, sum_f, layer, grads, weights):
    shape = jax.ShapeDtypeStruct
    return pl.pallas_call(
        partial(finish_kernel, S, T, I, micro),
        out_shape=(shape(layer.shape, BF), shape(grads.shape, BF))
        + tuple(shape(w.shape, F32) for w in weights),
        in_specs=[VMEM] * 6,
        out_specs=(VMEM,) * 9,
        scratch_shapes=[pltpu.VMEM((I * T, weights[6].shape[1]), F32)],
        compiler_params=pltpu.CompilerParams(vmem_limit_bytes=LIMIT),
        name="finish",
    )(time, rows, sum_a, sum_f, layer, grads)


def per_device(
    S, T, frames, time_embed, lengths, w_query, w_key, w_value, w_out, w_up, w_down, w_mod, out_grad
):
    micro, rows_own, fl, _ = frames.shape
    batch = lengths.shape[1]
    I = micro * rows_own
    rs = w_query.shape[0]
    cb = min(256, w_query.shape[1])
    hb = min(256, w_up.shape[1])
    time = time_embed
    weights = (w_query, w_key, w_value, w_out.T, w_up, w_down.T, w_mod)
    (
        all_a, xm, q, k, v, att, lse, grad_f, cosine, sine, mask,
        frames_in, mod, layer, d_mid, d_branch, d_rows,
    ) = front_call(
        S, T, I, cb, hb, frames.reshape(I, fl, D), out_grad.reshape(I, fl, D), time, lengths, weights
    )
    layer_out, grad_input, rows_in, sum_a, sum_f = back_call(
        S, T, I, cb, layer, all_a.reshape(all_a.shape[:2] + (D, 4 * cb)),
        grad_f.reshape((grad_f.shape[0], T, S // 4, 2, 2, rs, 2 * hb)), k, v, xm, d_mid,
        frames_in, q, att, lse, mod, d_branch, d_rows, cosine, sine, mask,
    )
    outs = finish_call(S, T, I, micro, time, rows_in, sum_a, sum_f, layer_out, grad_input, weights)
    layer_out, grad_input, g_query, g_key, g_value, g_out, g_up, g_down, g_mod = outs
    return (
        layer_out.reshape(frames.shape), grad_input.reshape(frames.shape),
        g_query, g_key, g_value, g_out.T, g_up, g_down.T, g_mod,
    )


def solution(mesh):
    S, T = mesh.shape["seq"], mesh.shape["tp"]
    rows = P(None, "tp", "seq", None)
    return jax.shard_map(
        partial(per_device, S, T),
        mesh=mesh,
        in_specs=(
            rows,
            P(),
            P(),
            P("seq", "tp"),
            P("seq", "tp"),
            P("seq", "tp"),
            P("tp", "seq"),
            P("seq", "tp"),
            P("tp", "seq"),
            P("seq", "tp"),
            rows,
        ),
        out_specs=(
            rows,
            rows,
            P("seq", "tp"),
            P("seq", "tp"),
            P("seq", "tp"),
            P("tp", "seq"),
            P("seq", "tp"),
            P("tp", "seq"),
            P("seq", "tp"),
        ),
        check_vma=False,
    )
```

```python
from functools import partial
import math

import jax
import jax.numpy as jnp
from jax import lax
from jax.experimental import pallas as pl
from jax.experimental.pallas import tpu as pltpu
from jax.sharding import PartitionSpec as P

D = 1024
HEAD_DIM = 64
EPSILON = 1e-06
NEGATIVE = -1e30
BF = jnp.bfloat16
F32 = jnp.float32
HIGHEST = lax.Precision.HIGHEST
MESH = pl.DeviceIdType.MESH
ANY = pl.BlockSpec(memory_space=pl.ANY)
VMEM = pl.BlockSpec(memory_space=pltpu.VMEM)
LIMIT = 62 * 1024 * 1024


def nn(a, b):
    return lax.dot_general(a, b, (((1,), (0,)), ((), ())), preferred_element_type=F32)


def nt(a, b):
    return lax.dot_general(a, b, (((1,), (1,)), ((), ())), preferred_element_type=F32)


class Place:
    def __init__(self, S, T, I):
        self.S, self.T, self.I = S, T, I
        self.Z, self.R = S // 4, S // I
        self.Q = self.R // 2
        self.s, self.t = lax.axis_index("seq"), lax.axis_index("tp")
        self.z = lax.div(self.s, 4)
        self.x = lax.rem(lax.div(self.s, 2), 2)
        self.c = lax.rem(self.s, 2)
        self.i = lax.div(self.s, self.R)
        self.r = lax.rem(self.s, self.R)
        self.q = lax.div(self.r, 2)

    def at(self, z=None, x=None, c=None, t=None):
        z = self.z if z is None else z
        x = self.x if x is None else x
        c = self.c if c is None else c
        t = self.t if t is None else t
        return ((z * 2 + x) * 2 + c, t)

    def tp(self, k):
        return (self.s, lax.rem(self.t + k, self.T))

    def zs(self, k):
        return lax.rem(self.z + k, self.Z)

    def group(self, k, c=None):
        c = self.c if c is None else c
        return (self.i * self.R + lax.rem(self.q + k, self.Q) * 2 + c, self.t)


class Wires:
    def __init__(self, send, recv, local):
        self.send, self.recv, self.local = send, recv, local
        self.remote_count = self.local_count = 0
        self.sent = []

    def push(self, src, dst, device):
        n = self.remote_count
        self.remote_count += 1
        copy = pltpu.make_async_remote_copy(
            src_ref=src,
            dst_ref=dst,
            send_sem=self.send.at[n],
            recv_sem=self.recv.at[n],
            device_id=device,
            device_id_type=MESH,
        )
        copy.start()
        self.sent.append(copy)
        return copy

    def move(self, src, dst):
        n = self.local_count
        self.local_count += 1
        copy = pltpu.make_async_copy(src, dst, self.local.at[n])
        copy.start()
        return copy

    def close(self):
        for copy in self.sent:
            copy.wait_send()


def landed(copies):
    for copy in copies:
        copy.wait_recv()


def loop_group(place, first, body):
    total = place.R * place.T
    me = place.r * place.T + place.t

    def step(d, carry):
        other = lax.rem(me + d, total)
        body(d, place.i * place.R + lax.div(other, place.T), lax.rem(other, place.T))
        return carry

    lax.fori_loop(first, total, step, 0)


def greet(place):
    barrier = pltpu.get_barrier_semaphore()

    def signal(d, s, t):
        pl.semaphore_signal(barrier, inc=1, device_id=(s, t), device_id_type=MESH)

    for k in range(1, place.Z):
        signal(k, *place.at(z=place.zs(k)))
    loop_group(place, 1, signal)
    pl.semaphore_wait(barrier, place.Z - 1 + place.R * place.T - 1)


def spread_group(place, send, recv, src_of, dst):
    def copy(d, s, t):
        return pltpu.make_async_remote_copy(
            src_ref=src_of(t),
            dst_ref=dst.at[place.t, place.r],
            send_sem=send.at[d],
            recv_sem=recv.at[d],
            device_id=(s, t),
            device_id_type=MESH,
        )

    loop_group(place, 1, lambda d, s, t: copy(d, s, t).start())
    return lambda: loop_group(place, 1, lambda d, s, t: copy(d, s, t).wait())


class Phased:
    done = 0

    def upto(self, phase):
        while self.done <= phase:
            getattr(self, f"phase{self.done}")()
            self.done += 1


def split_rows(rs, quarters):
    upper = rs * quarters // 4 if rs * quarters // 4 % 16 == 0 else rs // 2
    return pl.ds(0, upper), pl.ds(upper, rs - upper)


class Gather(Phased):
    def __init__(self, place, wires, dst, quarters, paired):
        self.p, self.w, self.dst = place, wires, dst
        self.paired = paired and place.Z == 4
        self.upper, self.lower = split_rows(dst.shape[4], quarters)

    def phase0(self):
        p, w, dst = self.p, self.w, self.dst
        own = dst.at[0, p.z, p.x, p.c]
        self.across = []
        if self.paired:
            self.across = [w.push(own, own, p.at(z=p.zs(2)))]
            near = p.z + 1 - 2 * lax.rem(p.z, 2)
            self.along = [w.push(own, own, p.at(z=near))]
        else:
            self.along = [w.push(own, own, p.at(z=p.zs(k))) for k in range(1, p.Z)]

    def pass_on(self):
        p, w, dst = self.p, self.w, self.dst
        landed(self.across)
        if self.paired and self.across:
            near = p.z + 1 - 2 * lax.rem(p.z, 2)
            far = dst.at[0, p.zs(2), p.x, p.c]
            self.along.append(w.push(far, far, p.at(z=near)))
        self.across = []

    def phase1(self):
        p, w, dst = self.p, self.w, self.dst
        self.pass_on()
        landed(self.along)
        line = dst.at[0, :, p.x, p.c]
        self.sides = [
            w.push(
                dst.at[0, :, p.x, p.c, self.upper],
                dst.at[0, :, p.x, p.c, self.upper],
                p.at(x=1 - p.x),
            )
        ]
        for k in range(1, p.T):
            self.sides.append(
                w.push(
                    dst.at[0, :, p.x, p.c, self.lower],
                    dst.at[p.T - k, :, p.x, p.c, self.lower],
                    p.tp(k),
                )
            )
        self.cores = [w.push(line, line, p.at(c=1 - p.c))]

    def phase2(self):
        p, w, dst = self.p, self.w, self.dst
        landed(self.sides)
        self.last = []
        for k in range(1, p.T):
            self.last.append(
                w.push(
                    dst.at[0, :, :, p.c, self.upper],
                    dst.at[p.T - k, :, :, p.c, self.upper],
                    p.tp(k),
                )
            )
        part = dst.at[:, :, p.x, p.c, self.lower]
        self.last.append(w.push(part, part, p.at(x=1 - p.x)))
        part = dst.at[0, :, 1 - p.x, p.c, self.upper]
        self.cores.append(w.push(part, part, p.at(c=1 - p.c)))
        part = dst.at[pl.ds(1, p.T - 1), :, p.x, p.c, self.lower]
        self.cores.append(w.push(part, part, p.at(c=1 - p.c)))

    def phase3(self):
        p, w, dst = self.p, self.w, self.dst
        landed(self.last)
        part = dst.at[pl.ds(1, p.T - 1), :, :, p.c, self.upper]
        self.cores.append(w.push(part, part, p.at(c=1 - p.c)))
        part = dst.at[:, :, 1 - p.x, p.c, self.lower]
        self.cores.append(w.push(part, part, p.at(c=1 - p.c)))

    def phase4(self):
        landed(self.cores)


class Reduce(Phased):
    def __init__(self, place, wires, src, out, own, core_at, quarters, landing):
        self.p, self.w, self.src, self.out = place, wires, src, out
        self.own, self.core_at = own, core_at
        self.core, self.y_up, self.x_low, self.x_up, self.y_low, self.z_in = landing
        self.upper, self.lower = split_rows(own.shape[4], quarters)

    @staticmethod
    def landing(T, Z, rs, C, quarters):
        upper, lower = (part.size for part in split_rows(rs, quarters))
        return [
            pltpu.VMEM((T, Z, 2, rs, C), BF),
            pltpu.VMEM((T - 1, Z, 2, upper, C), BF),
            pltpu.VMEM((T, Z, lower, C), BF),
            pltpu.VMEM((Z, upper, C), BF),
            pltpu.VMEM((T - 1, Z, lower, C), BF),
            pltpu.VMEM((Z - 1, rs, C), BF),
        ]

    def phase0(self):
        p, w, src = self.p, self.w, self.src
        self.mine = None
        if self.own is not src:
            self.mine = w.move(src.at[:, :, :, pl.ds(p.c, 1)], self.own)
        self.pair = [w.push(src.at[:, :, :, 1 - p.c], self.core, p.at(c=1 - p.c))]

    def phase1(self):
        p, w, own, c = self.p, self.w, self.own, self.core_at
        if self.mine is not None:
            self.mine.wait()
        landed(self.pair)

        def add(n, carry):
            k, z = lax.div(n, p.Z), lax.rem(n, p.Z)
            for x in range(2):
                own[k, z, x, c] = own[k, z, x, c] + self.core[k, z, x]
            return carry

        lax.fori_loop(0, p.T * p.Z, add, 0)
        self.sides = [
            w.push(own.at[k, :, :, c, self.upper], self.y_up.at[k - 1], p.tp(k))
            for k in range(1, p.T)
        ]
        self.sides.append(
            w.push(own.at[:, :, 1 - p.x, c, self.lower], self.x_low, p.at(x=1 - p.x))
        )

    def phase2(self):
        p, w, own, c = self.p, self.w, self.own, self.core_at
        landed(self.sides)

        def add(z, carry):
            for x in range(2):
                total = own[0, z, x, c, self.upper].astype(F32)
                for k in range(1, p.T):
                    total = total + self.y_up[k - 1, z, x].astype(F32)
                own[0, z, x, c, self.upper] = total.astype(BF)
            for k in range(p.T):
                own[k, z, p.x, c, self.lower] = own[k, z, p.x, c, self.lower] + self.x_low[k, z]
            return carry

        lax.fori_loop(0, p.Z, add, 0)
        self.last = [w.push(own.at[0, :, 1 - p.x, c, self.upper], self.x_up, p.at(x=1 - p.x))]
        for k in range(1, p.T):
            self.last.append(
                w.push(own.at[k, :, p.x, c, self.lower], self.y_low.at[k - 1], p.tp(k))
            )

    def phase3(self):
        p, w, own, c = self.p, self.w, self.own, self.core_at
        landed(self.last)

        def add(z, carry):
            own[0, z, p.x, c, self.upper] = own[0, z, p.x, c, self.upper] + self.x_up[z]
            total = own[0, z, p.x, c, self.lower].astype(F32)
            for k in range(1, p.T):
                total = total + self.y_low[k - 1, z].astype(F32)
            own[0, z, p.x, c, self.lower] = total.astype(BF)
            return carry

        lax.fori_loop(0, p.Z, add, 0)
        if p.Z == 4:
            near = p.z + 1 - 2 * lax.rem(p.z, 2)
            self.along = [
                w.push(own.at[0, near, p.x, c], self.z_in.at[0], p.at(z=near)),
                w.push(own.at[0, 3 - p.z, p.x, c], self.z_in.at[1], p.at(z=near)),
            ]
        else:
            self.along = [
                w.push(own.at[0, p.zs(k), p.x, c], self.z_in.at[k - 1], p.at(z=p.zs(k)))
                for k in range(1, p.Z)
            ]

    def phase4(self):
        p, w, own, c = self.p, self.w, self.own, self.core_at
        landed(self.along)
        self.across = []
        if p.Z == 4:
            far = p.zs(2)
            own[0, far, p.x, c] = own[0, far, p.x, c] + self.z_in[1]
            self.across.append(w.push(own.at[0, far, p.x, c], self.z_in.at[2], p.at(z=far)))

    def phase5(self):
        p = self.p
        landed(self.across)
        blocks = (0, 2) if p.Z == 4 else range(p.Z - 1)
        total = self.own[0, p.z, p.x, self.core_at].astype(F32)
        for k in blocks:
            total = total + self.z_in[k].astype(F32)
        self.out[...] = total


def swap_items(place, wires, src, dst):
    p = place
    block = src if callable(src) else lambda n: src.at[n]
    own = wires.move(block(p.i), dst.at[p.i])
    copies = []
    for k in range(1, p.I):
        other = lax.rem(p.i + k, p.I)
        copies.append(wires.push(block(other), dst.at[p.i], (other * p.R + p.r, p.t)))
    return own, copies


def swap_pairs(v):
    lane = lax.broadcasted_iota(jnp.int32, v.shape, 1)
    return jnp.where(lax.rem(lane, 2) == 0, pltpu.roll(v, 127, 1), pltpu.roll(v, 1, 1))


def head_split(v):
    lane = lax.broadcasted_iota(jnp.int32, v.shape, 1)
    zero = jnp.zeros_like(v)
    return jnp.where(lane < HEAD_DIM, v, zero), jnp.where(lane < HEAD_DIM, zero, v)


def first_lane(rows):
    lane = lax.broadcasted_iota(jnp.int32, (rows, 128), 1)
    return jnp.where(lane == 0, 1.0, 0.0).astype(BF)


def attend_block(rows, cb, xm, weight, cos_ref, sin_ref, mask_ref, q_ref, k_ref, v_ref, att_ref, lse_ref):
    q_lin = nn(xm[0:rows, :], weight(0))
    k_lin = nn(xm, weight(1))
    v_ref[...] = nn(xm, weight(2)).astype(BF)
    ones = first_lane(rows)
    factor = HEAD_DIM**-0.5
    for p in range(cb // 128):
        lanes = slice(p * 128, p * 128 + 128)
        q2, k2 = q_lin[:, lanes], k_lin[:, lanes]
        q2 = (q2 * cos_ref[0:rows, :] + swap_pairs(q2) * sin_ref[0:rows, :]).astype(BF)
        q2 = q2 * jnp.asarray(factor, BF)
        k2 = (k2 * cos_ref[...] + swap_pairs(k2) * sin_ref[...]).astype(BF)
        q_ref[:, lanes] = q2
        k_ref[:, lanes] = k2
        k_long = jnp.concatenate([k2, mask_ref[...]], axis=1)
        v_turned = v_ref[:, lanes].T
        outs = []
        for h, q1 in enumerate(head_split(q2)):
            scores = nt(k_long, jnp.concatenate([q1, ones], axis=1))
            highest = jnp.max(scores, axis=0, keepdims=True)
            unnormed = jnp.exp(scores - highest)
            total = jnp.sum(unnormed, axis=0, keepdims=True)
            probs = (unnormed * (1.0 / total)).astype(BF)
            lse_ref[pl.ds(2 * p + h, 1), :] = highest + jnp.log(total)
            outs.append(nn(v_turned[h * HEAD_DIM : (h + 1) * HEAD_DIM], probs))
        att_ref[:, lanes] = jnp.concatenate(outs, axis=0).T.astype(BF)
    return nt(att_ref[...], weight(3))


def own_columns(place, time, rs):
    time = jnp.concatenate([time[m] for m in range(time.shape[0])], axis=0)
    silu = (time / (1.0 + jnp.exp(-time))).astype(BF)
    feature = lax.broadcasted_iota(jnp.int32, (D, rs), 0)
    chosen = feature == lax.broadcasted_iota(jnp.int32, (D, rs), 1) + place.s * rs
    return nn(silu, jnp.where(chosen, 1.0, 0.0).astype(BF)).astype(BF)


def fill_tables(place, fl, length, cos_ref, sin_ref, mask_ref, live_ref):
    p = place
    lane = lax.broadcasted_iota(jnp.int32, (fl, 128), 1)
    row = lax.broadcasted_iota(jnp.int32, (fl, 128), 0)
    column = lax.div(lax.rem(lane, HEAD_DIM), 2).astype(F32)
    inverse = jnp.exp(column * (-2.0 * math.log(10000.0) / HEAD_DIM))
    sign = jnp.where(lax.rem(lane, 2) == 0, -1.0, 1.0)
    for g in range(p.R):
        r = lax.rem(p.q + g // 2, p.Q) * 2 + lax.rem(p.c + g % 2, 2)
        for n in range(p.I):
            at = pl.ds((g * p.I + n) * fl, fl)
            pos = row + fl * (n * p.R + r)
            angles = pos.astype(F32) * inverse
            cos_ref[at, :] = jnp.cos(angles)
            sin_ref[at, :] = jnp.sin(angles) * sign
            alive = pos < length
            mask_ref[at, :] = jnp.where((lane == 0) & ~alive, NEGATIVE, 0.0).astype(BF)
            if g == 0:
                live_ref[at, :] = jnp.where(alive, 1.0, 0.0)[:, 0:1]


def front_kernel(
    S, T, I, cb, hb,
    frames, cotangent, time_ref, lengths_ref, wq_ref, wk_ref, wv_ref, wo_ref, wu_ref, wd_ref, wm_ref,
    all_a, xm_out, q_out, k_out, v_out, att_out, lse_out, grad_f, cos_out, sin_out, mask_out,
    frames_in, mod_ref, layer_ref, dmid_ref, dbranch_ref, dmod_ref,
    xm_ref, q_ref, k_ref, v_ref, att_ref, lse_ref, cos_ref, sin_ref, mask_ref,
    a_ref, f_ref, cot_in, parts, line_in, line_sum, parts_in, live_ref, branch_ref, mid_ref,
    normed_ref, mf_ref, mf_turned, db_ref, db_turned, out_sum, dmf_sum, stage,
    send, recv, local, row_send, row_recv, out_sem,
):
    p = Place(S, T, I)
    wires = Wires(send, recv, local)
    nq, nh = a_ref.shape[0], f_ref.shape[0]
    fl, rs = frames.shape[1], wq_ref.shape[0]
    rows, L = I * fl, I * fl * p.R
    micro, batch = lengths_ref.shape
    rows_own = I // micro
    for j in range(nq):
        cols = slice(j * cb, (j + 1) * cb)
        blocks = (wq_ref[:, cols], wk_ref[:, cols], wv_ref[:, cols], wo_ref[:, cols])
        a_ref[j, 0, p.z, p.x, p.c] = jnp.concatenate(blocks, axis=1)
    greet(p)
    chunks_a = [Gather(p, wires, a_ref.at[j], 2, False) for j in range(nq)]
    chunks_f = [Gather(p, wires, f_ref.at[j], 2, True) for j in range(nh)]
    chunks = chunks_a + chunks_f

    def pass_on(m):
        if m < len(chunks):
            chunks[m].pass_on()

    def upto(m, phase):
        if m < len(chunks):
            chunks[m].upto(phase)

    upto(0, 0)
    product = nn(own_columns(p, time_ref[...], rs), wm_ref[...])
    high = parts.shape[2]
    for item in range(micro * batch):
        m, b = divmod(item, batch)
        t, own = divmod(b, rows_own)
        for n in range(high):
            parts[t, m * rows_own + own, n : n + 1, :] = product[
                item : item + 1, n * 128 : (n + 1) * 128
            ]
    line = []
    for k in range(1, I):
        other = lax.rem(p.i + k, I)
        line.append(
            wires.push(parts.at[:, other], line_in.at[k - 1], (other * p.R + p.r, p.t))
        )
    for j in range(nh):
        cols = slice(j * hb, (j + 1) * hb)
        f_ref[j, 0, p.z, p.x, p.c] = jnp.concatenate([wu_ref[:, cols], wd_ref[:, cols]], axis=1)
    upto(0, 1)
    frames_own, frames_got = swap_items(p, wires, frames, frames_in)
    landed(line)
    for t in range(T):
        total = parts[t, p.i]
        for k in range(1, I):
            total = total + line_in[k - 1, t]
        line_sum[t] = total
    parts_in[p.t, p.r] = line_sum[p.t]
    group_done = spread_group(p, row_send, row_recv, lambda t: line_sum.at[t], parts_in)
    upto(0, 2)
    length = lengths_ref[lax.div(p.i, rows_own), p.t * rows_own + lax.rem(p.i, rows_own)]
    fill_tables(p, fl, length, cos_ref, sin_ref, mask_ref, live_ref)
    group_done()
    mod_ref[...] = jnp.zeros_like(mod_ref)
    for t in range(T):
        total = jnp.sum(parts_in[t], axis=0).astype(BF).astype(F32)
        for n in range(high):
            row, col = divmod((t * high + n) * 128, D)
            mod_ref[row : row + 1, col : col + 128] = total[n : n + 1]
    frames_own.wait()
    landed(frames_got)
    upto(1, 0)
    frame_rows = frames_in[...].reshape(rows, D).astype(F32)
    normed, _ = layer_stats(frame_rows)
    low = normed.astype(BF).astype(F32)
    xm_ref[0, 0] = (low * (1.0 + mod_ref[1:2, :]) + mod_ref[0:1, :]).astype(BF)
    sibling = p.group(0, 1 - p.c)
    across = [wires.push(xm_ref.at[0, 0], xm_ref.at[p.Q - k, 0], p.group(k)) for k in range(1, p.Q)]
    cores = [wires.push(xm_ref.at[0, 0], xm_ref.at[0, 1], sibling)]
    upto(0, 3)
    pass_on(1)
    upto(1, 1)
    upto(2, 0)
    for k in range(1, p.Q):
        across[k - 1].wait_recv()
        cores.append(wires.push(xm_ref.at[p.Q - k, 0], xm_ref.at[p.Q - k, 1], sibling))
    pass_on(2)
    upto(1, 2)
    upto(2, 1)
    upto(3, 0)
    landed(cores)

    cot_copies, steps = [], nq * T

    def ask_cotangent():
        own, got = swap_items(p, wires, cotangent, cot_in)
        cot_copies.extend([own, got])

    between = {
        0: lambda: (pass_on(3), upto(1, 3), upto(2, 2), upto(3, 1), upto(4, 0)),
        1: lambda: (pass_on(4), upto(2, 3), upto(3, 2), upto(4, 1), upto(5, 0)),
        2: lambda: (pass_on(5), upto(3, 3), upto(4, 2), upto(5, 1), ask_cotangent(),),
        4: lambda: (upto(4, 3), upto(5, 2),),
        7: lambda: (upto(5, 3),),
    }
    if len(chunks) < 4:
        between = {}

    xm = xm_ref[...].reshape(L, D)
    copies = [
        wires.move(xm_ref, xm_out),
        wires.move(cos_ref, cos_out),
        wires.move(sin_ref, sin_out),
        wires.move(mask_ref, mask_out),
    ]
    for j in range(nq):
        chunks_a[j].upto(4)
        copies.append(wires.move(a_ref.at[j], all_a.at[j]))
        for t in range(T):
            n = j * T + t
            part = attend_block(
                rows, cb, xm,
                lambda b: a_ref[j, t, :, :, :, :, b * cb : (b + 1) * cb].reshape(D, cb),
                cos_ref, sin_ref, mask_ref,
                q_ref.at[n], k_ref.at[n], v_ref.at[n], att_ref.at[n], lse_ref.at[n],
            )
            if n == 0:
                branch_ref[...] = part
            else:
                branch_ref[...] += part
            between.get(n, tuple)()
    if not cot_copies:
        ask_cotangent()

    for src, dst in (
        (q_ref, q_out), (k_ref, k_out), (v_ref, v_out), (att_ref, att_out), (lse_ref, lse_out)
    ):
        copies.append(wires.move(src, dst))
    gate_attn, shift_ff = mod_ref[2:3, :], mod_ref[3:4, :]
    scale_ff, gate_ff = mod_ref[4:5, :], mod_ref[5:6, :]
    middle = (
        frames_in[...].reshape(rows, D).astype(F32)
        + gate_attn * live_ref[...] * branch_ref[...]
    )
    mid_ref[...] = middle
    normed, _ = layer_stats(middle)
    low = normed.astype(BF)
    normed_ref[...] = low
    modulated = (low.astype(F32) * (1.0 + scale_ff) + shift_ff).astype(BF)
    mf_ref[...] = modulated
    mf_turned[...] = modulated.T
    cot_copies[0].wait()
    landed(cot_copies[1])
    d_branch = (cot_in[...].reshape(rows, D).astype(F32) * gate_ff).astype(BF)
    db_ref[...] = d_branch
    db_turned[...] = d_branch.T

    pending = [None, None]
    for j in range(nh):
        chunks_f[j].upto(4)
        for t in range(T):
            n = j * T + t
            w_up = f_ref[j, t, :, :, :, :, 0:hb].reshape(D, hb)
            w_down = f_ref[j, t, :, :, :, :, hb : 2 * hb].reshape(D, hb)
            upper = nn(mf_ref[...], w_up)
            square = upper * upper
            slope = 0.7978845608
            tanh = jnp.tanh(slope * (upper + 0.044715 * upper * square))
            half = 0.5 * (1.0 + tanh)
            active = (upper * half).astype(BF)
            bend = half + 0.5 * upper * (1.0 - tanh * tanh) * (
                slope * (1.0 + 3 * 0.044715 * square)
            )
            d_upper = (nn(db_ref[...], w_down) * bend).astype(BF)
            if n == 0:
                out_sum[...] = nt(active, w_down)
                dmf_sum[...] = nt(d_upper, w_up)
            else:
                out_sum[...] += nt(active, w_down)
                dmf_sum[...] += nt(d_upper, w_up)
            slot = n % 2
            if pending[slot] is not None:
                pending[slot].wait()
            stage[slot, :, 0:hb] = nn(mf_turned[...], d_upper).astype(BF)
            stage[slot, :, hb : 2 * hb] = nn(db_turned[...], active).astype(BF)
            pending[slot] = pltpu.make_async_copy(stage.at[slot], grad_f.at[j, t], out_sem.at[slot])
            pending[slot].start()
            between.get(steps + n, tuple)()

    middle, branch_f = mid_ref[...], out_sum[...]
    layer_ref[...] = (middle + gate_ff * branch_f).astype(BF).reshape(layer_ref.shape)
    cot = cot_in[...].reshape(rows, D).astype(F32)
    normed, inverse = layer_stats(middle)
    dmf = dmf_sum[...]
    d_mid = cot + layer_back(normed, inverse, dmf * (1.0 + scale_ff))
    dmid_ref[...] = d_mid
    alive = d_mid * live_ref[...]
    dbranch_ref[...] = (alive * gate_attn).astype(BF)
    dmod_ref[...] = jnp.zeros_like(dmod_ref)
    dmod_ref[2:3, :] = jnp.sum(alive * branch_ref[...], axis=0, keepdims=True)
    dmod_ref[3:4, :] = jnp.sum(dmf, axis=0, keepdims=True)
    dmod_ref[4:5, :] = jnp.sum(dmf * normed_ref[...].astype(F32), axis=0, keepdims=True)
    dmod_ref[5:6, :] = jnp.sum(cot * branch_f, axis=0, keepdims=True)
    for copy in copies + [c for c in pending if c is not None]:
        copy.wait()
    wires.close()


def front_call(S, T, I, cb, hb, frames, cotangent, time, lengths, weights):
    w_query, w_up, w_mod = weights[0], weights[4], weights[6]
    rs = w_query.shape[0]
    nq, wide_a = w_query.shape[1] // cb, 4 * cb
    nh, wide_f = w_up.shape[1] // hb, 2 * hb
    fl = frames.shape[1]
    rows, Z, R = I * fl, S // 4, S // I
    Q, L, steps = R // 2, rows * R, nq * T
    high = w_mod.shape[1] // 128
    remote = 3 * (I - 1) + (nq + nh) * (Z + 2 * T + 4) + 2 * Q
    shape = jax.ShapeDtypeStruct
    vmem, dma = pltpu.VMEM, pltpu.SemaphoreType.DMA
    kept = [
        ((Q, 2, rows, D), BF),
        ((steps, rows, cb), BF),
        ((steps, L, cb), BF),
        ((steps, L, cb), BF),
        ((steps, rows, cb), BF),
        ((steps, 8, rows), F32),
        ((L, 128), F32),
        ((L, 128), F32),
        ((L, 128), BF),
    ]
    return pl.pallas_call(
        partial(front_kernel, S, T, I, cb, hb),
        out_shape=tuple(shape(*x) for x in [((nq, T, Z, 2, 2, rs, wide_a), BF)] + kept[:6])
        + (shape((nh, T, D, wide_f), BF),)
        + tuple(shape(*x) for x in kept[6:])
        + (
            shape(frames.shape, BF),
            shape((8, D), F32),
            shape(frames.shape, BF),
            shape((rows, D), F32),
            shape((rows, D), BF),
            shape((8, D), F32),
        ),
        in_specs=[ANY] * 2 + [VMEM, pl.BlockSpec(memory_space=pltpu.SMEM)] + [VMEM] * 7,
        out_specs=(ANY,) * 11 + (VMEM,) * 6,
        scratch_shapes=[vmem(*x) for x in kept]
        + [
            vmem((nq, T, Z, 2, 2, rs, wide_a), BF),
            vmem((nh, T, Z, 2, 2, rs, wide_f), BF),
            vmem(frames.shape, BF),
            vmem((T, I, high, 128), F32),
            vmem((I - 1, T, high, 128), F32),
            vmem((T, high, 128), F32),
            vmem((T, R, high, 128), F32),
            vmem((rows, 1), F32),
            vmem((rows, D), F32),
            vmem((rows, D), F32),
            vmem((rows, D), BF),
            vmem((rows, D), BF),
            vmem((D, rows), BF),
            vmem((rows, D), BF),
            vmem((D, rows), BF),
            vmem((rows, D), F32),
            vmem((rows, D), F32),
            vmem((2, D, wide_f), BF),
            dma((remote,)),
            dma((remote,)),
            dma((11 + nq,)),
            dma((R * T,)),
            dma((R * T,)),
            dma((2,)),
        ],
        compiler_params=pltpu.CompilerParams(
            collective_id=0, has_side_effects=True, vmem_limit_bytes=LIMIT
        ),
        name="forward",
    )(frames, cotangent, time, lengths, *weights)


def attend_back_block(
    rows, cb, weight, wide, db_ref, xm_turned, db_turned, cos_ref, sin_ref, mask_ref,
    q_ref, k_ref, v_ref, att_ref, lse_ref, store,
):
    d_att = nn(db_ref[...], weight(3)).astype(BF)
    store(3, nn(db_turned[...], att_ref[...]))
    ones = first_lane(rows)
    factor = HEAD_DIM**-0.5
    dqs, dks, dvs = [], [], []
    for p in range(cb // 128):
        lanes = slice(p * 128, p * 128 + 128)
        q2, k2, v2 = q_ref[:, lanes], k_ref[:, lanes], v_ref[:, lanes]
        k_long = jnp.concatenate([k2, mask_ref[...]], axis=1)
        k_turned = k2.T
        dq_parts, ds_all, p_all = [], [], []
        q_heads, d_heads = head_split(q2), head_split(d_att[:, lanes])
        for h in range(2):
            scores = nt(k_long, jnp.concatenate([q_heads[h], ones], axis=1))
            probs = jnp.exp(scores - lse_ref[pl.ds(2 * p + h, 1), :])
            d_probs = nt(v2, d_heads[h])
            row_dot = jnp.sum(probs * d_probs, axis=0, keepdims=True)
            d_scores = (probs * (d_probs - row_dot)).astype(BF)
            dq_parts.append(nn(k_turned[h * HEAD_DIM : (h + 1) * HEAD_DIM], d_scores))
            ds_all.append(d_scores)
            p_all.append(probs.astype(BF))
        dk2 = nn(jnp.concatenate(ds_all, axis=1), jnp.concatenate(q_heads, axis=0))
        dv2 = nn(jnp.concatenate(p_all, axis=1), jnp.concatenate(d_heads, axis=0))
        dq2 = jnp.concatenate(dq_parts, axis=0).T * factor
        dqs.append(
            (dq2 * cos_ref[0:rows, :] - swap_pairs(dq2) * sin_ref[0:rows, :]).astype(BF)
        )
        dks.append((dk2 * cos_ref[...] - swap_pairs(dk2) * sin_ref[...]).astype(BF))
        dvs.append(dv2.astype(BF))
    dq, dk, dv = (jnp.concatenate(v, axis=1) for v in (dqs, dks, dvs))
    store(0, nn(xm_turned[:, 0:rows], dq))
    store(1, nn(xm_turned[...], dk))
    store(2, nn(xm_turned[...], dv))
    return nt(jnp.concatenate([dk, dv], axis=1), wide(1, 3)), nt(dq, weight(0))


def back_kernel(
    S, T, I, cb,
    layer, all_a, grad_f, k_all, v_all, xm_all, dmid, frames,
    q_ref, att_ref, lse_ref, mod_ref, db_ref, dmod_ref,
    cos_ref, sin_ref, mask_ref,
    layer_out, grads_out, rows_out, sum_a, sum_f,
    *scratch,
):
    nh, nq = grad_f.shape[0], all_a.shape[0]
    (xm_turned, db_turned, dx_sum, dx_ref, near, far, d_rows, group_in, group_sum, ga_ref,
     w_stage, k_stage, v_stage, in_sem, send, recv, local, row_send, row_recv) = scratch[:19]
    rest = scratch[19:]
    p = Place(S, T, I)
    wires = Wires(send, recv, local)
    Q, _, rows, _ = xm_all.shape
    L = Q * 2 * rows
    steps, slots = nq * T, w_stage.shape[0]

    def fetch(n):
        j, t = divmod(n, T)
        slot = n % slots
        copies = [
            pltpu.make_async_copy(all_a.at[j, t], w_stage.at[slot], in_sem.at[0, slot]),
            pltpu.make_async_copy(k_all.at[n], k_stage.at[slot], in_sem.at[1, slot]),
            pltpu.make_async_copy(v_all.at[n], v_stage.at[slot], in_sem.at[2, slot]),
        ]
        for copy in copies:
            copy.start()
        return copies

    xm_copy = wires.move(xm_all, dx_ref)
    fetched = fetch(0)
    greet(p)
    chunks_f, chunks_a = [], []
    for j in range(nh):
        own, landing, rest = rest[0], rest[1:7], rest[7:]
        chunks_f.append(Reduce(p, wires, grad_f.at[j], sum_f.at[j], own, 0, 2, landing))
    for j in range(nq):
        for h in (1, 0):
            landing, rest = rest[:6], rest[6:]
            cols = pl.ds(2 * cb * h, 2 * cb)
            g = ga_ref.at[j, :, :, :, :, :, cols]
            chunks_a.append(Reduce(p, wires, g, sum_a.at[j, :, cols], g, p.c, 3 if j == 1 else 2, landing))
    chunks = chunks_f + chunks_a

    def upto(m, phase):
        if m < len(chunks):
            chunks[m].upto(phase)

    upto(0, 0)
    if nh > 1:
        upto(1, 0)
    xm_copy.wait()
    db_turned[...] = db_ref[...].T
    upto(0, 1)
    for m in range(2, nh):
        upto(m, 0)
    xm_turned[...] = dx_ref[...].reshape(L, D).T
    for m in range(1, nh):
        upto(m, 1)
    layer_own, layer_in = swap_items(p, wires, layer, layer_out)

    between = {}
    if nq == 2 and T == 2 and nh == 4:
        between = {
            0: lambda: (upto(0, 2), upto(1, 2)),
            1: lambda: (upto(4, 0), upto(5, 0), upto(2, 2), upto(3, 2), upto(4, 1), upto(5, 1)),
            2: lambda: (upto(0, 3), upto(1, 3), upto(2, 3), upto(3, 3)),
        }

    for n in range(steps):
        j, t = divmod(n, T)
        slot = n % slots
        coming = fetch(n + 1) if slots == 2 and n + 1 < steps else None
        for copy in fetched:
            copy.wait()
        fetched = coming

        def store(b, value):
            ga_ref[j, t, :, :, :, :, b * cb : (b + 1) * cb] = value.astype(BF).reshape(
                ga_ref.shape[2:6] + (cb,)
            )

        dx, dx_own = attend_back_block(
            rows, cb,
            lambda b: w_stage[slot, :, b * cb : (b + 1) * cb],
            lambda b, e: w_stage[slot, :, b * cb : e * cb],
            db_ref, xm_turned, db_turned, cos_ref, sin_ref, mask_ref,
            q_ref.at[n], k_stage.at[slot], v_stage.at[slot], att_ref.at[n], lse_ref.at[n], store,
        )
        if n == 0:
            dx_sum[...] = dx
        else:
            dx_sum[...] += dx
        dx_sum[0:rows, :] += dx_own
        if slots == 1 and n + 1 < steps:
            fetched = fetch(n + 1)
        if n < steps - 1:
            between.get(n, tuple)()

    dx_ref[...] = dx_sum[...].astype(BF).reshape(dx_ref.shape)
    dmid_copy = wires.move(dmid, dx_sum.at[pl.ds(rows, rows)])
    fl = layer.shape[1]
    frame_copies = [
        wires.move(frames.at[n], xm_turned.at[pl.ds(n * fl, fl), pl.ds(0, D)]) for n in range(I)
    ]
    core = wires.push(dx_ref.at[:, 1], near, p.group(0, 1 - p.c))
    last = len(chunks) - 1
    upto(last - 1, 0)
    upto(last, 0)
    core.wait_recv()
    across = []
    for k in range(1, Q):
        dx_ref[k, 0] = dx_ref[k, 0] + near[k]
        across.append(wires.push(dx_ref.at[k, 0], far.at[k - 1], p.group(k)))
    for m in range(last - 1):
        upto(m, 2)
    upto(last - 1, 1)
    upto(last, 1)
    for m in range(nh):
        upto(m, 4)

    for copy in frame_copies:
        copy.wait()
    normed, inverse = layer_stats(xm_turned[0:rows, 0:D].astype(F32))
    d_mod = dx_sum[0:rows, :] + near[0].astype(F32)
    for k in range(1, Q):
        across[k - 1].wait_recv()
        d_mod = d_mod + far[k - 1].astype(F32)
    incoming = layer_back(normed, inverse, d_mod * (1.0 + mod_ref[1:2, :]))
    dmid_copy.wait()
    dx_ref[0, 0] = (dx_sum[rows : 2 * rows, :] + incoming).astype(BF)
    grads_own, grads_in = swap_items(
        p, wires, lambda n: dx_ref.at[0, 0, pl.ds(n * fl, fl)], grads_out
    )
    high = d_rows.shape[1]
    first = [
        jnp.sum(d_mod, axis=0, keepdims=True),
        jnp.sum(d_mod * normed.astype(BF).astype(F32), axis=0, keepdims=True),
    ]
    for t in range(T):
        for n in range(high):
            row, col = divmod((t * high + n) * 128, D)
            value = first[row] if row < 2 else dmod_ref[row : row + 1, :]
            d_rows[t, n : n + 1, :] = value[:, col : col + 128]
    group_in[p.t, p.r] = d_rows[p.t]
    group_done = spread_group(p, row_send, row_recv, lambda t: d_rows.at[t], group_in)
    for m in range(last - 1):
        upto(m, 3)
    group_done()
    for t in range(T):
        group_sum[t] = jnp.sum(group_in[t], axis=0)
    rows_own = wires.move(group_sum, rows_out.at[p.i])
    line = []
    for k in range(1, I):
        other = lax.rem(p.i + k, I)
        line.append(wires.push(group_sum, rows_out.at[p.i], (other * p.R + p.r, p.t)))
    upto(last - 1, 2)
    upto(last, 2)
    for m in range(last - 1):
        upto(m, 4)
    upto(last - 1, 3)
    upto(last, 3)
    upto(last - 1, 4)
    upto(last, 4)
    for m in range(last + 1):
        upto(m, 5)
    landed(line)
    for own in (grads_own, layer_own, rows_own):
        own.wait()
    landed(grads_in)
    landed(layer_in)
    wires.close()


def back_call(
    S, T, I, cb, layer, all_a, grad_f, k, v, xm, d_mid, frames,
    q, att, lse, mod, d_branch, d_mod, cosine, sine, mask,
):
    nq, ca = all_a.shape[0], all_a.shape[3]
    nh, cf = grad_f.shape[0], grad_f.shape[6]
    rs = grad_f.shape[5]
    Z, Q, rows = S // 4, xm.shape[0], xm.shape[2]
    L = Q * 2 * rows
    high = 6 * D // T // 128
    slots = 2 if L <= 1024 else 1
    remote = 3 * (I - 1) + (2 * nq + nh) * (Z + 2 * T + 2) + Q
    R = S // I
    shape = jax.ShapeDtypeStruct
    dma = pltpu.SemaphoreType.DMA
    scratch = [
        pltpu.VMEM((D, L), BF),
        pltpu.VMEM((D, rows), BF),
        pltpu.VMEM((L, D), F32),
        pltpu.VMEM((Q, 2, rows, D), BF),
        pltpu.VMEM((Q, rows, D), BF),
        pltpu.VMEM((Q - 1, rows, D), BF),
        pltpu.VMEM((T, high, 128), F32),
        pltpu.VMEM((T, R, high, 128), F32),
        pltpu.VMEM((T, high, 128), F32),
        pltpu.VMEM((nq, T, Z, 2, 2, rs, ca), BF),
        pltpu.VMEM((slots, D, ca), BF),
        pltpu.VMEM((slots, L, cb), BF),
        pltpu.VMEM((slots, L, cb), BF),
        dma((3, slots)),
        dma((remote,)),
        dma((remote,)),
        dma((5 + nh + I,)),
        dma((R * T,)),
        dma((R * T,)),
    ]
    for _ in range(nh):
        scratch += [pltpu.VMEM((T, Z, 2, 1, rs, cf), BF)] + Reduce.landing(T, Z, rs, cf, 2)
    for j in range(2 * nq):
        scratch += Reduce.landing(T, Z, rs, ca // 2, 3 if j // 2 == 1 else 2)
    return pl.pallas_call(
        partial(back_kernel, S, T, I, cb),
        out_shape=(
            shape(layer.shape, BF),
            shape(layer.shape, BF),
            shape((I, T, high, 128), F32),
            shape((nq, rs, ca), F32),
            shape((nh, rs, cf), F32),
        ),
        in_specs=[ANY] * 8 + [VMEM] * 9,
        out_specs=(ANY, ANY, ANY, VMEM, VMEM),
        scratch_shapes=scratch,
        compiler_params=pltpu.CompilerParams(
            collective_id=1, has_side_effects=True, vmem_limit_bytes=LIMIT
        ),
        name="backward",
    )(
        layer, all_a, grad_f, k, v, xm, d_mid, frames,
        q, att, lse, mod, d_branch, d_mod, cosine, sine, mask,
    )


def layer_stats(values):
    center = values - jnp.mean(values, axis=-1, keepdims=True)
    inverse = lax.rsqrt(jnp.mean(center * center, axis=-1, keepdims=True) + EPSILON)
    return center * inverse, inverse


def layer_back(normed, inverse, incoming):
    return inverse * (
        incoming
        - jnp.mean(incoming, axis=-1, keepdims=True)
        - normed * jnp.mean(incoming * normed, axis=-1, keepdims=True)
    )


def finish_kernel(
    S, T, I, micro, time_ref, rows_ref, sum_a, sum_f, layer_in, grads_in,
    layer_ref, grads_ref, gq_ref, gk_ref, gv_ref, go_ref, gu_ref, gd_ref, gm_ref, items_ref,
):
    p = Place(S, T, I)
    nq, rs, wide_a = sum_a.shape
    nh, _, wide_f = sum_f.shape
    cb, hb = wide_a // 4, wide_f // 2
    layer_ref[...] = layer_in[...]
    grads_ref[...] = grads_in[...]
    for j in range(nq):
        for b, ref in enumerate((gq_ref, gk_ref, gv_ref, go_ref)):
            ref[:, j * cb : (j + 1) * cb] = sum_a[j, :, b * cb : (b + 1) * cb]
    for j in range(nh):
        gu_ref[:, j * hb : (j + 1) * hb] = sum_f[j, :, 0:hb]
        gd_ref[:, j * hb : (j + 1) * hb] = sum_f[j, :, hb : 2 * hb]
    high = rows_ref.shape[2]
    rows_own = I // micro
    for item in range(I * T):
        m, b = divmod(item, rows_own * T)
        i, t = m * rows_own + b % rows_own, b // rows_own
        for n in range(high):
            items_ref[item : item + 1, n * 128 : (n + 1) * 128] = rows_ref[i, t, n : n + 1, :]
    silu = own_columns(p, time_ref[...], rs).astype(F32)
    gm_ref[...] = lax.dot_general(
        silu, items_ref[...], (((0,), (0,)), ((), ())), precision=HIGHEST,
        preferred_element_type=F32,
    )


def finish_call(S, T, I, micro, time, rows, sum_a, sum_f, layer, grads, weights):
    shape = jax.ShapeDtypeStruct
    return pl.pallas_call(
        partial(finish_kernel, S, T, I, micro),
        out_shape=(shape(layer.shape, BF), shape(grads.shape, BF))
        + tuple(shape(w.shape, F32) for w in weights),
        in_specs=[VMEM] * 6,
        out_specs=(VMEM,) * 9,
        scratch_shapes=[pltpu.VMEM((I * T, weights[6].shape[1]), F32)],
        compiler_params=pltpu.CompilerParams(vmem_limit_bytes=LIMIT),
        name="finish",
    )(time, rows, sum_a, sum_f, layer, grads)


def per_device(
    S, T, frames, time_embed, lengths, w_query, w_key, w_value, w_out, w_up, w_down, w_mod, out_grad
):
    micro, rows_own, fl, _ = frames.shape
    batch = lengths.shape[1]
    I = micro * rows_own
    rs = w_query.shape[0]
    cb = min(256, w_query.shape[1])
    hb = min(256, w_up.shape[1])
    time = time_embed
    weights = (w_query, w_key, w_value, w_out.T, w_up, w_down.T, w_mod)
    (
        all_a, xm, q, k, v, att, lse, grad_f, cosine, sine, mask,
        frames_in, mod, layer, d_mid, d_branch, d_rows,
    ) = front_call(
        S, T, I, cb, hb, frames.reshape(I, fl, D), out_grad.reshape(I, fl, D), time, lengths, weights
    )
    layer_out, grad_input, rows_in, sum_a, sum_f = back_call(
        S, T, I, cb, layer, all_a.reshape(all_a.shape[:2] + (D, 4 * cb)),
        grad_f.reshape((grad_f.shape[0], T, S // 4, 2, 2, rs, 2 * hb)), k, v, xm, d_mid,
        frames_in, q, att, lse, mod, d_branch, d_rows, cosine, sine, mask,
    )
    outs = finish_call(S, T, I, micro, time, rows_in, sum_a, sum_f, layer_out, grad_input, weights)
    layer_out, grad_input, g_query, g_key, g_value, g_out, g_up, g_down, g_mod = outs
    return (
        layer_out.reshape(frames.shape), grad_input.reshape(frames.shape),
        g_query, g_key, g_value, g_out.T, g_up, g_down.T, g_mod,
    )


def solution(mesh):
    S, T = mesh.shape["seq"], mesh.shape["tp"]
    rows = P(None, "tp", "seq", None)
    return jax.shard_map(
        partial(per_device, S, T),
        mesh=mesh,
        in_specs=(
            rows,
            P(),
            P(),
            P("seq", "tp"),
            P("seq", "tp"),
            P("seq", "tp"),
            P("tp", "seq"),
            P("seq", "tp"),
            P("tp", "seq"),
            P("seq", "tp"),
            rows,
        ),
        out_specs=(
            rows,
            rows,
            P("seq", "tp"),
            P("seq", "tp"),
            P("seq", "tp"),
            P("tp", "seq"),
            P("seq", "tp"),
            P("tp", "seq"),
            P("seq", "tp"),
        ),
        check_vma=False,
    )
```
